128 devices in a mesh: grp: 8 (over x, z_lo), slab: 16 (over z_hi, y, core).
Axes of the slice: x: 4, y: 4, z: 4 (z_hi: 2, z_lo: 2; z = z_hi * 2 + z_lo), core: 2. Of those that a mesh axis runs over, the one named last changes fastest.
Arguments:
- valence_waves: bfloat16 [8, 128, 128, 256], P('grp', 'slab'), may hold values from -6 to 6
- conduction_waves: bfloat16 [128, 128, 128, 256], P('grp', 'slab'), may hold values from -6 to 6
- valence_energy: float32 [8], replicated, may hold values from -3 to -0.5
- conduction_energy: float32 [128], P('grp'), may hold values from 0.5 to 4
- occupation: int32 [8], replicated, may hold values from 1 to 2
- gvec_ids: int32 [12000], replicated, may hold values from 0 to 32767, as said below
Outputs:
- chi0: float32 [2, 12000, 12000], P(None, 'grp', 'slab')
The draws below stay inside these ranges and needn't reach their ends.
Inputs may be any that keep to these rules, and one draw needn't show every extreme that they name: `gvec_ids`: 12000 distinct indices (kx 32 + ky) * 32 + kz of points of the frequency box, ordered by their distance from a shifted centre; every one has f(ky)^2 + f(kz)^2 <= 196.
All inputs are finite; a program needn't handle non-finite values.
Results may differ from the reference program's by a relative error of at most 0.0086.
Values may be sent and summed in bfloat16 or wider, within the bound.
A program may use at most 256 MiB of HBM per device.

```python
import math
import jax
import jax.numpy as jnp
from jax import lax

NV = 8
NC = 128
NF = 128
KB = 32
NG = 12000
DISC = 196


def draw_gvec_ids(key, part):
    key = jax.random.fold_in(key, 7)
    shift_key, order_key = jax.random.split(key)
    centre = jax.random.randint(shift_key, (3,), -2, 3)
    points = jnp.arange(KB ** 3, dtype=jnp.int32)
    along_x = points // (KB * KB)
    along_y = points // KB % KB
    along_z = points % KB
    half_box = KB // 2
    freq_x = along_x - KB * (along_x >= half_box).astype(jnp.int32)
    freq_y = along_y - KB * (along_y >= half_box).astype(jnp.int32)
    freq_z = along_z - KB * (along_z >= half_box).astype(jnp.int32)
    energy = (4 * freq_x + centre[0]) ** 2 + (4 * freq_y + centre[1]) ** 2 + (4 * freq_z + centre[2]) ** 2
    outside = (freq_y * freq_y + freq_z * freq_z > DISC).astype(jnp.int32)
    ceiling = 3 * (2 * KB + 2) ** 2 + 1
    energy = energy * (1 - outside) + ceiling * outside
    breaker = jax.random.permutation(order_key, KB ** 3).astype(jnp.int32)
    scores = energy * KB ** 3 + breaker
    _, chosen = lax.top_k(-scores, NG)
    return chosen.astype(jnp.int32)


def with_ends(array, key, smallest, top_value):
    place = [jax.random.randint(jax.random.fold_in(key, axis), (), 0, length) for axis, length in enumerate(array.shape)]
    main_axis = array.shape.index(max(array.shape))
    beside = place[:main_axis] + [(place[main_axis] + 1) % array.shape[main_axis]] + place[main_axis + 1:]
    return array.at[tuple(place)].set(smallest).at[tuple(beside)].set(top_value)


def level_of(stream_key, dims, cuts, least, high):
    factor_of, own = 1.0, jax.random.fold_in(stream_key, 6)
    for position, parts in cuts:
        heights = jnp.exp(jax.random.uniform(jax.random.fold_in(own, position), (parts,), jnp.float32, least / len(cuts), high / len(cuts)))
        factor_of = factor_of * jnp.repeat(heights, dims[position] // parts).reshape([-1 if axis == position else 1 for axis in range(len(dims))])
    return factor_of


def scatter_about(rng, dims, width, reach, shards=(), kind=jnp.bfloat16):
    array = jax.random.normal(rng, dims, jnp.float32) * width
    if len(shards) > 0:
        array = level_of(rng, dims, shards, -0.22, 0.18) * array
    return jnp.clip(array, min=-reach, max=reach).astype(kind)


def setup_inputs(seed: int = 0) -> dict:
    streams_of = jax.random.split(jax.random.key(seed), 7)
    return {
        "valence_waves": scatter_about(streams_of[0], (NV, NF, NF, 2 * NF), 1.0, 6.0, ((0, 8), (1, 16))),
        "conduction_waves": scatter_about(streams_of[1], (NC, NF, NF, 2 * NF), 1.0, 6.0, ((0, 8), (1, 16))),
        "valence_energy": jnp.clip(jax.random.uniform(streams_of[2], (NV,), jnp.float32, -3.0, -0.5), -3.0, -0.5),
        "conduction_energy": jnp.clip(0.5 + 3.5 * jax.random.uniform(streams_of[3], (NC,), jnp.float32) ** level_of(streams_of[3], (NC,), ((0, 8),), -0.2, 0.2), 0.5, 4.0),
        "occupation": with_ends(jax.random.randint(streams_of[4], (NV,), 1, 3), jax.random.fold_in(streams_of[4], 1), 1, 2).astype(jnp.int32),
        "gvec_ids": draw_gvec_ids(jax.random.fold_in(streams_of[6], 71), 0),
    }


def frequency(length):
    positions = jnp.arange(length, dtype=jnp.int32)
    return positions - length * (positions >= length // 2).astype(jnp.int32)

def phase_tables(positions):
    angle = jnp.mod(positions[:, None] * frequency(KB)[None, :], NF).astype(jnp.float32) * (2.0 * math.pi / NF)
    return (jnp.cos(angle), jnp.sin(angle))

def plane_tables():
    cosine, sine = phase_tables(jnp.arange(NF, dtype=jnp.int32))
    cosine_table = cosine.astype(jnp.bfloat16)
    sine_table = sine.astype(jnp.bfloat16)
    upper = jnp.concatenate([cosine_table, -sine_table], 1)
    lower = jnp.concatenate([sine_table, cosine_table], 1)
    return (cosine_table, sine_table, jnp.concatenate([upper, lower], 0))

def pair_density(valence, conduction):
    val_real = valence[..., :NF].astype(jnp.float32)
    val_imag = valence[..., NF:].astype(jnp.float32)
    con_real = conduction[..., :NF].astype(jnp.float32)
    con_imag = conduction[..., NF:].astype(jnp.float32)
    real_part = val_real * con_real + val_imag * con_imag
    imag_part = val_real * con_imag - val_imag * con_real
    return jnp.concatenate([real_part, imag_part], -1).astype(jnp.bfloat16)

def plane_transform(density, cosine_table, sine_table, depth_table):
    highest = lax.Precision.HIGHEST
    dense = density.astype(jnp.float32)
    cosine_part = jnp.einsum('bxyz,yq->bxqz', dense, cosine_table.astype(jnp.float32), precision=highest)
    sine_part = jnp.einsum('bxyz,yq->bxqz', dense, sine_table.astype(jnp.float32), precision=highest)
    first = cosine_part + jnp.concatenate([sine_part[..., NF:], -sine_part[..., :NF]], -1)
    first = first.astype(jnp.bfloat16)
    second = jnp.einsum('bxqz,zk->bxqk', first.astype(jnp.float32), depth_table.astype(jnp.float32), precision=highest)
    return second.reshape(second.shape[0], second.shape[1], 2 * KB * KB)

def box_transform(planes, first_plane):
    highest = lax.Precision.HIGHEST
    positions = first_plane + jnp.arange(planes.shape[1], dtype=jnp.int32)
    cosine, sine = phase_tables(positions)
    shaped = planes.reshape(planes.shape[0], planes.shape[1], KB, 2, KB)
    cosine_part = jnp.einsum('bxyrz,xk->bkyrz', shaped, cosine, precision=highest)
    sine_part = jnp.einsum('bxyrz,xk->bkyrz', shaped, sine, precision=highest)
    real_part = cosine_part[:, :, :, 0] + sine_part[:, :, :, 1]
    imag_part = cosine_part[:, :, :, 1] - sine_part[:, :, :, 0]
    return jnp.stack([real_part, imag_part], 3).reshape(planes.shape[0], 2 * KB * KB * KB)

def sphere_columns(gvec_ids):
    along_x = gvec_ids // (KB * KB)
    along_y = gvec_ids // KB % KB
    along_z = gvec_ids % KB
    base = along_x * (2 * KB * KB) + along_y * (2 * KB) + along_z
    return (base, base + KB)

def reference(valence_waves, conduction_waves, valence_energy, conduction_energy, occupation, gvec_ids):
    cosine_table, sine_table, depth_table = plane_tables()
    column_real, column_imag = sphere_columns(gvec_ids)
    scaling = 0.5 / float(NF) ** 1.5

    def one_band(wavefunction):
        density = pair_density(valence_waves, wavefunction[None])
        planes = plane_transform(density, cosine_table, sine_table, depth_table)
        boxed = box_transform(planes, jnp.int32(0))
        picked = jnp.stack([jnp.take(boxed, column_real, axis=1), jnp.take(boxed, column_imag, axis=1)], 1)
        return (picked * scaling).astype(jnp.bfloat16)
    coefficients = lax.map(one_band, conduction_waves)
    factor = occupation.astype(jnp.float32)[None, :] / ((valence_energy[None, :] - conduction_energy[:, None]) * math.sqrt(NV * NC))
    weighted = (coefficients.astype(jnp.float32) * factor[:, :, None, None]).astype(jnp.bfloat16)
    pair_total = NC * NV
    right_side = coefficients.reshape(pair_total, 2, NG).transpose(2, 1, 0)
    left_side = weighted.reshape(pair_total, 2, NG).transpose(2, 1, 0)
    right_flat = right_side.reshape(NG, 2 * pair_total).astype(jnp.float32)
    left_flat = left_side.reshape(NG, 2 * pair_total).astype(jnp.float32)
    swapped = jnp.concatenate([left_side[:, 1], -left_side[:, 0]], 1).astype(jnp.float32)
    highest = lax.Precision.HIGHEST
    chi_real = jnp.dot(left_flat, right_flat.T, precision=highest)
    chi_imag = jnp.dot(swapped, right_flat.T, precision=highest)
    return jnp.stack([chi_real, chi_imag], 0)
```

```python
import functools
import math

import jax
import jax.numpy as jnp
import ml_dtypes
import numpy as np
from jax import lax
from jax.experimental import pallas as pl
from jax.experimental.pallas import tpu as pltpu
from jax.sharding import PartitionSpec as P

NV = 8
NC = 128
NF = 128
KB = 32
NG = 12000
NGRP = 8
NSLAB = 16
NX = NF // NSLAB
NR = 24
RB = NG // NGRP
CB = NG // NSLAB
RP = 1536
CP = 768
NBOX = NR * KB
MESH = pl.DeviceIdType.MESH
BF = jnp.bfloat16
F32 = jnp.float32

WIDE = [9, -9, 11, -11, 5, -5]
NARROW = [13, -13, 12, -12, 14, -14]
SINGLE = [0, 1, -1, 2, -2, 3, -3, 4, -4, 6, -6, 7, -7, 8, -8, 10, -10]
ROW_FREQ = SINGLE[:16] + [SINGLE[16]] + WIDE + [15] + [15] + NARROW + [15]


def freq(j):
    return j - KB if j >= KB // 2 else j


def row_tables():
    row = np.zeros(KB, np.int32)
    shifted = np.zeros(KB, np.int32)
    for place, f in enumerate(ROW_FREQ[:NR]):
        if f != 15:
            row[f % KB] = place
    for place, f in enumerate(NARROW):
        row[f % KB] = 17 + place
        shifted[f % KB] = KB // 2
    return row, shifted


def phases(positions, freqs):
    angle = np.mod(np.outer(positions, freqs), NF).astype(np.float32) * np.float32(2.0 * math.pi / NF)
    return np.cos(angle).astype(np.float32), np.sin(angle).astype(np.float32)


def depth_weights():
    cos, sin = phases(np.arange(NF), [freq(j) for j in range(KB)])
    w = np.zeros((4, 2, NF, 2, KB, 4), np.float32)
    for vl in range(4):
        w[vl, 0, :, 0, :, vl] = cos
        w[vl, 1, :, 0, :, vl] = sin
        w[vl, 0, :, 1, :, vl] = -sin
        w[vl, 1, :, 1, :, vl] = cos
    return w.reshape(8 * NF, 8 * KB).astype(ml_dtypes.bfloat16)


def height_weights():
    cos, sin = phases(np.arange(NF), ROW_FREQ)
    return np.concatenate([cos.T, sin.T], 0).astype(ml_dtypes.bfloat16)


def wide_mask():
    mask = np.ones((8, KB, 4), np.float32)
    for place, f in enumerate(WIDE):
        half = math.isqrt(196 - f * f)
        for j in range(KB):
            if abs(freq(j)) > half:
                mask[1 + place, j] = 0.0
    return mask.reshape(8, 4 * KB)


def box_weights():
    cos, sin = phases(np.arange(NF), [freq(j) for j in range(KB)])
    cos, sin = cos.T.reshape(KB, NSLAB, NX), sin.T.reshape(KB, NSLAB, NX)
    t = np.zeros((2, KB, NSLAB, 2, NX), np.float32)
    t[0, :, :, 0] = cos
    t[0, :, :, 1] = sin
    t[1, :, :, 0] = -sin
    t[1, :, :, 1] = cos
    t = t.reshape(2 * KB, 2 * NF)
    high = t.astype(ml_dtypes.bfloat16)
    low = (t - high.astype(np.float32)).astype(ml_dtypes.bfloat16)
    return np.concatenate([high, low], 0)


def lane_order():
    m = np.zeros((2, 2, KB, 4, KB, 2, 2, 4), np.float32)
    for reim in range(2):
        for vg in range(2):
            for kz in range(KB):
                for vl in range(4):
                    m[reim, vg, kz, vl, kz, reim, vg, vl] = 1.0
    return m.reshape(512, 512).astype(ml_dtypes.bfloat16)


def place_in_groups():
    g = lax.axis_index("grp")
    gx, gz = g // 2, lax.rem(g, 2)

    def at(dx, dz):
        return lax.rem(gx + dx + 4, 4) * 2 + (lax.rem(gz + dz, 2))

    return g, at


def place_in_slabs():
    s = lax.axis_index("slab")
    sz, sy, sc = s // 8, lax.rem(s // 2, 4), lax.rem(s, 2)

    def at(dy, dz, dc):
        return lax.rem(sz + dz, 2) * 8 + lax.rem(sy + dy + 4, 4) * 2 + lax.rem(sc + dc, 2)

    return s, at


def enter(groups, slabs):
    barrier = pltpu.get_barrier_semaphore()
    for one in groups:
        pl.semaphore_signal(barrier, inc=1, device_id={"grp": one}, device_id_type=MESH)
    for one in slabs:
        pl.semaphore_signal(barrier, inc=1, device_id={"slab": one}, device_id_type=MESH)
    pl.semaphore_wait(barrier, len(groups) + len(slabs))


def remote(src, dst, send, recv, device):
    return pltpu.make_async_remote_copy(
        src_ref=src, dst_ref=dst, send_sem=send, recv_sem=recv, device_id=device, device_id_type=MESH
    )


def planes_kernel(
    val_ref, con_ref, wz_ref, ty_ref, mask_ref, out_ref, val, con, msg, dbuf, scr, con_sem, own_sem, vs, vr, ms, mr, local_sem
):
    g, gat = place_in_groups()
    s, sat = place_in_slabs()
    own = pltpu.make_async_copy(val_ref.at[0], val.at[0], own_sem)
    own.start()

    def con_copy(c):
        return pltpu.make_async_copy(con_ref.at[c], con.at[c], con_sem.at[c])

    def start_con(i, _):
        con_copy(lax.rem(s + i + 1, NSLAB)).start()
        return 0

    lax.fori_loop(0, NSLAB, start_con, 0)
    partner, ahead, behind = gat(0, 1), gat(1, 0), gat(-1, 0)
    enter([partner, ahead, behind], [lax.rem(s + i, NSLAB) for i in range(1, NSLAB)])
    own.wait()

    def hop(k, slot, to, landing):
        return remote(val.at[slot], val.at[landing], vs.at[k], vr.at[landing], {"grp": to})

    to_partner, to_ahead, to_behind = hop(0, 0, partner, 1), hop(1, 0, ahead, 2), hop(2, 0, behind, 3)
    to_ahead.start()
    to_behind.start()
    to_partner.start()
    p_ahead, p_behind = hop(3, 1, ahead, 4), hop(4, 1, behind, 5)
    l_ahead, r_behind = hop(5, 2, ahead, 6), hop(6, 5, behind, 7)
    to_partner.wait_recv()
    p_ahead.start()
    p_behind.start()
    to_ahead.wait_recv()
    l_ahead.start()
    to_behind.wait_recv()

    def message(vg, c):
        return remote(
            msg.at[vg, c], out_ref.at[vg, s], ms.at[vg, c], mr.at[vg, s], {"slab": c}
        )

    def arrival(vg, src):
        return remote(
            msg.at[vg, src], out_ref.at[vg, src], ms.at[vg, src], mr.at[vg, src], {"slab": src}
        )

    def one_plane(vg, c, x, par):
        for y0 in range(0, NF, 32):
            rows = pl.ds(y0, 32)
            cr = con[c, x, rows, 0:NF].astype(F32)
            ci = con[c, x, rows, NF : 2 * NF].astype(F32)
            for vl in range(4):
                pr = val[vg * 4 + vl, x, rows, 0:NF].astype(F32)
                pi = val[vg * 4 + vl, x, rows, NF : 2 * NF].astype(F32)
                dbuf[par, rows, vl * 256 : vl * 256 + NF] = (pr * cr + pi * ci).astype(BF)
                dbuf[par, rows, vl * 256 + NF : vl * 256 + 256] = (pr * ci - pi * cr).astype(BF)
        f = jnp.dot(dbuf[par], wz_ref[...], preferred_element_type=F32).astype(BF)
        o = jnp.dot(ty_ref[...], f, preferred_element_type=F32)
        keep = mask_ref[...] > 0.5
        for reim in range(2):
            if reim == 0:
                full = o[0:32, 0:128] + o[32:64, 128:256]
            else:
                full = o[0:32, 128:256] - o[32:64, 0:128]
            merged = jnp.where(keep, full[16:24], pltpu.roll(full[24:32], 64, 1))
            base = pl.multiple_of(x * NR, 8)
            scr[reim, pl.ds(base, 16), :] = full[0:16]
            scr[reim, pl.ds(base + 16, 8), :] = merged

    for vg in range(2):
        if vg == 1:
            p_ahead.wait_recv()
            l_ahead.wait_recv()
            r_behind.wait_recv()

        def one_band(i, _):
            c = lax.rem(s + i + 1, NSLAB)
            if vg == 0:
                con_copy(c).wait()

                @pl.when(i == 8)
                def _():
                    p_behind.wait_recv()
                    r_behind.start()

            def planes(j, _):
                one_plane(vg, c, 2 * j, 0)
                one_plane(vg, c, 2 * j + 1, 1)
                return 0

            lax.fori_loop(0, NX // 2, planes, 0)

            for r in range(NR):
                both = jnp.concatenate(
                    [scr[0, pl.ds(r, NX, stride=NR), :], scr[1, pl.ds(r, NX, stride=NR), :]], 0
                )
                msg[vg, c, r] = both.astype(BF)

            @pl.when(i < NSLAB - 1)
            def _():
                message(vg, c).start()

            @pl.when(i == NSLAB - 1)
            def _():
                pltpu.make_async_copy(msg.at[vg, c], out_ref.at[vg, s], local_sem.at[vg]).start()

            return 0

        lax.fori_loop(0, NSLAB, one_band, 0)

    def finish(i, _):
        other = lax.rem(s + i + 1, NSLAB)
        for vg in range(2):
            arrival(vg, other).wait_recv()
            message(vg, other).wait_send()
        return 0

    lax.fori_loop(0, NSLAB - 1, finish, 0)
    for vg in range(2):
        pltpu.make_async_copy(msg.at[vg, s], out_ref.at[vg, s], local_sem.at[vg]).wait()
    for copy in (to_partner, to_ahead, to_behind, p_ahead, p_behind, l_ahead, r_behind):
        copy.wait_send()


def planes_call(valence, conduction):
    return pl.pallas_call(
        planes_kernel,
        name="planes",
        out_shape=jax.ShapeDtypeStruct((2, NSLAB, NR, 2 * NX, 128), BF),
        in_specs=[
            pl.BlockSpec(memory_space=pl.ANY),
            pl.BlockSpec(memory_space=pl.ANY),
            pl.BlockSpec(memory_space=pltpu.VMEM),
            pl.BlockSpec(memory_space=pltpu.VMEM),
            pl.BlockSpec(memory_space=pltpu.VMEM),
        ],
        out_specs=pl.BlockSpec(memory_space=pl.ANY),
        scratch_shapes=[
            pltpu.VMEM((8, NX, NF, 2 * NF), BF),
            pltpu.VMEM((NSLAB, NX, NF, 2 * NF), BF),
            pltpu.VMEM((2, NSLAB, NR, 2 * NX, 128), BF),
            pltpu.VMEM((2, NF, 8 * NF), BF),
            pltpu.VMEM((2, NX * NR, 128), F32),
            pltpu.SemaphoreType.DMA((NSLAB,)),
            pltpu.SemaphoreType.DMA,
            pltpu.SemaphoreType.DMA((7,)),
            pltpu.SemaphoreType.DMA((8,)),
            pltpu.SemaphoreType.DMA((2, NSLAB)),
            pltpu.SemaphoreType.DMA((2, NSLAB)),
            pltpu.SemaphoreType.DMA((2,)),
        ],
        compiler_params=pltpu.CompilerParams(
            collective_id=0, has_side_effects=True, vmem_limit_bytes=40 * 1024 * 1024
        ),
    )(
        valence,
        conduction,
        jnp.asarray(depth_weights()),
        jnp.asarray(height_weights()),
        jnp.asarray(wide_mask()),
    )


def sphere_kernel(idx_ref, in_ref, tab_ref, order_ref, fac_ref, row_ref, col_ref, xb, box, sph):
    scaling = 0.5 / float(NF) ** 1.5

    def one_row(r, _):
        a = [in_ref[vg, :, pl.ds(r, 1)].reshape(2 * NF, 128) for vg in range(2)]
        o = jnp.dot(tab_ref[...], jnp.concatenate(a, 1), preferred_element_type=F32)
        o = ((o[0:64] + o[64:128]) * scaling).astype(BF)
        rows = pl.ds(pl.multiple_of(r * KB, KB), KB)
        xb[rows, 0:256] = o[0:32]
        xb[rows, 256:512] = o[32:64]
        return 0

    lax.fori_loop(0, NR, one_row, 0)

    def spread(j, _):
        rows = pl.multiple_of(j * 96, 32)
        o = jnp.dot(xb[pl.ds(rows, 96), :], order_ref[...], preferred_element_type=F32)
        for kz in range(KB):
            part = o[:, (kz // 8) * 128 : (kz // 8 + 1) * 128]
            if kz % 8:
                part = pltpu.roll(part, 128 - 16 * (kz % 8), 1)
            box[pl.ds(pl.multiple_of(kz * NBOX + rows, 8), 96), :] = part
        return 0

    lax.fori_loop(0, NBOX // 96, spread, 0)

    def pick(j, _):
        base = pl.multiple_of(j * 32, 8)
        for k in range(32):
            sph[pl.ds(base + k, 1), :] = box[pl.ds(idx_ref[base + k], 1), :]
        return 0

    lax.fori_loop(0, NG // 32, pick, 0)
    sph[NG : NG + 64, :] = jnp.zeros((64, 128), F32)
    lane = lax.broadcasted_iota(jnp.int32, (16, 128), 1)
    row = lax.broadcasted_iota(jnp.int32, (16, 128), 0)
    unit = jnp.where(lane == row, 1.0, 0.0).astype(BF)
    contract = (((1,), (1,)), ((), ()))
    for g in range(NGRP):
        part = sph[g * RB : g * RB + RP, :].astype(BF)
        o = lax.dot_general(unit, part, contract, preferred_element_type=F32)
        row_ref[g] = (o * fac_ref[:, 0:1]).astype(BF)
    for s in range(NSLAB):
        part = sph[s * CB : s * CB + CP, :].astype(BF)
        col_ref[s] = lax.dot_general(unit, part, contract, preferred_element_type=F32).astype(BF)


def sphere_call(index, planes, factor):
    vmem = pl.BlockSpec(memory_space=pltpu.VMEM)
    return pl.pallas_call(
        sphere_kernel,
        name="sphere",
        out_shape=(
            jax.ShapeDtypeStruct((NGRP, 16, RP), BF),
            jax.ShapeDtypeStruct((NSLAB, 16, CP), BF),
        ),
        in_specs=[pl.BlockSpec(memory_space=pltpu.SMEM), vmem, vmem, vmem, vmem],
        out_specs=(vmem, vmem),
        scratch_shapes=[
            pltpu.VMEM((NBOX, 512), BF),
            pltpu.VMEM((KB * NBOX, 128), F32),
            pltpu.VMEM((NG + 64, 128), F32),
        ],
        compiler_params=pltpu.CompilerParams(vmem_limit_bytes=48 * 1024 * 1024),
    )(index, planes, jnp.asarray(box_weights()), jnp.asarray(lane_order()), factor)


def panels_kernel(row_ref, col_ref, rp_ref, cp_ref, landed, rsa, rra, csa, cra, rs, rr, cs, cr, sib_s, sib_r, lsem):
    g, gat = place_in_groups()
    s, sat = place_in_slabs()
    enter(
        [lax.rem(g + i, NGRP) for i in range(1, NGRP)],
        [lax.rem(s + i, NSLAB) for i in range(1, NSLAB)],
    )

    def row_out(i):
        to = lax.rem(g + i, NGRP)
        return remote(row_ref.at[to], landed.at[g], rsa.at[i], rra.at[g], {"grp": to})

    def row_in(i):
        src = lax.rem(g + i, NGRP)
        return remote(row_ref.at[src], landed.at[src], rsa.at[i], rra.at[src], {"grp": src})

    def col_out(i):
        to = lax.rem(s + i, NSLAB)
        return remote(col_ref.at[to], cp_ref.at[g, s], csa.at[i], cra.at[s], {"slab": to})

    def col_in(i):
        src = lax.rem(s + i, NSLAB)
        return remote(col_ref.at[src], cp_ref.at[g, src], csa.at[i], cra.at[src], {"slab": src})

    for i in range(1, NGRP):
        row_out(i).start()
    for i in range(1, NSLAB):
        col_out(i).start()
    keep_row = pltpu.make_async_copy(row_ref.at[g], landed.at[g], lsem.at[0])
    keep_col = pltpu.make_async_copy(col_ref.at[s], cp_ref.at[g, s], lsem.at[1])
    keep_row.start()
    keep_col.start()
    keep_row.wait()
    for i in range(1, NGRP):
        row_in(i).wait_recv()
    for j in range(RP // 128):
        part = landed[:, :, j * 128 : (j + 1) * 128].reshape(128, 128).astype(F32)
        rp_ref[s, j * 128 : (j + 1) * 128, :] = part.T.astype(BF)

    def sib(place, k):
        return remote(rp_ref.at[place], rp_ref.at[place], sib_s.at[k], sib_r.at[k], {"slab": sat(0, 0, 1)})

    def sib_in(place, k):
        return remote(rp_ref.at[place], rp_ref.at[place], sib_s.at[k], sib_r.at[k], {"slab": sat(0, 0, 1)})

    spots = [(0, 0), (0, 1), (-1, 0), (1, 0), (-1, 1), (1, 1), (2, 0), (2, 1)]

    def row_hop(k, spot, to):
        place = sat(*spots[spot], 0)
        return remote(rp_ref.at[place], rp_ref.at[place], rs.at[k], rr.at[LANDS[k]], {"slab": sat(*to, 0)})

    def row_wait(spot):
        place = sat(*spots[spot], 0)
        return remote(rp_ref.at[place], rp_ref.at[place], rs.at[0], rr.at[spot], {"slab": sat(0, 1, 0)})

    def col_hop(k, spot, to):
        place = gat(*spots[spot])
        return remote(cp_ref.at[place], cp_ref.at[place], cs.at[k], cr.at[LANDS[k]], {"grp": gat(*to)})

    def col_wait(spot):
        place = gat(*spots[spot])
        return remote(cp_ref.at[place], cp_ref.at[place], cs.at[0], cr.at[spot], {"grp": gat(0, 1)})

    hops = [(0, (0, 1)), (0, (1, 0)), (0, (-1, 0)), (1, (1, 0)), (1, (-1, 0)), (2, (1, 0)), (5, (-1, 0))]
    row_hops = [row_hop(k, spot, to) for k, (spot, to) in enumerate(hops)]
    col_hops = [col_hop(k, spot, to) for k, (spot, to) in enumerate(hops)]
    sibs = [sib(sat(*spot, 0), k) for k, spot in enumerate(spots)]
    for k in (1, 2, 0):
        row_hops[k].start()
    sibs[0].start()
    keep_col.wait()
    for i in range(1, NSLAB):
        col_in(i).wait_recv()
    for k in (1, 2, 0):
        col_hops[k].start()
    for spot, after in ((1, (3, 4)), (2, (5,)), (3, ()), (5, (6,)), (4, ()), (6, ()), (7, ())):
        col_wait(spot).wait_recv()
        for k in after:
            col_hops[k].start()
        row_wait(spot).wait_recv()
        for k in after:
            row_hops[k].start()
        sibs[spot].start()
    for k, spot in enumerate(spots):
        sib_in(sat(*spot, 1), k).wait_recv()
    for i in range(1, NGRP):
        row_out(i).wait_send()
    for i in range(1, NSLAB):
        col_out(i).wait_send()
    for copy in row_hops + col_hops + sibs:
        copy.wait_send()


LANDS = [1, 2, 3, 4, 5, 6, 7]


def panels_call(rows, columns):
    vmem = pl.BlockSpec(memory_space=pltpu.VMEM)
    dma = pltpu.SemaphoreType.DMA
    return pl.pallas_call(
        panels_kernel,
        name="panels",
        out_shape=(
            jax.ShapeDtypeStruct((NSLAB, RP, 128), BF),
            jax.ShapeDtypeStruct((NGRP, NSLAB, 16, CP), BF),
        ),
        in_specs=[vmem, vmem],
        out_specs=(vmem, vmem),
        scratch_shapes=[
            pltpu.VMEM((NGRP, 16, RP), BF),
            dma((NGRP,)),
            dma((NGRP,)),
            dma((NSLAB,)),
            dma((NSLAB,)),
            dma((7,)),
            dma((8,)),
            dma((7,)),
            dma((8,)),
            dma((8,)),
            dma((8,)),
            dma((2,)),
        ],
        compiler_params=pltpu.CompilerParams(
            collective_id=1, has_side_effects=True, vmem_limit_bytes=40 * 1024 * 1024
        ),
    )(rows, columns)


def tile_kernel(rp_ref, cp_ref, out_ref, ca, cb):
    @pl.when(pl.program_id(0) == 0)
    def _():
        def arrange(s, _):
            for g in range(NGRP):
                part = cp_ref[g, pl.ds(s, 1)].reshape(16, CP)
                rows = pl.ds(pl.multiple_of(s * 128 + g * 16, 16), 16)
                ca[rows, :] = part
                wide = part.astype(F32)
                cb[rows, :] = jnp.concatenate([-wide[8:16], wide[0:8]], 0).astype(BF)
            return 0

        lax.fori_loop(0, NSLAB, arrange, 0)

    left = jnp.concatenate([rp_ref[s] for s in range(NSLAB)], 1)
    out_ref[0] = jnp.dot(left, ca[...], preferred_element_type=F32)[:, :CB]
    out_ref[1] = jnp.dot(left, cb[...], preferred_element_type=F32)[:, :CB]


def tile_call(row_panel, column_panel):
    rows = 256
    return pl.pallas_call(
        tile_kernel,
        name="tile",
        grid=(RP // rows,),
        out_shape=jax.ShapeDtypeStruct((2, RB, CB), F32),
        in_specs=[
            pl.BlockSpec((NSLAB, rows, 128), lambda i: (0, i, 0)),
            pl.BlockSpec((NGRP, NSLAB, 16, CP), lambda i: (0, 0, 0, 0)),
        ],
        out_specs=pl.BlockSpec((2, rows, CB), lambda i: (0, i, 0)),
        scratch_shapes=[pltpu.VMEM((2048, CP), BF), pltpu.VMEM((2048, CP), BF)],
        compiler_params=pltpu.CompilerParams(vmem_limit_bytes=48 * 1024 * 1024),
    )(row_panel, column_panel)


def table_look_up(index, table):
    hot = index[:, None] == jnp.arange(KB, dtype=jnp.int32)[None, :]
    return jnp.sum(jnp.where(hot, jnp.asarray(table)[None, :], 0), 1)


def on_device(
    valence_waves, conduction_waves, valence_energy, conduction_energy, occupation, gvec_ids
):
    g, gat = place_in_groups()
    s = lax.axis_index("slab")
    row, shifted = row_tables()
    along_x = gvec_ids // (KB * KB)
    along_y = gvec_ids // KB % KB
    along_z = gvec_ids % KB
    place = table_look_up(along_y, row * KB + shifted * 1024 * KB)
    index = (along_z ^ (place // (1024 * KB))) * NBOX + place % (1024 * KB) + along_x

    bands = [(0, 0), (0, 1), (-1, 0), (1, 0), (-1, 1), (1, 1), (2, 0), (2, 1)]
    order = jnp.stack([gat(*spot) for spot in bands])
    hot = (order[:, None] == jnp.arange(NV, dtype=jnp.int32)[None, :]).astype(F32)
    full = occupation.astype(F32)[:, None] / (
        (valence_energy[:, None] - conduction_energy[None, :]) * math.sqrt(NV * NC)
    )
    mine = jnp.sum(jnp.where(jnp.arange(NSLAB)[None, :] == s, full, 0.0), 1)
    factor = jnp.sum(hot * mine[None, :], 1)
    factor = jnp.broadcast_to(jnp.concatenate([factor, factor])[:, None], (16, 128))

    planes = planes_call(valence_waves, conduction_waves)
    rows, columns = sphere_call(index, planes, factor)
    row_panel, column_panel = panels_call(rows, columns)
    return tile_call(row_panel, column_panel)


def solution(mesh):
    in_specs = (P("grp", "slab", None, None), P("grp", "slab", None, None), P(), P("grp"), P(), P())
    out_specs = P(None, "grp", "slab")
    return jax.shard_map(
        on_device, mesh=mesh, in_specs=in_specs, out_specs=out_specs, check_vma=False
    )
```

```python
import functools
import math

import jax
import jax.numpy as jnp
import ml_dtypes
import numpy as np
from jax import lax
from jax.experimental import pallas as pl
from jax.experimental.pallas import tpu as pltpu
from jax.sharding import PartitionSpec as P

NV = 8
NC = 128
NF = 128
KB = 32
NG = 12000
NGRP = 8
NSLAB = 16
NX = NF // NSLAB
NR = 24
RB = NG // NGRP
CB = NG // NSLAB
RP = 1536
CP = 768
NBOX = NR * KB
MESH = pl.DeviceIdType.MESH
BF = jnp.bfloat16
F32 = jnp.float32

WIDE = [9, -9, 11, -11, 5, -5]
NARROW = [13, -13, 12, -12, 14, -14]
SINGLE = [0, 1, -1, 2, -2, 3, -3, 4, -4, 6, -6, 7, -7, 8, -8, 10, -10]
ROW_FREQ = SINGLE[:16] + [SINGLE[16]] + WIDE + [15] + [15] + NARROW + [15]


def freq(j):
    return j - KB if j >= KB // 2 else j


def row_tables():
    row = np.zeros(KB, np.int32)
    shifted = np.zeros(KB, np.int32)
    for place, f in enumerate(ROW_FREQ[:NR]):
        if f != 15:
            row[f % KB] = place
    for place, f in enumerate(NARROW):
        row[f % KB] = 17 + place
        shifted[f % KB] = KB // 2
    return row, shifted


def phases(positions, freqs):
    angle = np.mod(np.outer(positions, freqs), NF).astype(np.float32) * np.float32(2.0 * math.pi / NF)
    return np.cos(angle).astype(np.float32), np.sin(angle).astype(np.float32)


def depth_weights():
    cos, sin = phases(np.arange(NF), [freq(j) for j in range(KB)])
    w = np.zeros((4, 2, NF, 2, KB, 4), np.float32)
    for vl in range(4):
        w[vl, 0, :, 0, :, vl] = cos
        w[vl, 1, :, 0, :, vl] = sin
        w[vl, 0, :, 1, :, vl] = -sin
        w[vl, 1, :, 1, :, vl] = cos
    return w.reshape(8 * NF, 8 * KB).astype(ml_dtypes.bfloat16)


def height_weights():
    cos, sin = phases(np.arange(NF), ROW_FREQ)
    return np.concatenate([cos.T, sin.T], 0).astype(ml_dtypes.bfloat16)


def wide_mask():
    mask = np.ones((8, KB, 4), np.float32)
    for place, f in enumerate(WIDE):
        half = math.isqrt(196 - f * f)
        for j in range(KB):
            if abs(freq(j)) > half:
                mask[1 + place, j] = 0.0
    return mask.reshape(8, 4 * KB)


def box_weights():
    cos, sin = phases(np.arange(NF), [freq(j) for j in range(KB)])
    cos, sin = cos.T.reshape(KB, NSLAB, NX), sin.T.reshape(KB, NSLAB, NX)
    t = np.zeros((2, KB, NSLAB, 2, NX), np.float32)
    t[0, :, :, 0] = cos
    t[0, :, :, 1] = sin
    t[1, :, :, 0] = -sin
    t[1, :, :, 1] = cos
    t = t.reshape(2 * KB, 2 * NF)
    high = t.astype(ml_dtypes.bfloat16)
    low = (t - high.astype(np.float32)).astype(ml_dtypes.bfloat16)
    return np.concatenate([high, low], 0)


def lane_order():
    m = np.zeros((2, 2, KB, 4, KB, 2, 2, 4), np.float32)
    for reim in range(2):
        for vg in range(2):
            for kz in range(KB):
                for vl in range(4):
                    m[reim, vg, kz, vl, kz, reim, vg, vl] = 1.0
    return m.reshape(512, 512).astype(ml_dtypes.bfloat16)


def place_in_groups():
    g = lax.axis_index("grp")
    gx, gz = g // 2, lax.rem(g, 2)

    def at(dx, dz):
        return lax.rem(gx + dx + 4, 4) * 2 + (lax.rem(gz + dz, 2))

    return g, at


def place_in_slabs():
    s = lax.axis_index("slab")
    sz, sy, sc = s // 8, lax.rem(s // 2, 4), lax.rem(s, 2)

    def at(dy, dz, dc):
        return lax.rem(sz + dz, 2) * 8 + lax.rem(sy + dy + 4, 4) * 2 + lax.rem(sc + dc, 2)

    return s, at


def enter(groups, slabs):
    barrier = pltpu.get_barrier_semaphore()
    for one in groups:
        pl.semaphore_signal(barrier, inc=1, device_id={"grp": one}, device_id_type=MESH)
    for one in slabs:
        pl.semaphore_signal(barrier, inc=1, device_id={"slab": one}, device_id_type=MESH)
    pl.semaphore_wait(barrier, len(groups) + len(slabs))


def remote(src, dst, send, recv, device):
    return pltpu.make_async_remote_copy(
        src_ref=src, dst_ref=dst, send_sem=send, recv_sem=recv, device_id=device, device_id_type=MESH
    )


def planes_kernel(
    val_ref, con_ref, wz_ref, ty_ref, mask_ref, out_ref, val, con, msg, wz, even, odd, first, scr, con_sem, own_sem, wz_sem, vs, vr, ms, mr, local_sem
):
    g, gat = place_in_groups()
    s, sat = place_in_slabs()
    own = pltpu.make_async_copy(val_ref.at[0], val.at[0], own_sem)
    own.start()
    weights = pltpu.make_async_copy(wz_ref, wz, wz_sem)
    weights.start()

    def con_copy(c):
        return pltpu.make_async_copy(con_ref.at[c], con.at[c], con_sem.at[c])

    def start_con(i, _):
        con_copy(lax.rem(s + i + 1, NSLAB)).start()
        return 0

    lax.fori_loop(0, NSLAB, start_con, 0)
    partner, ahead, behind = gat(0, 1), gat(1, 0), gat(-1, 0)
    enter([partner, ahead, behind], [lax.rem(s + i, NSLAB) for i in range(1, NSLAB)])
    own.wait()

    def hop(k, slot, to, landing):
        return remote(val.at[slot], val.at[landing], vs.at[k], vr.at[landing], {"grp": to})

    to_partner, to_ahead, to_behind = hop(0, 0, partner, 1), hop(1, 0, ahead, 2), hop(2, 0, behind, 3)
    to_ahead.start()
    to_behind.start()
    to_partner.start()
    p_ahead, p_behind = hop(3, 1, ahead, 4), hop(4, 1, behind, 5)
    l_ahead, r_behind = hop(5, 2, ahead, 6), hop(6, 5, behind, 7)
    to_partner.wait_recv()
    p_behind.start()
    p_ahead.start()
    to_ahead.wait_recv()
    l_ahead.start()
    to_behind.wait_recv()
    weights.wait()

    def message(vg, c):
        return remote(
            msg.at[vg, c], out_ref.at[vg, s], ms.at[vg, c], mr.at[vg, s], {"slab": c}
        )

    def arrival(vg, src):
        return remote(
            msg.at[vg, src], out_ref.at[vg, src], ms.at[vg, src], mr.at[vg, src], {"slab": src}
        )

    def density(vg, c, half, buf):
        for x in range(half * 4, half * 4 + 4):
            for y0 in range(0, NF, 32):
                rows = pl.ds(y0, 32)
                put = pl.ds(x * NF + y0, 32)
                cr = con[c, x, rows, 0:NF].astype(F32)
                ci = con[c, x, rows, NF : 2 * NF].astype(F32)
                for vl in range(4):
                    pr = val[vg * 4 + vl, x, rows, 0:NF].astype(F32)
                    pi = val[vg * 4 + vl, x, rows, NF : 2 * NF].astype(F32)
                    buf[put, vl * 256 : vl * 256 + NF] = (pr * cr + pi * ci).astype(BF)
                    buf[put, vl * 256 + NF : vl * 256 + 256] = (pr * ci - pi * cr).astype(BF)

    def along_z(half, buf):
        rows = pl.ds(half * 512, 512)
        first[rows, :] = jnp.dot(buf[rows, :], wz[...], preferred_element_type=F32).astype(BF)

    def along_y(half):
        for x in range(half * 4, half * 4 + 4):
            o = jnp.dot(ty_ref[...], first[x * NF : x * NF + NF, :], preferred_element_type=F32)
            keep = mask_ref[...] > 0.5
            for reim in range(2):
                if reim == 0:
                    full = o[0:32, 0:128] + o[32:64, 128:256]
                else:
                    full = o[0:32, 128:256] - o[32:64, 0:128]
                merged = jnp.where(keep, full[16:24], pltpu.roll(full[24:32], 64, 1))
                scr[reim, x * NR : x * NR + 16, :] = full[0:16]
                scr[reim, x * NR + 16 : x * NR + 24, :] = merged

    def pack(vg, c):
        for r in range(NR):
            both = jnp.concatenate(
                [scr[0, pl.ds(r, NX, stride=NR), :], scr[1, pl.ds(r, NX, stride=NR), :]], 0
            )
            msg[vg, c, r] = both.astype(BF)

    def one_band(vg, c, after, buf, other):
        along_z(0, buf)
        density(vg, after, 0, other)
        along_z(1, buf)
        density(vg, after, 1, other)
        along_y(0)
        along_y(1)
        pack(vg, c)

    for vg in range(2):
        if vg == 1:
            p_ahead.wait_recv()
            l_ahead.wait_recv()
            r_behind.wait_recv()
        start = lax.rem(s + 1, NSLAB)
        if vg == 0:
            con_copy(start).wait()
        density(vg, start, 0, even)
        density(vg, start, 1, even)

        def two_bands(j, _):
            c0 = lax.rem(s + 2 * j + 1, NSLAB)
            c1 = lax.rem(s + 2 * j + 2, NSLAB)
            c2 = lax.rem(s + 2 * j + 3, NSLAB)
            if vg == 0:
                con_copy(c1).wait()
            one_band(vg, c0, c1, even, odd)
            message(vg, c0).start()
            if vg == 0:

                @pl.when(j == 3)
                def _():
                    p_behind.wait_recv()
                    r_behind.start()

                @pl.when(j < NSLAB // 2 - 1)
                def _():
                    con_copy(c2).wait()

            one_band(vg, c1, c2, odd, even)

            @pl.when(j < NSLAB // 2 - 1)
            def _():
                message(vg, c1).start()

            @pl.when(j == NSLAB // 2 - 1)
            def _():
                pltpu.make_async_copy(msg.at[vg, c1], out_ref.at[vg, s], local_sem.at[vg]).start()

            return 0

        lax.fori_loop(0, NSLAB // 2, two_bands, 0)

    def finish(i, _):
        other = lax.rem(s + i + 1, NSLAB)
        for vg in range(2):
            arrival(vg, other).wait_recv()
            message(vg, other).wait_send()
        return 0

    lax.fori_loop(0, NSLAB - 1, finish, 0)
    for vg in range(2):
        pltpu.make_async_copy(msg.at[vg, s], out_ref.at[vg, s], local_sem.at[vg]).wait()
    for copy in (to_partner, to_ahead, to_behind, p_ahead, p_behind, l_ahead, r_behind):
        copy.wait_send()


def planes_call(valence, conduction):
    anywhere = pl.BlockSpec(memory_space=pl.ANY)
    vmem = pl.BlockSpec(memory_space=pltpu.VMEM)
    return pl.pallas_call(
        planes_kernel,
        name="planes",
        out_shape=jax.ShapeDtypeStruct((2, NSLAB, NR, 2 * NX, 128), BF),
        in_specs=[anywhere, anywhere, anywhere, vmem, vmem],
        out_specs=anywhere,
        scratch_shapes=[
            pltpu.VMEM((8, NX, NF, 2 * NF), BF),
            pltpu.VMEM((NSLAB, NX, NF, 2 * NF), BF),
            pltpu.VMEM((2, NSLAB, NR, 2 * NX, 128), BF),
            pltpu.VMEM((8 * NF, 2 * NF), BF),
            pltpu.VMEM((NX * NF, 8 * NF), BF),
            pltpu.VMEM((NX * NF, 8 * NF), BF),
            pltpu.VMEM((NX * NF, 2 * NF), BF),
            pltpu.VMEM((2, NX * NR, 128), F32),
            pltpu.SemaphoreType.DMA((NSLAB,)),
            pltpu.SemaphoreType.DMA,
            pltpu.SemaphoreType.DMA,
            pltpu.SemaphoreType.DMA((7,)),
            pltpu.SemaphoreType.DMA((8,)),
            pltpu.SemaphoreType.DMA((2, NSLAB)),
            pltpu.SemaphoreType.DMA((2, NSLAB)),
            pltpu.SemaphoreType.DMA((2,)),
        ],
        compiler_params=pltpu.CompilerParams(
            collective_id=0, has_side_effects=True, vmem_limit_bytes=56 * 1024 * 1024
        ),
    )(
        valence,
        conduction,
        jnp.asarray(depth_weights()),
        jnp.asarray(height_weights()),
        jnp.asarray(wide_mask()),
    )


def sphere_kernel(idx_ref, in_ref, tab_ref, order_ref, fac_ref, row_ref, col_ref, xb, box, sph):
    scaling = 0.5 / float(NF) ** 1.5

    def one_row(r, _):
        a = [in_ref[vg, :, pl.ds(r, 1)].reshape(2 * NF, 128) for vg in range(2)]
        o = jnp.dot(tab_ref[...], jnp.concatenate(a, 1), preferred_element_type=F32)
        o = ((o[0:64] + o[64:128]) * scaling).astype(BF)
        rows = pl.ds(pl.multiple_of(r * KB, KB), KB)
        xb[rows, 0:256] = o[0:32]
        xb[rows, 256:512] = o[32:64]
        return 0

    lax.fori_loop(0, NR, one_row, 0)

    def spread(j, _):
        rows = pl.multiple_of(j * 96, 32)
        o = jnp.dot(xb[pl.ds(rows, 96), :], order_ref[...], preferred_element_type=F32)
        for kz in range(KB):
            part = o[:, (kz // 8) * 128 : (kz // 8 + 1) * 128]
            if kz % 8:
                part = pltpu.roll(part, 128 - 16 * (kz % 8), 1)
            box[pl.ds(pl.multiple_of(kz * NBOX + rows, 8), 96), :] = part
        return 0

    lax.fori_loop(0, NBOX // 96, spread, 0)

    def pick(j, _):
        base = pl.multiple_of(j * 32, 8)
        for k in range(32):
            sph[pl.ds(base + k, 1), :] = box[pl.ds(idx_ref[base + k], 1), :]
        return 0

    lax.fori_loop(0, NG // 32, pick, 0)
    sph[NG : NG + 64, :] = jnp.zeros((64, 128), F32)
    lane = lax.broadcasted_iota(jnp.int32, (16, 128), 1)
    row = lax.broadcasted_iota(jnp.int32, (16, 128), 0)
    unit = jnp.where(lane == row, 1.0, 0.0).astype(BF)
    contract = (((1,), (1,)), ((), ()))
    for g in range(NGRP):
        part = sph[g * RB : g * RB + RP, :].astype(BF)
        o = lax.dot_general(unit, part, contract, preferred_element_type=F32)
        row_ref[g] = (o * fac_ref[:, 0:1]).astype(BF)
    for s in range(NSLAB):
        part = sph[s * CB : s * CB + CP, :].astype(BF)
        col_ref[s] = lax.dot_general(unit, part, contract, preferred_element_type=F32).astype(BF)


def sphere_call(index, planes, factor):
    vmem = pl.BlockSpec(memory_space=pltpu.VMEM)
    return pl.pallas_call(
        sphere_kernel,
        name="sphere",
        out_shape=(
            jax.ShapeDtypeStruct((NGRP, 16, RP), BF),
            jax.ShapeDtypeStruct((NSLAB, 16, CP), BF),
        ),
        in_specs=[pl.BlockSpec(memory_space=pltpu.SMEM), vmem, vmem, vmem, vmem],
        out_specs=(vmem, vmem),
        scratch_shapes=[
            pltpu.VMEM((NBOX, 512), BF),
            pltpu.VMEM((KB * NBOX, 128), F32),
            pltpu.VMEM((NG + 64, 128), F32),
        ],
        compiler_params=pltpu.CompilerParams(vmem_limit_bytes=48 * 1024 * 1024),
    )(index, planes, jnp.asarray(box_weights()), jnp.asarray(lane_order()), factor)


def panels_kernel(row_ref, col_ref, rp_ref, cp_ref, landed, rsa, rra, csa, cra, rs, rr, cs, cr, sib_s, sib_r, lsem):
    g, gat = place_in_groups()
    s, sat = place_in_slabs()
    enter(
        [lax.rem(g + i, NGRP) for i in range(1, NGRP)],
        [lax.rem(s + i, NSLAB) for i in range(1, NSLAB)],
    )

    def row_out(i):
        to = lax.rem(g + i, NGRP)
        return remote(row_ref.at[to], landed.at[g], rsa.at[i], rra.at[g], {"grp": to})

    def row_in(i):
        src = lax.rem(g + i, NGRP)
        return remote(row_ref.at[src], landed.at[src], rsa.at[i], rra.at[src], {"grp": src})

    def col_out(i):
        to = lax.rem(s + i, NSLAB)
        return remote(col_ref.at[to], cp_ref.at[g, s], csa.at[i], cra.at[s], {"slab": to})

    def col_in(i):
        src = lax.rem(s + i, NSLAB)
        return remote(col_ref.at[src], cp_ref.at[g, src], csa.at[i], cra.at[src], {"slab": src})

    for i in range(1, NGRP):
        row_out(i).start()
    for i in range(1, NSLAB):
        col_out(i).start()
    keep_row = pltpu.make_async_copy(row_ref.at[g], landed.at[g], lsem.at[0])
    keep_col = pltpu.make_async_copy(col_ref.at[s], cp_ref.at[g, s], lsem.at[1])
    keep_row.start()
    keep_col.start()
    keep_row.wait()
    for i in range(1, NGRP):
        row_in(i).wait_recv()
    for j in range(RP // 128):
        part = landed[:, :, j * 128 : (j + 1) * 128].reshape(128, 128).astype(F32)
        rp_ref[s, j * 128 : (j + 1) * 128, :] = part.T.astype(BF)

    def sib(place, k):
        return remote(rp_ref.at[place], rp_ref.at[place], sib_s.at[k], sib_r.at[k], {"slab": sat(0, 0, 1)})

    def sib_in(place, k):
        return remote(rp_ref.at[place], rp_ref.at[place], sib_s.at[k], sib_r.at[k], {"slab": sat(0, 0, 1)})

    spots = [(0, 0), (0, 1), (-1, 0), (1, 0), (-1, 1), (1, 1), (2, 0), (2, 1)]

    def row_hop(k, spot, to):
        place = sat(*spots[spot], 0)
        return remote(rp_ref.at[place], rp_ref.at[place], rs.at[k], rr.at[LANDS[k]], {"slab": sat(*to, 0)})

    def row_wait(spot):
        place = sat(*spots[spot], 0)
        return remote(rp_ref.at[place], rp_ref.at[place], rs.at[0], rr.at[spot], {"slab": sat(0, 1, 0)})

    def col_hop(k, spot, to):
        place = gat(*spots[spot])
        return remote(cp_ref.at[place], cp_ref.at[place], cs.at[k], cr.at[LANDS[k]], {"grp": gat(*to)})

    def col_wait(spot):
        place = gat(*spots[spot])
        return remote(cp_ref.at[place], cp_ref.at[place], cs.at[0], cr.at[spot], {"grp": gat(0, 1)})

    hops = [(0, (0, 1)), (0, (1, 0)), (0, (-1, 0)), (1, (1, 0)), (1, (-1, 0)), (2, (1, 0)), (5, (-1, 0))]
    row_hops = [row_hop(k, spot, to) for k, (spot, to) in enumerate(hops)]
    col_hops = [col_hop(k, spot, to) for k, (spot, to) in enumerate(hops)]
    sibs = [sib(sat(*spot, 0), k) for k, spot in enumerate(spots)]
    for k in (1, 2, 0):
        row_hops[k].start()
    sibs[0].start()
    keep_col.wait()
    for i in range(1, NSLAB):
        col_in(i).wait_recv()
    for k in (1, 2, 0):
        col_hops[k].start()
    for spot, after in ((1, (3, 4)), (2, (5,)), (3, ()), (5, (6,)), (4, ()), (6, ()), (7, ())):
        col_wait(spot).wait_recv()
        for k in after:
            col_hops[k].start()
        row_wait(spot).wait_recv()
        for k in after:
            row_hops[k].start()
        sibs[spot].start()
    for k, spot in enumerate(spots):
        sib_in(sat(*spot, 1), k).wait_recv()
    for i in range(1, NGRP):
        row_out(i).wait_send()
    for i in range(1, NSLAB):
        col_out(i).wait_send()
    for copy in row_hops + col_hops + sibs:
        copy.wait_send()


LANDS = [1, 2, 3, 4, 5, 6, 7]


def panels_call(rows, columns):
    vmem = pl.BlockSpec(memory_space=pltpu.VMEM)
    dma = pltpu.SemaphoreType.DMA
    return pl.pallas_call(
        panels_kernel,
        name="panels",
        out_shape=(
            jax.ShapeDtypeStruct((NSLAB, RP, 128), BF),
            jax.ShapeDtypeStruct((NGRP, NSLAB, 16, CP), BF),
        ),
        in_specs=[vmem, vmem],
        out_specs=(vmem, vmem),
        scratch_shapes=[
            pltpu.VMEM((NGRP, 16, RP), BF),
            dma((NGRP,)),
            dma((NGRP,)),
            dma((NSLAB,)),
            dma((NSLAB,)),
            dma((7,)),
            dma((8,)),
            dma((7,)),
            dma((8,)),
            dma((8,)),
            dma((8,)),
            dma((2,)),
        ],
        compiler_params=pltpu.CompilerParams(
            collective_id=1, has_side_effects=True, vmem_limit_bytes=40 * 1024 * 1024
        ),
    )(rows, columns)


def tile_kernel(rp_ref, cp_ref, out_ref, ca, cb):
    @pl.when(pl.program_id(0) == 0)
    def _():
        def arrange(s, _):
            for g in range(NGRP):
                part = cp_ref[g, pl.ds(s, 1)].reshape(16, CP)
                rows = pl.ds(pl.multiple_of(s * 128 + g * 16, 16), 16)
                ca[rows, :] = part
                wide = part.astype(F32)
                cb[rows, :] = jnp.concatenate([-wide[8:16], wide[0:8]], 0).astype(BF)
            return 0

        lax.fori_loop(0, NSLAB, arrange, 0)

    left = jnp.concatenate([rp_ref[s] for s in range(NSLAB)], 1)
    out_ref[:, 0, :] = jnp.dot(left, ca[...], preferred_element_type=F32)[:, :CB]
    out_ref[:, 1, :] = jnp.dot(left, cb[...], preferred_element_type=F32)[:, :CB]


def tile_call(row_panel, column_panel):
    rows = 256
    tiles = pl.pallas_call(
        tile_kernel,
        name="tile",
        grid=(RP // rows,),
        out_shape=jax.ShapeDtypeStruct((RB, 2, CB), F32),
        in_specs=[
            pl.BlockSpec((NSLAB, rows, 128), lambda i: (0, i, 0)),
            pl.BlockSpec((NGRP, NSLAB, 16, CP), lambda i: (0, 0, 0, 0)),
        ],
        out_specs=pl.BlockSpec((rows, 2, CB), lambda i: (i, 0, 0)),
        scratch_shapes=[pltpu.VMEM((2048, CP), BF), pltpu.VMEM((2048, CP), BF)],
        compiler_params=pltpu.CompilerParams(vmem_limit_bytes=48 * 1024 * 1024),
    )(row_panel, column_panel)
    return jnp.transpose(tiles, (1, 0, 2))


def table_look_up(index, table):
    hot = index[:, None] == jnp.arange(KB, dtype=jnp.int32)[None, :]
    return jnp.sum(jnp.where(hot, jnp.asarray(table)[None, :], 0), 1)


def on_device(
    valence_waves, conduction_waves, valence_energy, conduction_energy, occupation, gvec_ids
):
    g, gat = place_in_groups()
    s = lax.axis_index("slab")
    row, shifted = row_tables()
    along_x = gvec_ids // (KB * KB)
    along_y = gvec_ids // KB % KB
    along_z = gvec_ids % KB
    place = table_look_up(along_y, row * KB + shifted * 1024 * KB)
    index = (along_z ^ (place // (1024 * KB))) * NBOX + place % (1024 * KB) + along_x

    bands = [(0, 0), (0, 1), (-1, 0), (1, 0), (-1, 1), (1, 1), (2, 0), (2, 1)]
    order = jnp.stack([gat(*spot) for spot in bands])
    hot = (order[:, None] == jnp.arange(NV, dtype=jnp.int32)[None, :]).astype(F32)
    full = occupation.astype(F32)[:, None] / (
        (valence_energy[:, None] - conduction_energy[None, :]) * math.sqrt(NV * NC)
    )
    mine = jnp.sum(jnp.where(jnp.arange(NSLAB)[None, :] == s, full, 0.0), 1)
    factor = jnp.sum(hot * mine[None, :], 1)
    factor = jnp.broadcast_to(jnp.concatenate([factor, factor])[:, None], (16, 128))

    planes = planes_call(valence_waves, conduction_waves)
    rows, columns = sphere_call(index, planes, factor)
    row_panel, column_panel = panels_call(rows, columns)
    return tile_call(row_panel, column_panel)


def solution(mesh):
    in_specs = (P("grp", "slab", None, None), P("grp", "slab", None, None), P(), P("grp"), P(), P())
    out_specs = P(None, "grp", "slab")
    return jax.shard_map(
        on_device, mesh=mesh, in_specs=in_specs, out_specs=out_specs, check_vma=False
    )
```

```python
import functools
import math

import jax
import jax.numpy as jnp
import ml_dtypes
import numpy as np
from jax import lax
from jax.experimental import pallas as pl
from jax.experimental.pallas import tpu as pltpu
from jax.sharding import PartitionSpec as P

NV = 8
NC = 128
NF = 128
KB = 32
NG = 12000
NGRP = 8
NSLAB = 16
NX = NF // NSLAB
NR = 24
RB = NG // NGRP
CB = NG // NSLAB
RP = 1536
CP = 768
NBOX = NR * KB
MESH = pl.DeviceIdType.MESH
BF = jnp.bfloat16
F32 = jnp.float32

WIDE = [9, -9, 11, -11, 5, -5]
NARROW = [13, -13, 12, -12, 14, -14]
SINGLE = [0, 1, -1, 2, -2, 3, -3, 4, -4, 6, -6, 7, -7, 8, -8, 10, -10]
ROW_FREQ = SINGLE[:16] + [SINGLE[16]] + WIDE + [15] + [15] + NARROW + [15]


def freq(j):
    return j - KB if j >= KB // 2 else j


def row_tables():
    row = np.zeros(KB, np.int32)
    shifted = np.zeros(KB, np.int32)
    for place, f in enumerate(ROW_FREQ[:NR]):
        if f != 15:
            row[f % KB] = place
    for place, f in enumerate(NARROW):
        row[f % KB] = 17 + place
        shifted[f % KB] = KB // 2
    return row, shifted


def phases(positions, freqs):
    angle = np.mod(np.outer(positions, freqs), NF).astype(np.float32) * np.float32(2.0 * math.pi / NF)
    return np.cos(angle).astype(np.float32), np.sin(angle).astype(np.float32)


def depth_weights():
    cos, sin = phases(np.arange(NF), [freq(j) for j in range(KB)])
    w = np.zeros((4, 2, NF, 2, KB, 4), np.float32)
    for vl in range(4):
        w[vl, 0, :, 0, :, vl] = cos
        w[vl, 1, :, 0, :, vl] = sin
        w[vl, 0, :, 1, :, vl] = -sin
        w[vl, 1, :, 1, :, vl] = cos
    return w.reshape(8 * NF, 8 * KB).astype(ml_dtypes.bfloat16)


def height_weights():
    cos, sin = phases(np.arange(NF), ROW_FREQ)
    return np.concatenate([cos.T, sin.T], 0).astype(ml_dtypes.bfloat16)


def wide_mask():
    mask = np.ones((8, KB, 4), np.float32)
    for place, f in enumerate(WIDE):
        half = math.isqrt(196 - f * f)
        for j in range(KB):
            if abs(freq(j)) > half:
                mask[1 + place, j] = 0.0
    return mask.reshape(8, 4 * KB)


def box_weights():
    cos, sin = phases(np.arange(NF), [freq(j) for j in range(KB)])
    cos, sin = cos.T.reshape(KB, NSLAB, NX), sin.T.reshape(KB, NSLAB, NX)
    t = np.zeros((2, KB, NSLAB, 2, NX), np.float32)
    t[0, :, :, 0] = cos
    t[0, :, :, 1] = sin
    t[1, :, :, 0] = -sin
    t[1, :, :, 1] = cos
    t = t.reshape(2 * KB, 2 * NF)
    high = t.astype(ml_dtypes.bfloat16)
    low = (t - high.astype(np.float32)).astype(ml_dtypes.bfloat16)
    return np.concatenate([high, low], 0)


def lane_order():
    m = np.zeros((2, 2, KB, 4, KB, 2, 2, 4), np.float32)
    for reim in range(2):
        for vg in range(2):
            for kz in range(KB):
                for vl in range(4):
                    m[reim, vg, kz, vl, kz, reim, vg, vl] = 1.0
    return m.reshape(512, 512).astype(ml_dtypes.bfloat16)


def place_in_groups():
    g = lax.axis_index("grp")
    gx, gz = g // 2, lax.rem(g, 2)

    def at(dx, dz):
        return lax.rem(gx + dx + 4, 4) * 2 + (lax.rem(gz + dz, 2))

    return g, at


def place_in_slabs():
    s = lax.axis_index("slab")
    sz, sy, sc = s // 8, lax.rem(s // 2, 4), lax.rem(s, 2)

    def at(dy, dz, dc):
        return lax.rem(sz + dz, 2) * 8 + lax.rem(sy + dy + 4, 4) * 2 + lax.rem(sc + dc, 2)

    return s, at


def enter(groups, slabs):
    barrier = pltpu.get_barrier_semaphore()
    for one in groups:
        pl.semaphore_signal(barrier, inc=1, device_id={"grp": one}, device_id_type=MESH)
    for one in slabs:
        pl.semaphore_signal(barrier, inc=1, device_id={"slab": one}, device_id_type=MESH)
    pl.semaphore_wait(barrier, len(groups) + len(slabs))


def remote(src, dst, send, recv, device):
    return pltpu.make_async_remote_copy(
        src_ref=src, dst_ref=dst, send_sem=send, recv_sem=recv, device_id=device, device_id_type=MESH
    )


def planes_kernel(
    val_ref, con_ref, wz_ref, ty_ref, mask_ref, out_ref, val, con, msg, wz, even, odd, first, scr, con_sem, own_sem, wz_sem, vs, vr, ms, mr, local_sem
):
    g, gat = place_in_groups()
    s, sat = place_in_slabs()
    own = pltpu.make_async_copy(val_ref.at[0], val.at[0], own_sem)
    own.start()
    weights = pltpu.make_async_copy(wz_ref, wz, wz_sem)
    weights.start()

    def con_copy(c):
        return pltpu.make_async_copy(con_ref.at[c], con.at[c], con_sem.at[c])

    def start_con(i, _):
        con_copy(lax.rem(s + i + 1, NSLAB)).start()
        return 0

    lax.fori_loop(0, NSLAB, start_con, 0)
    partner, ahead, behind = gat(0, 1), gat(1, 0), gat(-1, 0)
    enter([partner, ahead, behind], [lax.rem(s + i, NSLAB) for i in range(1, NSLAB)])
    own.wait()

    def hop(k, slot, to, landing):
        return remote(val.at[slot], val.at[landing], vs.at[k], vr.at[landing], {"grp": to})

    to_partner, to_ahead, to_behind = hop(0, 0, partner, 1), hop(1, 0, ahead, 2), hop(2, 0, behind, 3)
    to_ahead.start()
    to_behind.start()
    to_partner.start()
    p_ahead, p_behind = hop(3, 1, ahead, 4), hop(4, 1, behind, 5)
    l_ahead, r_behind = hop(5, 2, ahead, 6), hop(6, 5, behind, 7)
    to_partner.wait_recv()
    p_behind.start()
    p_ahead.start()
    to_ahead.wait_recv()
    l_ahead.start()
    to_behind.wait_recv()
    weights.wait()

    def message(vg, c):
        return remote(
            msg.at[vg, c], out_ref.at[vg, s], ms.at[vg, c], mr.at[vg, s], {"slab": c}
        )

    def arrival(vg, src):
        return remote(
            msg.at[vg, src], out_ref.at[vg, src], ms.at[vg, src], mr.at[vg, src], {"slab": src}
        )

    def density(vg, c, half, buf):
        for x in range(half * 4, half * 4 + 4):
            for y0 in range(0, NF, 32):
                rows = pl.ds(y0, 32)
                put = pl.ds(x * NF + y0, 32)
                cr = con[c, x, rows, 0:NF].astype(F32)
                ci = con[c, x, rows, NF : 2 * NF].astype(F32)
                for vl in range(4):
                    pr = val[vg * 4 + vl, x, rows, 0:NF].astype(F32)
                    pi = val[vg * 4 + vl, x, rows, NF : 2 * NF].astype(F32)
                    buf[put, vl * 256 : vl * 256 + NF] = (pr * cr + pi * ci).astype(BF)
                    buf[put, vl * 256 + NF : vl * 256 + 256] = (pr * ci - pi * cr).astype(BF)

    def along_z(half, buf):
        rows = pl.ds(half * 512, 512)
        first[rows, :] = jnp.dot(buf[rows, :], wz[...], preferred_element_type=F32).astype(BF)

    def along_y(half):
        for x in range(half * 4, half * 4 + 4):
            o = jnp.dot(ty_ref[...], first[x * NF : x * NF + NF, :], preferred_element_type=F32)
            keep = mask_ref[...] > 0.5
            for reim in range(2):
                if reim == 0:
                    full = o[0:32, 0:128] + o[32:64, 128:256]
                else:
                    full = o[0:32, 128:256] - o[32:64, 0:128]
                merged = jnp.where(keep, full[16:24], pltpu.roll(full[24:32], 64, 1))
                scr[reim, x * NR : x * NR + 16, :] = full[0:16]
                scr[reim, x * NR + 16 : x * NR + 24, :] = merged

    def pack(vg, c):
        for r in range(NR):
            both = jnp.concatenate(
                [scr[0, pl.ds(r, NX, stride=NR), :], scr[1, pl.ds(r, NX, stride=NR), :]], 0
            )
            msg[vg, c, r] = both.astype(BF)

    def one_band(vg, c, after, buf, other):
        along_z(0, buf)
        density(vg, after, 0, other)
        along_z(1, buf)
        density(vg, after, 1, other)
        along_y(0)
        along_y(1)
        pack(vg, c)

    for vg in range(2):
        if vg == 1:
            p_ahead.wait_recv()
            l_ahead.wait_recv()
            r_behind.wait_recv()
        start = lax.rem(s + 1, NSLAB)
        if vg == 0:
            con_copy(start).wait()
        density(vg, start, 0, even)
        density(vg, start, 1, even)

        def two_bands(j, _):
            c0 = lax.rem(s + 2 * j + 1, NSLAB)
            c1 = lax.rem(s + 2 * j + 2, NSLAB)
            c2 = lax.rem(s + 2 * j + 3, NSLAB)
            if vg == 0:
                con_copy(c1).wait()
            one_band(vg, c0, c1, even, odd)
            message(vg, c0).start()
            if vg == 0:

                @pl.when(j == 3)
                def _():
                    p_behind.wait_recv()
                    r_behind.start()

                @pl.when(j < NSLAB // 2 - 1)
                def _():
                    con_copy(c2).wait()

            one_band(vg, c1, c2, odd, even)

            @pl.when(j < NSLAB // 2 - 1)
            def _():
                message(vg, c1).start()

            @pl.when(j == NSLAB // 2 - 1)
            def _():
                pltpu.make_async_copy(msg.at[vg, c1], out_ref.at[vg, s], local_sem.at[vg]).start()

            return 0

        lax.fori_loop(0, NSLAB // 2, two_bands, 0)

    def finish(i, _):
        other = lax.rem(s + i + 1, NSLAB)
        for vg in range(2):
            arrival(vg, other).wait_recv()
            message(vg, other).wait_send()
        return 0

    lax.fori_loop(0, NSLAB - 1, finish, 0)
    for vg in range(2):
        pltpu.make_async_copy(msg.at[vg, s], out_ref.at[vg, s], local_sem.at[vg]).wait()
    for copy in (to_partner, to_ahead, to_behind, p_ahead, p_behind, l_ahead, r_behind):
        copy.wait_send()


def planes_call(valence, conduction):
    anywhere = pl.BlockSpec(memory_space=pl.ANY)
    vmem = pl.BlockSpec(memory_space=pltpu.VMEM)
    return pl.pallas_call(
        planes_kernel,
        name="planes",
        out_shape=jax.ShapeDtypeStruct((2, NSLAB, NR, 2 * NX, 128), BF),
        in_specs=[anywhere, anywhere, anywhere, vmem, vmem],
        out_specs=anywhere,
        scratch_shapes=[
            pltpu.VMEM((8, NX, NF, 2 * NF), BF),
            pltpu.VMEM((NSLAB, NX, NF, 2 * NF), BF),
            pltpu.VMEM((2, NSLAB, NR, 2 * NX, 128), BF),
            pltpu.VMEM((8 * NF, 2 * NF), BF),
            pltpu.VMEM((NX * NF, 8 * NF), BF),
            pltpu.VMEM((NX * NF, 8 * NF), BF),
            pltpu.VMEM((NX * NF, 2 * NF), BF),
            pltpu.VMEM((2, NX * NR, 128), F32),
            pltpu.SemaphoreType.DMA((NSLAB,)),
            pltpu.SemaphoreType.DMA,
            pltpu.SemaphoreType.DMA,
            pltpu.SemaphoreType.DMA((7,)),
            pltpu.SemaphoreType.DMA((8,)),
            pltpu.SemaphoreType.DMA((2, NSLAB)),
            pltpu.SemaphoreType.DMA((2, NSLAB)),
            pltpu.SemaphoreType.DMA((2,)),
        ],
        compiler_params=pltpu.CompilerParams(
            collective_id=0, has_side_effects=True, vmem_limit_bytes=56 * 1024 * 1024
        ),
    )(
        valence,
        conduction,
        jnp.asarray(depth_weights()),
        jnp.asarray(height_weights()),
        jnp.asarray(wide_mask()),
    )


def panels_kernel(
    idx_ref, in_ref, tab_ref, order_ref, fac_ref, rp_ref, cab_ref,
    xb, wide, box, blk, rows, cols, landed, cp,
    rsa, rra, csa, cra, rs, rr, cs, cr, sib_s, sib_r, lsem,
):
    g, gat = place_in_groups()
    s, sat = place_in_slabs()
    gx, gz = g // 2, lax.rem(g, 2)
    sz, yc = s // 8, lax.rem(s, 8)
    scaling = 0.5 / float(NF) ** 1.5

    barrier = pltpu.get_barrier_semaphore()
    for i in range(2 * NSLAB):
        if i:
            to = {"grp": gat(0, i // NSLAB), "slab": lax.rem(s + i, NSLAB)}
            pl.semaphore_signal(barrier, inc=1, device_id=to, device_id_type=MESH)
    for i in range(4, 16):
        to = {"grp": gat(i // 4, i // 2 % 2), "slab": sat(0, i % 2, 0)}
        pl.semaphore_signal(barrier, inc=1, device_id=to, device_id_type=MESH)

    def four_rows(j, _):
        for k in range(4):
            r = j * 4 + k
            a = [in_ref[vg, :, pl.ds(r, 1)].reshape(2 * NF, 128) for vg in range(2)]
            o = jnp.dot(tab_ref[...], jnp.concatenate(a, 1), preferred_element_type=F32)
            o = ((o[0:64] + o[64:128]) * scaling).astype(BF)
            put = pl.ds(pl.multiple_of(r * KB, KB), KB)
            xb[put, 0:256] = o[0:32]
            xb[put, 256:512] = o[32:64]
        return 0

    lax.fori_loop(0, NR // 4, four_rows, 0)
    wide[...] = jnp.dot(xb[...], order_ref[...], preferred_element_type=F32)

    def spread(j, _):
        base = pl.multiple_of(j * 96, 32)
        for kz in range(KB):
            part = wide[pl.ds(base, 96), (kz // 8) * 128 : (kz // 8 + 1) * 128]
            if kz % 8:
                part = pltpu.roll(part, 128 - 16 * (kz % 8), 1)
            box[pl.ds(pl.multiple_of(kz * NBOX + base, 8), 96), :] = part
        return 0

    lax.fori_loop(0, NBOX // 96, spread, 0)
    blk[1496:1536, :] = jnp.zeros((40, 128), F32)
    pl.semaphore_wait(barrier, 43)

    lane = lax.broadcasted_iota(jnp.int32, (16, 128), 1)
    row = lax.broadcasted_iota(jnp.int32, (16, 128), 0)
    unit = jnp.where(lane == row, 1.0, 0.0).astype(BF)
    contract = (((1,), (1,)), ((), ()))

    def row_copy(b, z):
        to = {"grp": b, "slab": z * 8 + yc}
        return remote(rows.at[b], landed.at[sz, g], rsa.at[b, z], rra.at[sz, g], to)

    def row_in(b, z):
        to = {"grp": b, "slab": z * 8 + yc}
        return remote(rows.at[b], landed.at[z, b], rsa.at[b, z], rra.at[z, b], to)

    def row_keep():
        return pltpu.make_async_copy(rows.at[g], landed.at[sz, g], lsem.at[0])

    def col_copy(t, z):
        to = {"grp": gx * 2 + z, "slab": t}
        return remote(cols.at[t], cp.at[gx, gz, s], csa.at[t, z], cra.at[gz, s], to)

    def col_in(t, z):
        to = {"grp": gx * 2 + z, "slab": t}
        return remote(cols.at[t], cp.at[gx, z, t], csa.at[t, z], cra.at[z, t], to)

    def col_keep():
        return pltpu.make_async_copy(cols.at[s], cp.at[gx, gz, s], lsem.at[1])

    def one_block(i, _):
        b = lax.rem(g + yc // 2 + sz * 4 + i, NGRP)

        def pick(j, _):
            base = j * 60
            for k in range(60):
                blk[pl.ds(base + k, 1), :] = box[pl.ds(idx_ref[b * RB + base + k], 1), :]
            return 0

        lax.fori_loop(0, RB // 60, pick, 0)
        o = lax.dot_general(unit, blk[0:RP, :].astype(BF), contract, preferred_element_type=F32)
        rows[b] = (o * fac_ref[:, 0:1]).astype(BF)
        for half in range(2):
            part = blk[half * CB : half * CB + CP, :].astype(BF)
            cols[2 * b + half] = lax.dot_general(unit, part, contract, preferred_element_type=F32).astype(BF)
        for z in range(2):
            mine = jnp.logical_and(b == g, z == sz)

            @pl.when(mine)
            def _():
                row_keep().start()

            @pl.when(jnp.logical_not(mine))
            def _():
                row_copy(b, z).start()

            for half in range(2):
                own = jnp.logical_and(2 * b + half == s, z == gz)

                @pl.when(own)
                def _():
                    col_keep().start()

                @pl.when(jnp.logical_not(own))
                def _():
                    col_copy(2 * b + half, z).start()

        return 0

    lax.fori_loop(0, NGRP, one_block, 0)

    def over_rows(act):
        def step(i, _):
            b, z = i // 2, lax.rem(i, 2)

            @pl.when(jnp.logical_not(jnp.logical_and(b == g, z == sz)))
            def _():
                act(b, z)

            return 0

        lax.fori_loop(0, 2 * NGRP, step, 0)

    def over_cols(act):
        def step(i, _):
            t, z = i // 2, lax.rem(i, 2)

            @pl.when(jnp.logical_not(jnp.logical_and(t == s, z == gz)))
            def _():
                act(t, z)

            return 0

        lax.fori_loop(0, 2 * NSLAB, step, 0)

    def row_part(dy, dc, half):
        return rp_ref.at[sat(dy, 0, dc) % 8, pl.ds(half * 768, 768)]

    def row_hop(k, dy, half, to, land):
        part = row_part(dy, 0, half)
        return remote(part, part, rs.at[k], rr.at[land], {"slab": sat(to, 0, 0)})

    def row_wait(land, dy, half):
        part = row_part(dy, 0, half)
        remote(part, part, rs.at[0], rr.at[land], {"slab": sat(1, 0, 0)}).wait_recv()

    def side(k, dy, half, dc=0):
        part = row_part(dy, dc, half)
        return remote(part, part, sib_s.at[k], sib_r.at[k], {"slab": sat(0, 0, 1)})

    def col_part(dx, half):
        return cp.at[gat(dx, 0) // 2, half]

    def col_hop(k, dx, half, to, land):
        part = col_part(dx, half)
        return remote(part, part, cs.at[k], cr.at[land], {"grp": gat(to, 0)})

    def col_wait(land, dx, half):
        part = col_part(dx, half)
        remote(part, part, cs.at[0], cr.at[land], {"grp": gat(1, 0)}).wait_recv()

    hops = [(0, 0, 1, 0), (0, 1, -1, 3), (0, 1, 1, 1), (0, 0, -1, 2), (-1, 0, 1, 4), (1, 1, -1, 5)]
    arrivals = [(0, -1, 0), (3, 1, 1), (1, -1, 1), (2, 1, 0), (4, 2, 0), (5, 2, 1)]
    row_hops = [row_hop(k, *hop) for k, hop in enumerate(hops)]
    col_hops = [col_hop(k, *hop) for k, hop in enumerate(hops)]
    sides = [side(0, 0, 0), side(1, 0, 1)] + [side(2 + k, dy, half) for k, (_, dy, half) in enumerate(arrivals)]

    def arrange(dx, half):
        x = gat(dx, 0) // 2

        def step(t, _):
            part = cp[x, half, pl.ds(t, 1)].reshape(16, CP)
            put = pl.multiple_of(lax.rem(t, 8) * 256 + (t // 8) * 128 + x * 32 + half * 16, 16)
            cab_ref[pl.ds(put, 16), 0:CP] = part
            value = part.astype(F32)
            cab_ref[pl.ds(put, 16), CP : 2 * CP] = jnp.concatenate([-value[8:16], value[0:8]], 0).astype(BF)
            return 0

        lax.fori_loop(0, NSLAB, step, 0)

    row_keep().wait()
    over_rows(lambda b, z: row_in(b, z).wait_recv())
    for j in range(RP // 128):
        part = landed[:, :, :, j * 128 : (j + 1) * 128].reshape(256, 128).astype(F32)
        rp_ref[yc, j * 128 : (j + 1) * 128, :] = part.T.astype(BF)
        if j == 5:
            row_hops[0].start()
            sides[0].start()
    row_hops[1].start()
    row_hops[2].start()
    row_hops[3].start()
    sides[1].start()
    col_keep().wait()
    over_cols(lambda t, z: col_in(t, z).wait_recv())
    for k in range(4):
        col_hops[k].start()
    arrange(0, 0)
    arrange(0, 1)
    for k, (land, d, half) in enumerate(arrivals):
        row_wait(land, d, half)
        if k < 2:
            row_hops[4 + k].start()
        sides[2 + k].start()
        col_wait(land, d, half)
        if k < 2:
            col_hops[4 + k].start()
        arrange(d, half)
    for k, (dy, half) in enumerate([(0, 0), (0, 1)] + [(dy, half) for _, dy, half in arrivals]):
        side(k, dy, half, 1).wait_recv()
    over_rows(lambda b, z: row_copy(b, z).wait_send())
    over_cols(lambda t, z: col_copy(t, z).wait_send())
    for copy in row_hops + col_hops + sides:
        copy.wait_send()


def panels_call(index, planes, factor):
    vmem = pl.BlockSpec(memory_space=pltpu.VMEM)
    dma = pltpu.SemaphoreType.DMA
    return pl.pallas_call(
        panels_kernel,
        name="panels",
        out_shape=(
            jax.ShapeDtypeStruct((8, RP, 256), BF),
            jax.ShapeDtypeStruct((2048, 2 * CP), BF),
        ),
        in_specs=[pl.BlockSpec(memory_space=pltpu.SMEM), vmem, vmem, vmem, vmem],
        out_specs=(vmem, vmem),
        scratch_shapes=[
            pltpu.VMEM((NBOX, 512), BF),
            pltpu.VMEM((NBOX, 512), F32),
            pltpu.VMEM((KB * NBOX, 128), F32),
            pltpu.VMEM((RP, 128), F32),
            pltpu.VMEM((NGRP, 16, RP), BF),
            pltpu.VMEM((NSLAB, 16, CP), BF),
            pltpu.VMEM((2, NGRP, 16, RP), BF),
            pltpu.VMEM((4, 2, NSLAB, 16, CP), BF),
            dma((NGRP, 2)),
            dma((2, NGRP)),
            dma((NSLAB, 2)),
            dma((2, NSLAB)),
            dma((6,)),
            dma((6,)),
            dma((6,)),
            dma((6,)),
            dma((8,)),
            dma((8,)),
            dma((2,)),
        ],
        compiler_params=pltpu.CompilerParams(
            collective_id=1, has_side_effects=True, vmem_limit_bytes=44 * 1024 * 1024
        ),
    )(index, planes, jnp.asarray(box_weights()), jnp.asarray(lane_order()), factor)


def tile_kernel(rp_ref, cab_ref, out_ref):
    rows = pl.ds(pl.multiple_of(pl.program_id(0) * 256, 256), 256)
    left = jnp.concatenate([rp_ref[k, rows, :] for k in range(8)], 1)
    o = jnp.dot(left, cab_ref[...], preferred_element_type=F32)
    out_ref[:, 0, :] = o[:, 0:CB]
    out_ref[:, 1, :] = o[:, CP : CP + CB]


def tile_call(row_panel, column_panel):
    rows = 256
    tiles = pl.pallas_call(
        tile_kernel,
        name="tile",
        grid=(RP // rows,),
        out_shape=jax.ShapeDtypeStruct((RB, 2, CB), F32),
        in_specs=[
            pl.BlockSpec((8, RP, 256), lambda i: (0, 0, 0)),
            pl.BlockSpec((2048, 2 * CP), lambda i: (0, 0)),
        ],
        out_specs=pl.BlockSpec((rows, 2, CB), lambda i: (i, 0, 0)),
        compiler_params=pltpu.CompilerParams(vmem_limit_bytes=44 * 1024 * 1024),
    )(row_panel, column_panel)
    return jnp.transpose(tiles, (1, 0, 2))


def table_look_up(index, table):
    hot = index[:, None] == jnp.arange(KB, dtype=jnp.int32)[None, :]
    return jnp.sum(jnp.where(hot, jnp.asarray(table)[None, :], 0), 1)


def on_device(
    valence_waves, conduction_waves, valence_energy, conduction_energy, occupation, gvec_ids
):
    g, gat = place_in_groups()
    s = lax.axis_index("slab")
    row, shifted = row_tables()
    along_x = gvec_ids // (KB * KB)
    along_y = gvec_ids // KB % KB
    along_z = gvec_ids % KB
    place = table_look_up(along_y, row * KB + shifted * 1024 * KB)
    index = (along_z ^ (place // (1024 * KB))) * NBOX + place % (1024 * KB) + along_x

    bands = [(0, 0), (0, 1), (-1, 0), (1, 0), (-1, 1), (1, 1), (2, 0), (2, 1)]
    order = jnp.stack([gat(*spot) for spot in bands])
    hot = (order[:, None] == jnp.arange(NV, dtype=jnp.int32)[None, :]).astype(F32)
    full = occupation.astype(F32)[:, None] / (
        (valence_energy[:, None] - conduction_energy[None, :]) * math.sqrt(NV * NC)
    )
    mine = jnp.sum(jnp.where(jnp.arange(NSLAB)[None, :] == s, full, 0.0), 1)
    factor = jnp.sum(hot * mine[None, :], 1)
    factor = jnp.broadcast_to(jnp.concatenate([factor, factor])[:, None], (16, 128))

    planes = planes_call(valence_waves, conduction_waves)
    row_panel, column_panel = panels_call(index, planes, factor)
    return tile_call(row_panel, column_panel)


def solution(mesh):
    in_specs = (P("grp", "slab", None, None), P("grp", "slab", None, None), P(), P("grp"), P(), P())
    out_specs = P(None, "grp", "slab")
    return jax.shard_map(
        on_device, mesh=mesh, in_specs=in_specs, out_specs=out_specs, check_vma=False
    )
```

```python
import functools
import math

import jax
import jax.numpy as jnp
import ml_dtypes
import numpy as np
from jax import lax
from jax.experimental import pallas as pl
from jax.experimental.pallas import tpu as pltpu
from jax.sharding import PartitionSpec as P

NV = 8
NC = 128
NF = 128
KB = 32
NG = 12000
NGRP = 8
NSLAB = 16
NX = NF // NSLAB
HX = NX // 2
NR = 24
RB = NG // NGRP
CB = NG // NSLAB
RP = 1536
CP = 768
NBOX = NR * KB
MESH = pl.DeviceIdType.MESH
BF = jnp.bfloat16
F32 = jnp.float32

WIDE = [9, -9, 11, -11, 5, -5]
NARROW = [13, -13, 12, -12, 14, -14]
SINGLE = [0, 1, -1, 2, -2, 3, -3, 4, -4, 6, -6, 7, -7, 8, -8, 10, -10]
ROW_FREQ = SINGLE[:16] + [SINGLE[16]] + WIDE + [15] + [15] + NARROW + [15]


def freq(j):
    return j - KB if j >= KB // 2 else j


def row_tables():
    row = np.zeros(KB, np.int32)
    shifted = np.zeros(KB, np.int32)
    for place, f in enumerate(ROW_FREQ[:NR]):
        if f != 15:
            row[f % KB] = place
    for place, f in enumerate(NARROW):
        row[f % KB] = 17 + place
        shifted[f % KB] = KB // 2
    return row, shifted


def phases(positions, freqs):
    angle = np.mod(np.outer(positions, freqs), NF).astype(np.float32) * np.float32(2.0 * math.pi / NF)
    return np.cos(angle).astype(np.float32), np.sin(angle).astype(np.float32)


def depth_weights():
    cos, sin = phases(np.arange(NF), [freq(j) for j in range(KB)])
    w = np.zeros((4, 2, NF, 2, KB, 4), np.float32)
    for vl in range(4):
        w[vl, 0, :, 0, :, vl] = cos
        w[vl, 1, :, 0, :, vl] = sin
        w[vl, 0, :, 1, :, vl] = -sin
        w[vl, 1, :, 1, :, vl] = cos
    return w.reshape(8 * NF, 8 * KB).astype(ml_dtypes.bfloat16)


def height_weights():
    cos, sin = phases(np.arange(NF), ROW_FREQ)
    return np.concatenate([cos.T, sin.T], 0).astype(ml_dtypes.bfloat16)


def wide_mask():
    mask = np.ones((8, KB, 4), np.float32)
    for place, f in enumerate(WIDE):
        half = math.isqrt(196 - f * f)
        for j in range(KB):
            if abs(freq(j)) > half:
                mask[1 + place, j] = 0.0
    return mask.reshape(8, 4 * KB)


def box_weights():
    cos, sin = phases(np.arange(NF), [freq(j) for j in range(KB)])
    cos = cos.T.reshape(KB, NSLAB, 2, HX).transpose(0, 2, 1, 3)
    sin = sin.T.reshape(KB, NSLAB, 2, HX).transpose(0, 2, 1, 3)
    t = np.zeros((2, KB, 2, NSLAB, 2, HX), np.float32)
    t[0, :, :, :, 0] = cos
    t[0, :, :, :, 1] = sin
    t[1, :, :, :, 0] = -sin
    t[1, :, :, :, 1] = cos
    high = t.astype(ml_dtypes.bfloat16)
    low = (t - high.astype(np.float32)).astype(ml_dtypes.bfloat16)
    pair = np.zeros((2, 2, 2, KB, 2, NSLAB, 2, 2, HX), ml_dtypes.bfloat16)
    for r in range(2):
        pair[r, 0, :, :, :, :, r] = high
        pair[r, 1, :, :, :, :, r] = low
    return pair.reshape(8 * KB, 4 * NF)


def lane_order():
    m = np.zeros((2, 2, KB, 4, KB, 2, 2, 4), np.float32)
    for reim in range(2):
        for vg in range(2):
            for kz in range(KB):
                for vl in range(4):
                    m[reim, vg, kz, vl, kz, reim, vg, vl] = 1.0
    return m.reshape(512, 512).astype(ml_dtypes.bfloat16)


def place_in_groups():
    g = lax.axis_index("grp")
    gx, gz = g // 2, lax.rem(g, 2)

    def at(dx, dz):
        return lax.rem(gx + dx + 4, 4) * 2 + (lax.rem(gz + dz, 2))

    return g, at


def place_in_slabs():
    s = lax.axis_index("slab")
    sz, sy, sc = s // 8, lax.rem(s // 2, 4), lax.rem(s, 2)

    def at(dy, dz, dc):
        return lax.rem(sz + dz, 2) * 8 + lax.rem(sy + dy + 4, 4) * 2 + lax.rem(sc + dc, 2)

    return s, at


def enter(groups, slabs):
    barrier = pltpu.get_barrier_semaphore()
    for one in groups:
        pl.semaphore_signal(barrier, inc=1, device_id={"grp": one}, device_id_type=MESH)
    for one in slabs:
        pl.semaphore_signal(barrier, inc=1, device_id={"slab": one}, device_id_type=MESH)
    pl.semaphore_wait(barrier, len(groups) + len(slabs))


def remote(src, dst, send, recv, device):
    return pltpu.make_async_remote_copy(
        src_ref=src, dst_ref=dst, send_sem=send, recv_sem=recv, device_id=device, device_id_type=MESH
    )


def planes_kernel(
    val_ref, con_ref, wz_ref, ty_ref, mask_ref, out_ref, val, con, msg, wz, even, odd, first, scr, con_sem, own_sem, wz_sem, vs, vr, ms, mr, local_sem
):
    g, gat = place_in_groups()
    s, sat = place_in_slabs()
    own = pltpu.make_async_copy(val_ref.at[0], val.at[0], own_sem)
    own.start()
    weights = pltpu.make_async_copy(wz_ref, wz, wz_sem)
    weights.start()

    def con_copy(c):
        return pltpu.make_async_copy(con_ref.at[c], con.at[c], con_sem.at[c])

    def start_con(i, _):
        con_copy(lax.rem(s + i + 1, NSLAB)).start()
        return 0

    lax.fori_loop(0, NSLAB, start_con, 0)
    partner, ahead, behind = gat(0, 1), gat(1, 0), gat(-1, 0)
    enter([partner, ahead, behind], [lax.rem(s + i, NSLAB) for i in range(1, NSLAB)])
    own.wait()

    def hop(k, slot, to, landing):
        return [
            remote(
                val.at[slot, pl.ds(half * HX, HX)],
                val.at[landing, pl.ds(half * HX, HX)],
                vs.at[k, half],
                vr.at[landing, half],
                {"grp": to},
            )
            for half in range(2)
        ]

    to_partner, to_ahead, to_behind = hop(0, 0, partner, 1), hop(1, 0, ahead, 2), hop(2, 0, behind, 3)
    p_ahead, p_behind = hop(3, 1, ahead, 4), hop(4, 1, behind, 5)
    l_ahead, r_behind = hop(5, 2, ahead, 6), hop(6, 5, behind, 7)
    for half in range(2):
        to_ahead[half].start()
        to_behind[half].start()
        to_partner[half].start()
    weights.wait()

    def message(vg, half, c):
        return remote(
            msg.at[vg, half, c], out_ref.at[vg, half, s], ms.at[vg, half, c], mr.at[vg, half, s], {"slab": c}
        )

    def arrival(vg, half, src):
        return remote(
            msg.at[vg, half, src],
            out_ref.at[vg, half, src],
            ms.at[vg, half, src],
            mr.at[vg, half, src],
            {"slab": src},
        )

    def kept(vg, half):
        return pltpu.make_async_copy(msg.at[vg, half, s], out_ref.at[vg, half, s], local_sem.at[vg, half])

    def density(vg, half, c, buf):
        for x in range(HX):
            for y0 in range(0, NF, 32):
                rows = pl.ds(y0, 32)
                put = pl.ds(x * NF + y0, 32)
                cr = con[c, half * HX + x, rows, 0:NF].astype(F32)
                ci = con[c, half * HX + x, rows, NF : 2 * NF].astype(F32)
                for vl in range(4):
                    pr = val[vg * 4 + vl, half * HX + x, rows, 0:NF].astype(F32)
                    pi = val[vg * 4 + vl, half * HX + x, rows, NF : 2 * NF].astype(F32)
                    buf[put, vl * 256 : vl * 256 + NF] = (pr * cr + pi * ci).astype(BF)
                    buf[put, vl * 256 + NF : vl * 256 + 256] = (pr * ci - pi * cr).astype(BF)

    def along_y(x):
        o = jnp.dot(ty_ref[...], first[x * NF : x * NF + NF, :], preferred_element_type=F32)
        keep = mask_ref[...] > 0.5
        for reim in range(2):
            if reim == 0:
                full = o[0:32, 0:128] + o[32:64, 128:256]
            else:
                full = o[0:32, 128:256] - o[32:64, 0:128]
            merged = jnp.where(keep, full[16:24], pltpu.roll(full[24:32], 64, 1))
            base = (reim * HX + x) * NR
            scr[base : base + 16, :] = full[0:16]
            scr[base + 16 : base + 24, :] = merged

    def one_band(vg, half, c, after, buf, other):
        first[...] = jnp.dot(buf[...], wz[...], preferred_element_type=F32).astype(BF)
        density(vg, half, after, other)
        for x in range(HX):
            along_y(x)
        for r in range(0, NR, 2):
            both = jnp.concatenate(
                [scr[pl.ds(r, 2 * HX, stride=NR), :], scr[pl.ds(r + 1, 2 * HX, stride=NR), :]], 0
            )
            msg[vg, half, c, r // 2] = both.astype(BF)

    for phase in range(4):
        vg, half = phase // 2, phase % 2
        if phase == 0:
            for copies in (to_partner, to_ahead, to_behind):
                copies[0].wait_recv()
            p_behind[0].start()
            p_ahead[0].start()
            l_ahead[0].start()
        if phase == 1:
            for copies in (to_partner, to_ahead, to_behind):
                copies[1].wait_recv()
            p_ahead[1].start()
            p_behind[0].wait_recv()
            r_behind[0].start()
            p_behind[1].start()
            l_ahead[1].start()
        if phase >= 2:
            for copies in (p_ahead, l_ahead, r_behind):
                copies[half].wait_recv()
        start = lax.rem(s + 1, NSLAB)
        if phase == 0:
            con_copy(start).wait()
        density(vg, half, start, even)

        def two_bands(j, _):
            c0 = lax.rem(s + 2 * j + 1, NSLAB)
            c1 = lax.rem(s + 2 * j + 2, NSLAB)
            c2 = lax.rem(s + 2 * j + 3, NSLAB)
            if phase == 0:
                con_copy(c1).wait()
            one_band(vg, half, c0, c1, even, odd)
            message(vg, half, c0).start()
            if phase == 0:

                @pl.when(j < NSLAB // 2 - 1)
                def _():
                    con_copy(c2).wait()

            if phase == 2:

                @pl.when(j == 2)
                def _():
                    p_behind[1].wait_recv()
                    r_behind[1].start()

            one_band(vg, half, c1, c2, odd, even)

            @pl.when(j < NSLAB // 2 - 1)
            def _():
                message(vg, half, c1).start()

            @pl.when(j == NSLAB // 2 - 1)
            def _():
                kept(vg, half).start()

            return 0

        lax.fori_loop(0, NSLAB // 2, two_bands, 0)

    def finish(i, _):
        other = lax.rem(s + i + 1, NSLAB)
        for vg in range(2):
            for half in range(2):
                arrival(vg, half, other).wait_recv()
                message(vg, half, other).wait_send()
        return 0

    lax.fori_loop(0, NSLAB - 1, finish, 0)
    for vg in range(2):
        for half in range(2):
            kept(vg, half).wait()
    for copies in (to_partner, to_ahead, to_behind, p_ahead, p_behind, l_ahead, r_behind):
        for half in range(2):
            copies[half].wait_send()


def planes_call(valence, conduction):
    anywhere = pl.BlockSpec(memory_space=pl.ANY)
    vmem = pl.BlockSpec(memory_space=pltpu.VMEM)
    return pl.pallas_call(
        planes_kernel,
        name="planes",
        out_shape=jax.ShapeDtypeStruct((2, 2, NSLAB, NR // 2, 16, 128), BF),
        in_specs=[anywhere, anywhere, anywhere, vmem, vmem],
        out_specs=vmem,
        scratch_shapes=[
            pltpu.VMEM((8, NX, NF, 2 * NF), BF),
            pltpu.VMEM((NSLAB, NX, NF, 2 * NF), BF),
            pltpu.VMEM((2, 2, NSLAB, NR // 2, 16, 128), BF),
            pltpu.VMEM((8 * NF, 2 * NF), BF),
            pltpu.VMEM((HX * NF, 8 * NF), BF),
            pltpu.VMEM((HX * NF, 8 * NF), BF),
            pltpu.VMEM((HX * NF, 2 * NF), BF),
            pltpu.VMEM((2 * HX * NR, 128), F32),
            pltpu.SemaphoreType.DMA((NSLAB,)),
            pltpu.SemaphoreType.DMA,
            pltpu.SemaphoreType.DMA,
            pltpu.SemaphoreType.DMA((7, 2)),
            pltpu.SemaphoreType.DMA((8, 2)),
            pltpu.SemaphoreType.DMA((2, 2, NSLAB)),
            pltpu.SemaphoreType.DMA((2, 2, NSLAB)),
            pltpu.SemaphoreType.DMA((2, 2)),
        ],
        compiler_params=pltpu.CompilerParams(
            collective_id=0, has_side_effects=True, vmem_limit_bytes=56 * 1024 * 1024
        ),
    )(
        valence,
        conduction,
        jnp.asarray(depth_weights()),
        jnp.asarray(height_weights()),
        jnp.asarray(wide_mask()),
    )


def panels_kernel(
    idx_ref, in_ref, tab_ref, order_ref, fac_ref, rp_ref, cab_ref,
    xb, wide, box, blk, rows, cols, landed, cp,
    rsa, rra, csa, cra, rs, rr, cs, cr, sib_s, sib_r, lsem,
):
    g, gat = place_in_groups()
    s, sat = place_in_slabs()
    gx, gz = g // 2, lax.rem(g, 2)
    sz, yc = s // 8, lax.rem(s, 8)
    scaling = 0.5 / float(NF) ** 1.5

    barrier = pltpu.get_barrier_semaphore()
    for i in range(2 * NSLAB):
        if i:
            to = {"grp": gat(0, i // NSLAB), "slab": lax.rem(s + i, NSLAB)}
            pl.semaphore_signal(barrier, inc=1, device_id=to, device_id_type=MESH)
    for i in range(4, 16):
        to = {"grp": gat(i // 4, i // 2 % 2), "slab": sat(0, i % 2, 0)}
        pl.semaphore_signal(barrier, inc=1, device_id=to, device_id_type=MESH)

    def four_rows(j, _):
        for k in range(2):
            p = j * 2 + k
            a = [in_ref[vg, :, :, pl.ds(p, 1)].reshape(4 * NF, 128) for vg in range(2)]
            both = jnp.dot(tab_ref[...], jnp.concatenate(a, 1), preferred_element_type=F32)
            for r in range(2):
                o = both[r * 128 : r * 128 + 128]
                o = ((o[0:64] + o[64:128]) * scaling).astype(BF)
                put = pl.ds(pl.multiple_of((p * 2 + r) * KB, KB), KB)
                xb[put, 0:256] = o[0:32]
                xb[put, 256:512] = o[32:64]
        return 0

    lax.fori_loop(0, NR // 4, four_rows, 0)
    wide[...] = jnp.dot(xb[...], order_ref[...], preferred_element_type=F32)

    def spread(j, _):
        base = pl.multiple_of(j * 96, 32)
        for kz in range(KB):
            part = wide[pl.ds(base, 96), (kz // 8) * 128 : (kz // 8 + 1) * 128]
            if kz % 8:
                part = pltpu.roll(part, 128 - 16 * (kz % 8), 1)
            box[pl.ds(pl.multiple_of(kz * NBOX + base, 8), 96), :] = part
        return 0

    lax.fori_loop(0, NBOX // 96, spread, 0)
    blk[1496:1536, :] = jnp.zeros((40, 128), F32)
    pl.semaphore_wait(barrier, 43)

    lane = lax.broadcasted_iota(jnp.int32, (16, 128), 1)
    row = lax.broadcasted_iota(jnp.int32, (16, 128), 0)
    unit = jnp.where(lane == row, 1.0, 0.0).astype(BF)
    contract = (((1,), (1,)), ((), ()))

    def row_copy(b, z):
        to = {"grp": b, "slab": z * 8 + yc}
        return remote(rows.at[b], landed.at[sz, g], rsa.at[b, z], rra.at[sz, g], to)

    def row_in(b, z):
        to = {"grp": b, "slab": z * 8 + yc}
        return remote(rows.at[b], landed.at[z, b], rsa.at[b, z], rra.at[z, b], to)

    def row_keep():
        return pltpu.make_async_copy(rows.at[g], landed.at[sz, g], lsem.at[0])

    def col_copy(t, z):
        to = {"grp": gx * 2 + z, "slab": t}
        return remote(cols.at[t], cp.at[gx, gz, s], csa.at[t, z], cra.at[gz, s], to)

    def col_in(t, z):
        to = {"grp": gx * 2 + z, "slab": t}
        return remote(cols.at[t], cp.at[gx, z, t], csa.at[t, z], cra.at[z, t], to)

    def col_keep():
        return pltpu.make_async_copy(cols.at[s], cp.at[gx, gz, s], lsem.at[1])

    def one_block(i, _):
        b = lax.rem(g + yc // 2 + sz * 4 + i, NGRP)

        def pick(j, _):
            base = j * 60
            for k in range(60):
                blk[pl.ds(base + k, 1), :] = box[pl.ds(idx_ref[b * RB + base + k], 1), :]
            return 0

        lax.fori_loop(0, RB // 60, pick, 0)
        o = lax.dot_general(unit, blk[0:RP, :].astype(BF), contract, preferred_element_type=F32)
        rows[b] = (o * fac_ref[:, 0:1]).astype(BF)
        for half in range(2):
            part = blk[half * CB : half * CB + CP, :].astype(BF)
            cols[2 * b + half] = lax.dot_general(unit, part, contract, preferred_element_type=F32).astype(BF)
        for z in range(2):
            mine = jnp.logical_and(b == g, z == sz)

            @pl.when(mine)
            def _():
                row_keep().start()

            @pl.when(jnp.logical_not(mine))
            def _():
                row_copy(b, z).start()

            for half in range(2):
                own = jnp.logical_and(2 * b + half == s, z == gz)

                @pl.when(own)
                def _():
                    col_keep().start()

                @pl.when(jnp.logical_not(own))
                def _():
                    col_copy(2 * b + half, z).start()

        return 0

    lax.fori_loop(0, NGRP, one_block, 0)

    def over_rows(act):
        def step(i, _):
            b, z = i // 2, lax.rem(i, 2)

            @pl.when(jnp.logical_not(jnp.logical_and(b == g, z == sz)))
            def _():
                act(b, z)

            return 0

        lax.fori_loop(0, 2 * NGRP, step, 0)

    def over_cols(act):
        def step(i, _):
            t, z = i // 2, lax.rem(i, 2)

            @pl.when(jnp.logical_not(jnp.logical_and(t == s, z == gz)))
            def _():
                act(t, z)

            return 0

        lax.fori_loop(0, 2 * NSLAB, step, 0)

    def row_part(dy, dc, half):
        return rp_ref.at[sat(dy, 0, dc) % 8, pl.ds(half * 768, 768)]

    def row_hop(k, dy, half, to, land):
        part = row_part(dy, 0, half)
        return remote(part, part, rs.at[k], rr.at[land], {"slab": sat(to, 0, 0)})

    def row_wait(land, dy, half):
        part = row_part(dy, 0, half)
        remote(part, part, rs.at[0], rr.at[land], {"slab": sat(1, 0, 0)}).wait_recv()

    def side(k, dy, half, dc=0):
        part = row_part(dy, dc, half)
        return remote(part, part, sib_s.at[k], sib_r.at[k], {"slab": sat(0, 0, 1)})

    def col_part(dx, half):
        return cp.at[gat(dx, 0) // 2, half]

    def col_hop(k, dx, half, to, land):
        part = col_part(dx, half)
        return remote(part, part, cs.at[k], cr.at[land], {"grp": gat(to, 0)})

    def col_wait(land, dx, half):
        part = col_part(dx, half)
        remote(part, part, cs.at[0], cr.at[land], {"grp": gat(1, 0)}).wait_recv()

    hops = [(0, 0, 1, 0), (0, 1, -1, 3), (0, 1, 1, 1), (0, 0, -1, 2), (-1, 0, 1, 4), (1, 1, -1, 5)]
    arrivals = [(0, -1, 0), (3, 1, 1), (1, -1, 1), (2, 1, 0), (4, 2, 0), (5, 2, 1)]
    row_hops = [row_hop(k, *hop) for k, hop in enumerate(hops)]
    col_hops = [col_hop(k, *hop) for k, hop in enumerate(hops)]
    sides = [side(0, 0, 0), side(1, 0, 1)] + [side(2 + k, dy, half) for k, (_, dy, half) in enumerate(arrivals)]

    def arrange(dx, half):
        x = gat(dx, 0) // 2

        def step(t, _):
            part = cp[x, half, pl.ds(t, 1)].reshape(16, CP)
            put = pl.multiple_of(lax.rem(t, 8) * 256 + (t // 8) * 128 + x * 32 + half * 16, 16)
            cab_ref[pl.ds(put, 16), 0:CP] = part
            value = part.astype(F32)
            cab_ref[pl.ds(put, 16), CP : 2 * CP] = jnp.concatenate([-value[8:16], value[0:8]], 0).astype(BF)
            return 0

        lax.fori_loop(0, NSLAB, step, 0)

    row_keep().wait()
    over_rows(lambda b, z: row_in(b, z).wait_recv())
    for j in range(RP // 128):
        part = landed[:, :, :, j * 128 : (j + 1) * 128].reshape(256, 128).astype(F32)
        rp_ref[yc, j * 128 : (j + 1) * 128, :] = part.T.astype(BF)
        if j == 5:
            row_hops[0].start()
            sides[0].start()
    row_hops[1].start()
    row_hops[2].start()
    row_hops[3].start()
    sides[1].start()
    col_keep().wait()
    over_cols(lambda t, z: col_in(t, z).wait_recv())
    for k in range(4):
        col_hops[k].start()
    arrange(0, 0)
    arrange(0, 1)
    for k, (land, d, half) in enumerate(arrivals):
        row_wait(land, d, half)
        if k < 2:
            row_hops[4 + k].start()
        sides[2 + k].start()
        col_wait(land, d, half)
        if k < 2:
            col_hops[4 + k].start()
        arrange(d, half)
    for k, (dy, half) in enumerate([(0, 0), (0, 1)] + [(dy, half) for _, dy, half in arrivals]):
        side(k, dy, half, 1).wait_recv()
    over_rows(lambda b, z: row_copy(b, z).wait_send())
    over_cols(lambda t, z: col_copy(t, z).wait_send())
    for copy in row_hops + col_hops + sides:
        copy.wait_send()


def panels_call(index, planes, factor):
    vmem = pl.BlockSpec(memory_space=pltpu.VMEM)
    dma = pltpu.SemaphoreType.DMA
    return pl.pallas_call(
        panels_kernel,
        name="panels",
        out_shape=(
            jax.ShapeDtypeStruct((8, RP, 256), BF),
            jax.ShapeDtypeStruct((2048, 2 * CP), BF),
        ),
        in_specs=[pl.BlockSpec(memory_space=pltpu.SMEM), vmem, vmem, vmem, vmem],
        out_specs=(vmem, vmem),
        scratch_shapes=[
            pltpu.VMEM((NBOX, 512), BF),
            pltpu.VMEM((NBOX, 512), F32),
            pltpu.VMEM((KB * NBOX, 128), F32),
            pltpu.VMEM((RP, 128), F32),
            pltpu.VMEM((NGRP, 16, RP), BF),
            pltpu.VMEM((NSLAB, 16, CP), BF),
            pltpu.VMEM((2, NGRP, 16, RP), BF),
            pltpu.VMEM((4, 2, NSLAB, 16, CP), BF),
            dma((NGRP, 2)),
            dma((2, NGRP)),
            dma((NSLAB, 2)),
            dma((2, NSLAB)),
            dma((6,)),
            dma((6,)),
            dma((6,)),
            dma((6,)),
            dma((8,)),
            dma((8,)),
            dma((2,)),
        ],
        compiler_params=pltpu.CompilerParams(
            collective_id=1, has_side_effects=True, vmem_limit_bytes=28 * 1024 * 1024
        ),
    )(index, planes, jnp.asarray(box_weights()), jnp.asarray(lane_order()), factor)


def tile_kernel(rp_ref, cab_ref, out_ref):
    rows = pl.ds(pl.multiple_of(pl.program_id(0) * 256, 256), 256)
    left = jnp.concatenate([rp_ref[k, rows, :] for k in range(8)], 1)
    o = jnp.dot(left, cab_ref[...], preferred_element_type=F32)
    out_ref[:, 0, :] = o[:, 0:CB]
    out_ref[:, 1, :] = o[:, CP : CP + CB]


def tile_call(row_panel, column_panel):
    rows = 256
    tiles = pl.pallas_call(
        tile_kernel,
        name="tile",
        grid=(RP // rows,),
        out_shape=jax.ShapeDtypeStruct((RB, 2, CB), F32),
        in_specs=[
            pl.BlockSpec((8, RP, 256), lambda i: (0, 0, 0)),
            pl.BlockSpec((2048, 2 * CP), lambda i: (0, 0)),
        ],
        out_specs=pl.BlockSpec((rows, 2, CB), lambda i: (i, 0, 0)),
        compiler_params=pltpu.CompilerParams(vmem_limit_bytes=32 * 1024 * 1024),
    )(row_panel, column_panel)
    return jnp.transpose(tiles, (1, 0, 2))


def table_look_up(index, table):
    hot = index[:, None] == jnp.arange(KB, dtype=jnp.int32)[None, :]
    return jnp.sum(jnp.where(hot, jnp.asarray(table)[None, :], 0), 1)


def on_device(
    valence_waves, conduction_waves, valence_energy, conduction_energy, occupation, gvec_ids
):
    g, gat = place_in_groups()
    s = lax.axis_index("slab")
    row, shifted = row_tables()
    along_x = gvec_ids // (KB * KB)
    along_y = gvec_ids // KB % KB
    along_z = gvec_ids % KB
    place = table_look_up(along_y, row * KB + shifted * 1024 * KB)
    index = (along_z ^ (place // (1024 * KB))) * NBOX + place % (1024 * KB) + along_x

    bands = [(0, 0), (0, 1), (-1, 0), (1, 0), (-1, 1), (1, 1), (2, 0), (2, 1)]
    order = jnp.stack([gat(*spot) for spot in bands])
    hot = (order[:, None] == jnp.arange(NV, dtype=jnp.int32)[None, :]).astype(F32)
    full = occupation.astype(F32)[:, None] / (
        (valence_energy[:, None] - conduction_energy[None, :]) * math.sqrt(NV * NC)
    )
    mine = jnp.sum(jnp.where(jnp.arange(NSLAB)[None, :] == s, full, 0.0), 1)
    factor = jnp.sum(hot * mine[None, :], 1)
    factor = jnp.broadcast_to(jnp.concatenate([factor, factor])[:, None], (16, 128))

    planes = planes_call(valence_waves, conduction_waves)
    row_panel, column_panel = panels_call(index, planes, factor)
    return tile_call(row_panel, column_panel)


def solution(mesh):
    in_specs = (P("grp", "slab", None, None), P("grp", "slab", None, None), P(), P("grp"), P(), P())
    out_specs = P(None, "grp", "slab")
    return jax.shard_map(
        on_device, mesh=mesh, in_specs=in_specs, out_specs=out_specs, check_vma=False
    )
```

```python
import functools
import math

import jax
import jax.numpy as jnp
import ml_dtypes
import numpy as np
from jax import lax
from jax.experimental import pallas as pl
from jax.experimental.pallas import tpu as pltpu
from jax.sharding import PartitionSpec as P

NV = 8
NC = 128
NF = 128
KB = 32
NG = 12000
NGRP = 8
NSLAB = 16
NX = NF // NSLAB
HX = NX // 2
NR = 24
RB = NG // NGRP
CB = NG // NSLAB
RP = 1536
CP = 768
NBOX = NR * KB
MESH = pl.DeviceIdType.MESH
BF = jnp.bfloat16
F32 = jnp.float32

WIDE = [9, -9, 11, -11, 5, -5]
NARROW = [13, -13, 12, -12, 14, -14]
SINGLE = [0, 1, -1, 2, -2, 3, -3, 4, -4, 6, -6, 7, -7, 8, -8, 10, -10]
ROW_FREQ = SINGLE[:16] + [SINGLE[16]] + WIDE + [15] + [15] + NARROW + [15]


def freq(j):
    return j - KB if j >= KB // 2 else j


def row_tables():
    row = np.zeros(KB, np.int32)
    shifted = np.zeros(KB, np.int32)
    for place, f in enumerate(ROW_FREQ[:NR]):
        if f != 15:
            row[f % KB] = place
    for place, f in enumerate(NARROW):
        row[f % KB] = 17 + place
        shifted[f % KB] = KB // 2
    return row, shifted


def phases(positions, freqs):
    angle = np.mod(np.outer(positions, freqs), NF).astype(np.float32) * np.float32(2.0 * math.pi / NF)
    return np.cos(angle).astype(np.float32), np.sin(angle).astype(np.float32)


def depth_weights():
    cos, sin = phases(np.arange(NF), [freq(j) for j in range(KB)])
    w = np.zeros((4, 2, NF, 2, KB, 4), np.float32)
    for vl in range(4):
        w[vl, 0, :, 0, :, vl] = cos
        w[vl, 1, :, 0, :, vl] = sin
        w[vl, 0, :, 1, :, vl] = -sin
        w[vl, 1, :, 1, :, vl] = cos
    return w.reshape(8 * NF, 8 * KB).astype(ml_dtypes.bfloat16)


def height_weights():
    cos, sin = phases(np.arange(NF), ROW_FREQ)
    return np.concatenate([cos.T, sin.T], 0).astype(ml_dtypes.bfloat16)


def wide_mask():
    mask = np.ones((8, KB, 4), np.float32)
    for place, f in enumerate(WIDE):
        half = math.isqrt(196 - f * f)
        for j in range(KB):
            if abs(freq(j)) > half:
                mask[1 + place, j] = 0.0
    return mask.reshape(8, 4 * KB)


def box_weights():
    cos, sin = phases(np.arange(NF), [freq(j) for j in range(KB)])
    cos = cos.T.reshape(KB, NSLAB, 2, HX).transpose(0, 2, 1, 3)
    sin = sin.T.reshape(KB, NSLAB, 2, HX).transpose(0, 2, 1, 3)
    t = np.zeros((2, KB, 2, NSLAB, 2, HX), np.float32)
    t[0, :, :, :, 0] = cos
    t[0, :, :, :, 1] = sin
    t[1, :, :, :, 0] = -sin
    t[1, :, :, :, 1] = cos
    high = t.astype(ml_dtypes.bfloat16)
    low = (t - high.astype(np.float32)).astype(ml_dtypes.bfloat16)
    pair = np.zeros((2, 2, 2, KB, 2, NSLAB, 2, 2, HX), ml_dtypes.bfloat16)
    for r in range(2):
        pair[r, 0, :, :, :, :, r] = high
        pair[r, 1, :, :, :, :, r] = low
    return pair.reshape(8 * KB, 4 * NF)


def lane_order():
    m = np.zeros((2, 2, KB, 4, KB, 2, 2, 4), np.float32)
    for reim in range(2):
        for vg in range(2):
            for kz in range(KB):
                for vl in range(4):
                    m[reim, vg, kz, vl, kz, reim, vg, vl] = 1.0
    return m.reshape(512, 512).astype(ml_dtypes.bfloat16)


def place_in_groups():
    g = lax.axis_index("grp")
    gx, gz = g // 2, lax.rem(g, 2)

    def at(dx, dz):
        return lax.rem(gx + dx + 4, 4) * 2 + (lax.rem(gz + dz, 2))

    return g, at


def place_in_slabs():
    s = lax.axis_index("slab")
    sz, sy, sc = s // 8, lax.rem(s // 2, 4), lax.rem(s, 2)

    def at(dy, dz, dc):
        return lax.rem(sz + dz, 2) * 8 + lax.rem(sy + dy + 4, 4) * 2 + lax.rem(sc + dc, 2)

    return s, at


def enter(groups, slabs):
    barrier = pltpu.get_barrier_semaphore()
    for one in groups:
        pl.semaphore_signal(barrier, inc=1, device_id={"grp": one}, device_id_type=MESH)
    for one in slabs:
        pl.semaphore_signal(barrier, inc=1, device_id={"slab": one}, device_id_type=MESH)
    pl.semaphore_wait(barrier, len(groups) + len(slabs))


def remote(src, dst, send, recv, device):
    return pltpu.make_async_remote_copy(
        src_ref=src, dst_ref=dst, send_sem=send, recv_sem=recv, device_id=device, device_id_type=MESH
    )


def planes_kernel(
    val_ref, con_ref, wz_ref, ty_ref, mask_ref, out_ref, val, con, msg, wz, even, odd, first_even, first_odd, scr, con_sem, own_sem, wz_sem, vs, vr, ms, mr, local_sem
):
    g, gat = place_in_groups()
    s, sat = place_in_slabs()
    own = pltpu.make_async_copy(val_ref.at[0], val.at[0], own_sem)
    own.start()
    weights = pltpu.make_async_copy(wz_ref, wz, wz_sem)
    weights.start()

    def band(i):
        k = lax.rem(i + 16, 16) // 2
        step = lax.rem(k + 1, 4)
        step = step + lax.rem(s, 2) * (4 - 2 * step)
        return sat(lax.rem(step, 4), lax.rem(i + 17, 2), 1 - k // 4)

    def con_copy(c):
        return pltpu.make_async_copy(con_ref.at[c], con.at[c], con_sem.at[c])

    def start_con(i, _):
        con_copy(band(i)).start()
        return 0

    lax.fori_loop(0, NSLAB, start_con, 0)
    partner, ahead, behind = gat(0, 1), gat(1, 0), gat(-1, 0)
    enter([partner, ahead, behind], [lax.rem(s + i, NSLAB) for i in range(1, NSLAB)])
    own.wait()

    def hop(k, slot, to, landing):
        return [
            remote(
                val.at[slot, pl.ds(half * HX, HX)],
                val.at[landing, pl.ds(half * HX, HX)],
                vs.at[k, half],
                vr.at[landing, half],
                {"grp": to},
            )
            for half in range(2)
        ]

    to_partner, to_ahead, to_behind = hop(0, 0, partner, 1), hop(1, 0, ahead, 2), hop(2, 0, behind, 3)
    p_ahead, p_behind = hop(3, 1, ahead, 4), hop(4, 1, behind, 5)
    l_ahead, r_behind = hop(5, 2, ahead, 6), hop(6, 5, behind, 7)
    for half in range(2):
        to_ahead[half].start()
        to_behind[half].start()
        to_partner[half].start()
    weights.wait()

    def message(vg, half, c):
        return remote(
            msg.at[vg, half, c], out_ref.at[vg, half, s], ms.at[vg, half, c], mr.at[vg, half, s], {"slab": c}
        )

    def arrival(vg, half, src):
        return remote(
            msg.at[vg, half, src],
            out_ref.at[vg, half, src],
            ms.at[vg, half, src],
            mr.at[vg, half, src],
            {"slab": src},
        )

    def kept(vg, half):
        return pltpu.make_async_copy(msg.at[vg, half, s], out_ref.at[vg, half, s], local_sem.at[vg, half])

    def density(vg, half, c, buf, x):
        for y0 in range(0, NF, 32):
            rows = pl.ds(y0, 32)
            put = pl.ds(x * NF + y0, 32)
            cr = con[c, half * HX + x, rows, 0:NF]
            ci = con[c, half * HX + x, rows, NF : 2 * NF]
            for vl in range(4):
                pr = val[vg * 4 + vl, half * HX + x, rows, 0:NF]
                pi = val[vg * 4 + vl, half * HX + x, rows, NF : 2 * NF]
                buf[put, vl * 256 : vl * 256 + NF] = pr * cr + pi * ci
                buf[put, vl * 256 + NF : vl * 256 + 256] = pr * ci - pi * cr

    def along_z(part, buf, first):
        rows = pl.ds(part * HX * NF // 2, HX * NF // 2)
        first[rows, :] = jnp.dot(buf[rows, :], wz[...], preferred_element_type=F32).astype(BF)

    def along_y(x, first):
        o = jnp.dot(ty_ref[...], first[x * NF : x * NF + NF, :], preferred_element_type=F32)
        keep = mask_ref[...] > 0.5
        for reim in range(2):
            if reim == 0:
                full = o[0:32, 0:128] + o[32:64, 128:256]
            else:
                full = o[0:32, 128:256] - o[32:64, 0:128]
            merged = jnp.where(keep, full[16:24], pltpu.roll(full[24:32], 64, 1))
            base = (reim * HX + x) * NR
            scr[base : base + 16, :] = full[0:16]
            scr[base + 16 : base + 24, :] = merged

    def pack(vg, half, c):
        for r in range(0, NR, 2):
            both = jnp.concatenate(
                [scr[pl.ds(r, 2 * HX, stride=NR), :], scr[pl.ds(r + 1, 2 * HX, stride=NR), :]], 0
            )
            msg[vg, half, c, r // 2] = both.astype(BF)

    def one_band(vg, half, before, after, buf, other, first, last):
        along_z(0, buf, first)
        density(vg, half, after, other, 0)
        density(vg, half, after, other, 1)
        along_y(0, last)
        along_y(1, last)
        along_z(1, buf, first)
        density(vg, half, after, other, 2)
        density(vg, half, after, other, 3)
        along_y(2, last)
        along_y(3, last)
        pack(vg, half, before)

    for phase in range(4):
        vg, half = phase // 2, phase % 2
        if phase == 0:
            for copies in (to_partner, to_ahead, to_behind):
                copies[0].wait_recv()
            p_behind[0].start()
            p_ahead[0].start()
            l_ahead[0].start()
        if phase == 1:
            for copies in (to_partner, to_ahead, to_behind):
                copies[1].wait_recv()
            p_ahead[1].start()
            p_behind[0].wait_recv()
            r_behind[0].start()
            p_behind[1].start()
            l_ahead[1].start()
        if phase >= 2:
            for copies in (p_ahead, l_ahead, r_behind):
                copies[half].wait_recv()
        start = band(0)
        if phase == 0:
            con_copy(start).wait()
        for x in range(HX):
            density(vg, half, start, even, x)

        def two_bands(j, _):
            before, c0, c1, c2 = band(2 * j - 1), band(2 * j), band(2 * j + 1), band(2 * j + 2)
            if phase == 0:
                con_copy(c1).wait()

                @pl.when(j < NSLAB // 2 - 1)
                def _():
                    con_copy(c2).wait()

            if phase == 2:

                @pl.when(j == 2)
                def _():
                    p_behind[1].wait_recv()
                    r_behind[1].start()

            one_band(vg, half, before, c1, even, odd, first_even, first_odd)

            @pl.when(j > 0)
            def _():
                message(vg, half, before).start()

            one_band(vg, half, c0, c2, odd, even, first_odd, first_even)
            message(vg, half, c0).start()
            return 0

        lax.fori_loop(0, NSLAB // 2, two_bands, 0)
        for x in range(HX):
            along_y(x, first_odd)
        pack(vg, half, s)
        kept(vg, half).start()

    def finish(i, _):
        other = lax.rem(s + i + 1, NSLAB)
        for vg in range(2):
            for half in range(2):
                arrival(vg, half, other).wait_recv()
                message(vg, half, other).wait_send()
        return 0

    lax.fori_loop(0, NSLAB - 1, finish, 0)
    for vg in range(2):
        for half in range(2):
            kept(vg, half).wait()
    for copies in (to_partner, to_ahead, to_behind, p_ahead, p_behind, l_ahead, r_behind):
        for half in range(2):
            copies[half].wait_send()


def planes_call(valence, conduction):
    anywhere = pl.BlockSpec(memory_space=pl.ANY)
    vmem = pl.BlockSpec(memory_space=pltpu.VMEM)
    return pl.pallas_call(
        planes_kernel,
        name="planes",
        out_shape=jax.ShapeDtypeStruct((2, 2, NSLAB, NR // 2, 16, 128), BF),
        in_specs=[anywhere, anywhere, anywhere, vmem, vmem],
        out_specs=vmem,
        scratch_shapes=[
            pltpu.VMEM((8, NX, NF, 2 * NF), BF),
            pltpu.VMEM((NSLAB, NX, NF, 2 * NF), BF),
            pltpu.VMEM((2, 2, NSLAB, NR // 2, 16, 128), BF),
            pltpu.VMEM((8 * NF, 2 * NF), BF),
            pltpu.VMEM((HX * NF, 8 * NF), BF),
            pltpu.VMEM((HX * NF, 8 * NF), BF),
            pltpu.VMEM((HX * NF, 2 * NF), BF),
            pltpu.VMEM((HX * NF, 2 * NF), BF),
            pltpu.VMEM((2 * HX * NR, 128), F32),
            pltpu.SemaphoreType.DMA((NSLAB,)),
            pltpu.SemaphoreType.DMA,
            pltpu.SemaphoreType.DMA,
            pltpu.SemaphoreType.DMA((7, 2)),
            pltpu.SemaphoreType.DMA((8, 2)),
            pltpu.SemaphoreType.DMA((2, 2, NSLAB)),
            pltpu.SemaphoreType.DMA((2, 2, NSLAB)),
            pltpu.SemaphoreType.DMA((2, 2)),
        ],
        compiler_params=pltpu.CompilerParams(
            collective_id=0, has_side_effects=True, vmem_limit_bytes=56 * 1024 * 1024
        ),
    )(
        valence,
        conduction,
        jnp.asarray(depth_weights()),
        jnp.asarray(height_weights()),
        jnp.asarray(wide_mask()),
    )


def panels_kernel(
    idx_ref, in_ref, tab_ref, order_ref, fac_ref, rp_ref, cab_ref,
    xb, wide, box, blk, rows, cols, landed, cp,
    rsa, rra, csa, cra, rs, rr, cs, cr, sib_s, sib_r, lsem,
):
    g, gat = place_in_groups()
    s, sat = place_in_slabs()
    gx, gz = g // 2, lax.rem(g, 2)
    sz, yc = s // 8, lax.rem(s, 8)
    scaling = 0.5 / float(NF) ** 1.5

    barrier = pltpu.get_barrier_semaphore()
    for i in range(2 * NSLAB):
        if i:
            to = {"grp": gat(0, i // NSLAB), "slab": lax.rem(s + i, NSLAB)}
            pl.semaphore_signal(barrier, inc=1, device_id=to, device_id_type=MESH)
    for i in range(4, 16):
        to = {"grp": gat(i // 4, i // 2 % 2), "slab": sat(0, i % 2, 0)}
        pl.semaphore_signal(barrier, inc=1, device_id=to, device_id_type=MESH)

    def four_rows(j, _):
        for k in range(2):
            p = j * 2 + k
            a = [in_ref[vg, :, :, pl.ds(p, 1)].reshape(4 * NF, 128) for vg in range(2)]
            both = jnp.dot(tab_ref[...], jnp.concatenate(a, 1), preferred_element_type=F32)
            for r in range(2):
                o = both[r * 128 : r * 128 + 128]
                o = ((o[0:64] + o[64:128]) * scaling).astype(BF)
                put = pl.ds(pl.multiple_of((p * 2 + r) * KB, KB), KB)
                xb[put, 0:256] = o[0:32]
                xb[put, 256:512] = o[32:64]
        return 0

    lax.fori_loop(0, NR // 4, four_rows, 0)
    wide[...] = jnp.dot(xb[...], order_ref[...], preferred_element_type=F32)

    def spread(j, _):
        base = pl.multiple_of(j * 96, 32)
        for kz in range(KB):
            part = wide[pl.ds(base, 96), (kz // 8) * 128 : (kz // 8 + 1) * 128]
            if kz % 8:
                part = pltpu.roll(part, 128 - 16 * (kz % 8), 1)
            box[pl.ds(pl.multiple_of(kz * NBOX + base, 8), 96), :] = part
        return 0

    lax.fori_loop(0, NBOX // 96, spread, 0)
    blk[1496:1536, :] = jnp.zeros((40, 128), F32)
    pl.semaphore_wait(barrier, 43)

    lane = lax.broadcasted_iota(jnp.int32, (16, 128), 1)
    row = lax.broadcasted_iota(jnp.int32, (16, 128), 0)
    unit = jnp.where(lane == row, 1.0, 0.0).astype(BF)
    contract = (((1,), (1,)), ((), ()))

    def row_copy(b, z):
        to = {"grp": b, "slab": z * 8 + yc}
        return remote(rows.at[b], landed.at[sz, g], rsa.at[b, z], rra.at[sz, g], to)

    def row_in(b, z):
        to = {"grp": b, "slab": z * 8 + yc}
        return remote(rows.at[b], landed.at[z, b], rsa.at[b, z], rra.at[z, b], to)

    def row_keep():
        return pltpu.make_async_copy(rows.at[g], landed.at[sz, g], lsem.at[0])

    def col_copy(t, z):
        to = {"grp": gx * 2 + z, "slab": t}
        return remote(cols.at[t], cp.at[gx, gz, s], csa.at[t, z], cra.at[gz, s], to)

    def col_in(t, z):
        to = {"grp": gx * 2 + z, "slab": t}
        return remote(cols.at[t], cp.at[gx, z, t], csa.at[t, z], cra.at[z, t], to)

    def col_keep():
        return pltpu.make_async_copy(cols.at[s], cp.at[gx, gz, s], lsem.at[1])

    def one_block(i, _):
        b = lax.rem(g + yc // 2 + sz * 4 + i, NGRP)

        def pick(j, _):
            base = j * 60
            for k in range(60):
                blk[pl.ds(base + k, 1), :] = box[pl.ds(idx_ref[b * RB + base + k], 1), :]
            return 0

        lax.fori_loop(0, RB // 60, pick, 0)
        o = lax.dot_general(unit, blk[0:RP, :].astype(BF), contract, preferred_element_type=F32)
        rows[b] = (o * fac_ref[:, 0:1]).astype(BF)
        for half in range(2):
            part = blk[half * CB : half * CB + CP, :].astype(BF)
            cols[2 * b + half] = lax.dot_general(unit, part, contract, preferred_element_type=F32).astype(BF)
        for z in range(2):
            mine = jnp.logical_and(b == g, z == sz)

            @pl.when(mine)
            def _():
                row_keep().start()

            @pl.when(jnp.logical_not(mine))
            def _():
                row_copy(b, z).start()

            for half in range(2):
                own = jnp.logical_and(2 * b + half == s, z == gz)

                @pl.when(own)
                def _():
                    col_keep().start()

                @pl.when(jnp.logical_not(own))
                def _():
                    col_copy(2 * b + half, z).start()

        return 0

    lax.fori_loop(0, NGRP, one_block, 0)

    def over_rows(act):
        def step(i, _):
            b, z = i // 2, lax.rem(i, 2)

            @pl.when(jnp.logical_not(jnp.logical_and(b == g, z == sz)))
            def _():
                act(b, z)

            return 0

        lax.fori_loop(0, 2 * NGRP, step, 0)

    def over_cols(act):
        def step(i, _):
            t, z = i // 2, lax.rem(i, 2)

            @pl.when(jnp.logical_not(jnp.logical_and(t == s, z == gz)))
            def _():
                act(t, z)

            return 0

        lax.fori_loop(0, 2 * NSLAB, step, 0)

    def row_part(dy, dc, half):
        return rp_ref.at[sat(dy, 0, dc) % 8, pl.ds(half * 768, 768)]

    def row_hop(k, dy, half, to, land):
        part = row_part(dy, 0, half)
        return remote(part, part, rs.at[k], rr.at[land], {"slab": sat(to, 0, 0)})

    def row_wait(land, dy, half):
        part = row_part(dy, 0, half)
        remote(part, part, rs.at[0], rr.at[land], {"slab": sat(1, 0, 0)}).wait_recv()

    def side(k, dy, half, dc=0):
        part = row_part(dy, dc, half)
        return remote(part, part, sib_s.at[k], sib_r.at[k], {"slab": sat(0, 0, 1)})

    def col_part(dx, half):
        return cp.at[gat(dx, 0) // 2, half]

    def col_hop(k, dx, half, to, land):
        part = col_part(dx, half)
        return remote(part, part, cs.at[k], cr.at[land], {"grp": gat(to, 0)})

    def col_wait(land, dx, half):
        part = col_part(dx, half)
        remote(part, part, cs.at[0], cr.at[land], {"grp": gat(1, 0)}).wait_recv()

    hops = [(0, 0, 1, 0), (0, 1, -1, 3), (0, 1, 1, 1), (0, 0, -1, 2), (-1, 0, 1, 4), (1, 1, -1, 5)]
    arrivals = [(0, -1, 0), (3, 1, 1), (1, -1, 1), (2, 1, 0), (4, 2, 0), (5, 2, 1)]
    row_hops = [row_hop(k, *hop) for k, hop in enumerate(hops)]
    col_hops = [col_hop(k, *hop) for k, hop in enumerate(hops)]
    sides = [side(0, 0, 0), side(1, 0, 1)] + [side(2 + k, dy, half) for k, (_, dy, half) in enumerate(arrivals)]

    def arrange(dx, half):
        x = gat(dx, 0) // 2

        def step(t, _):
            part = cp[x, half, pl.ds(t, 1)].reshape(16, CP)
            put = pl.multiple_of(lax.rem(t, 8) * 256 + (t // 8) * 128 + x * 32 + half * 16, 16)
            cab_ref[pl.ds(put, 16), 0:CP] = part
            value = part.astype(F32)
            cab_ref[pl.ds(put, 16), CP : 2 * CP] = jnp.concatenate([-value[8:16], value[0:8]], 0).astype(BF)
            return 0

        lax.fori_loop(0, NSLAB, step, 0)

    row_keep().wait()
    over_rows(lambda b, z: row_in(b, z).wait_recv())
    for j in range(RP // 128):
        part = landed[:, :, :, j * 128 : (j + 1) * 128].reshape(256, 128).astype(F32)
        rp_ref[yc, j * 128 : (j + 1) * 128, :] = part.T.astype(BF)
        if j == 5:
            row_hops[0].start()
            sides[0].start()
    row_hops[1].start()
    row_hops[2].start()
    row_hops[3].start()
    sides[1].start()
    col_keep().wait()
    over_cols(lambda t, z: col_in(t, z).wait_recv())
    for k in range(4):
        col_hops[k].start()
    arrange(0, 0)
    arrange(0, 1)
    for k, (land, d, half) in enumerate(arrivals):
        row_wait(land, d, half)
        if k < 2:
            row_hops[4 + k].start()
        sides[2 + k].start()
        col_wait(land, d, half)
        if k < 2:
            col_hops[4 + k].start()
        arrange(d, half)
    for k, (dy, half) in enumerate([(0, 0), (0, 1)] + [(dy, half) for _, dy, half in arrivals]):
        side(k, dy, half, 1).wait_recv()
    over_rows(lambda b, z: row_copy(b, z).wait_send())
    over_cols(lambda t, z: col_copy(t, z).wait_send())
    for copy in row_hops + col_hops + sides:
        copy.wait_send()


def panels_call(index, planes, factor):
    vmem = pl.BlockSpec(memory_space=pltpu.VMEM)
    dma = pltpu.SemaphoreType.DMA
    return pl.pallas_call(
        panels_kernel,
        name="panels",
        out_shape=(
            jax.ShapeDtypeStruct((8, RP, 256), BF),
            jax.ShapeDtypeStruct((2048, 2 * CP), BF),
        ),
        in_specs=[pl.BlockSpec(memory_space=pltpu.SMEM), vmem, vmem, vmem, vmem],
        out_specs=(vmem, vmem),
        scratch_shapes=[
            pltpu.VMEM((NBOX, 512), BF),
            pltpu.VMEM((NBOX, 512), F32),
            pltpu.VMEM((KB * NBOX, 128), F32),
            pltpu.VMEM((RP, 128), F32),
            pltpu.VMEM((NGRP, 16, RP), BF),
            pltpu.VMEM((NSLAB, 16, CP), BF),
            pltpu.VMEM((2, NGRP, 16, RP), BF),
            pltpu.VMEM((4, 2, NSLAB, 16, CP), BF),
            dma((NGRP, 2)),
            dma((2, NGRP)),
            dma((NSLAB, 2)),
            dma((2, NSLAB)),
            dma((6,)),
            dma((6,)),
            dma((6,)),
            dma((6,)),
            dma((8,)),
            dma((8,)),
            dma((2,)),
        ],
        compiler_params=pltpu.CompilerParams(
            collective_id=1, has_side_effects=True, vmem_limit_bytes=28 * 1024 * 1024
        ),
    )(index, planes, jnp.asarray(box_weights()), jnp.asarray(lane_order()), factor)


def tile_kernel(rp_ref, cab_ref, out_ref):
    rows = pl.ds(pl.multiple_of(pl.program_id(0) * 256, 256), 256)
    left = jnp.concatenate([rp_ref[k, rows, :] for k in range(8)], 1)
    o = jnp.dot(left, cab_ref[...], preferred_element_type=F32)
    out_ref[:, 0, :] = o[:, 0:CB]
    out_ref[:, 1, :] = o[:, CP : CP + CB]


def tile_call(row_panel, column_panel):
    rows = 256
    tiles = pl.pallas_call(
        tile_kernel,
        name="tile",
        grid=(RP // rows,),
        out_shape=jax.ShapeDtypeStruct((RB, 2, CB), F32),
        in_specs=[
            pl.BlockSpec((8, RP, 256), lambda i: (0, 0, 0)),
            pl.BlockSpec((2048, 2 * CP), lambda i: (0, 0)),
        ],
        out_specs=pl.BlockSpec((rows, 2, CB), lambda i: (i, 0, 0)),
        compiler_params=pltpu.CompilerParams(vmem_limit_bytes=32 * 1024 * 1024),
    )(row_panel, column_panel)
    return jnp.transpose(tiles, (1, 0, 2))


def table_look_up(index, table):
    hot = index[:, None] == jnp.arange(KB, dtype=jnp.int32)[None, :]
    return jnp.sum(jnp.where(hot, jnp.asarray(table)[None, :], 0), 1)


def on_device(
    valence_waves, conduction_waves, valence_energy, conduction_energy, occupation, gvec_ids
):
    g, gat = place_in_groups()
    s = lax.axis_index("slab")
    row, shifted = row_tables()
    along_x = gvec_ids // (KB * KB)
    along_y = gvec_ids // KB % KB
    along_z = gvec_ids % KB
    place = table_look_up(along_y, row * KB + shifted * 1024 * KB)
    index = (along_z ^ (place // (1024 * KB))) * NBOX + place % (1024 * KB) + along_x

    bands = [(0, 0), (0, 1), (-1, 0), (1, 0), (-1, 1), (1, 1), (2, 0), (2, 1)]
    order = jnp.stack([gat(*spot) for spot in bands])
    hot = (order[:, None] == jnp.arange(NV, dtype=jnp.int32)[None, :]).astype(F32)
    full = occupation.astype(F32)[:, None] / (
        (valence_energy[:, None] - conduction_energy[None, :]) * math.sqrt(NV * NC)
    )
    mine = jnp.sum(jnp.where(jnp.arange(NSLAB)[None, :] == s, full, 0.0), 1)
    factor = jnp.sum(hot * mine[None, :], 1)
    factor = jnp.broadcast_to(jnp.concatenate([factor, factor])[:, None], (16, 128))

    planes = planes_call(valence_waves, conduction_waves)
    row_panel, column_panel = panels_call(index, planes, factor)
    return tile_call(row_panel, column_panel)


def solution(mesh):
    in_specs = (P("grp", "slab", None, None), P("grp", "slab", None, None), P(), P("grp"), P(), P())
    out_specs = P(None, "grp", "slab")
    return jax.shard_map(
        on_device, mesh=mesh, in_specs=in_specs, out_specs=out_specs, check_vma=False
    )
```

```python
import functools
import math

import jax
import jax.numpy as jnp
import ml_dtypes
import numpy as np
from jax import lax
from jax.experimental import pallas as pl
from jax.experimental.pallas import tpu as pltpu
from jax.sharding import PartitionSpec as P

NV = 8
NC = 128
NF = 128
KB = 32
NG = 12000
NGRP = 8
NSLAB = 16
NX = NF // NSLAB
HX = NX // 2
NR = 24
RB = NG // NGRP
CB = NG // NSLAB
RP = 1536
CP = 768
NBOX = NR * KB
MESH = pl.DeviceIdType.MESH
BF = jnp.bfloat16
F32 = jnp.float32

WIDE = [9, -9, 11, -11, 5, -5]
NARROW = [13, -13, 12, -12, 14, -14]
SINGLE = [0, 1, -1, 2, -2, 3, -3, 4, -4, 6, -6, 7, -7, 8, -8, 10, -10]
ROW_FREQ = SINGLE[:16] + [SINGLE[16]] + WIDE + [15] + [15] + NARROW + [15]


def freq(j):
    return j - KB if j >= KB // 2 else j


def row_tables():
    row = np.zeros(KB, np.int32)
    shifted = np.zeros(KB, np.int32)
    for place, f in enumerate(ROW_FREQ[:NR]):
        if f != 15:
            row[f % KB] = place
    for place, f in enumerate(NARROW):
        row[f % KB] = 17 + place
        shifted[f % KB] = KB // 2
    return row, shifted


def phases(positions, freqs):
    angle = np.mod(np.outer(positions, freqs), NF).astype(np.float32) * np.float32(2.0 * math.pi / NF)
    return np.cos(angle).astype(np.float32), np.sin(angle).astype(np.float32)


def depth_weights():
    cos, sin = phases(np.arange(NF), [freq(j) for j in range(KB)])
    w = np.zeros((4, 2, NF, 2, KB, 4), np.float32)
    for vl in range(4):
        w[vl, 0, :, 0, :, vl] = cos
        w[vl, 1, :, 0, :, vl] = sin
        w[vl, 0, :, 1, :, vl] = -sin
        w[vl, 1, :, 1, :, vl] = cos
    return w.reshape(8 * NF, 8 * KB).astype(ml_dtypes.bfloat16)


def height_weights():
    cos, sin = phases(np.arange(NF), ROW_FREQ)
    return np.concatenate([cos.T, sin.T], 0).astype(ml_dtypes.bfloat16)


def wide_mask():
    mask = np.ones((8, KB, 4), np.float32)
    for place, f in enumerate(WIDE):
        half = math.isqrt(196 - f * f)
        for j in range(KB):
            if abs(freq(j)) > half:
                mask[1 + place, j] = 0.0
    return mask.reshape(8, 4 * KB)


def box_weights():
    cos, sin = phases(np.arange(NF), [freq(j) for j in range(KB)])
    cos = cos.T.reshape(KB, NSLAB, 2, HX).transpose(0, 2, 1, 3)
    sin = sin.T.reshape(KB, NSLAB, 2, HX).transpose(0, 2, 1, 3)
    t = np.zeros((2, KB, 2, NSLAB, 2, HX), np.float32)
    t[0, :, :, :, 0] = cos
    t[0, :, :, :, 1] = sin
    t[1, :, :, :, 0] = -sin
    t[1, :, :, :, 1] = cos
    high = t.astype(ml_dtypes.bfloat16)
    low = (t - high.astype(np.float32)).astype(ml_dtypes.bfloat16)
    pair = np.zeros((2, 2, 2, KB, 2, NSLAB, 2, 2, HX), ml_dtypes.bfloat16)
    for r in range(2):
        pair[r, 0, :, :, :, :, r] = high
        pair[r, 1, :, :, :, :, r] = low
    return pair.reshape(8 * KB, 4 * NF)


def lane_order():
    m = np.zeros((2, 2, KB, 4, KB, 2, 2, 4), np.float32)
    for reim in range(2):
        for vg in range(2):
            for kz in range(KB):
                for vl in range(4):
                    m[reim, vg, kz, vl, kz, reim, vg, vl] = 1.0
    return m.reshape(512, 512).astype(ml_dtypes.bfloat16)


def place_in_groups():
    g = lax.axis_index("grp")
    gx, gz = g // 2, lax.rem(g, 2)

    def at(dx, dz):
        return lax.rem(gx + dx + 4, 4) * 2 + (lax.rem(gz + dz, 2))

    return g, at


def place_in_slabs():
    s = lax.axis_index("slab")
    sz, sy, sc = s // 8, lax.rem(s // 2, 4), lax.rem(s, 2)

    def at(dy, dz, dc):
        return lax.rem(sz + dz, 2) * 8 + lax.rem(sy + dy + 4, 4) * 2 + lax.rem(sc + dc, 2)

    return s, at


def enter(groups, slabs):
    barrier = pltpu.get_barrier_semaphore()
    for one in groups:
        pl.semaphore_signal(barrier, inc=1, device_id={"grp": one}, device_id_type=MESH)
    for one in slabs:
        pl.semaphore_signal(barrier, inc=1, device_id={"slab": one}, device_id_type=MESH)
    pl.semaphore_wait(barrier, len(groups) + len(slabs))


def remote(src, dst, send, recv, device):
    return pltpu.make_async_remote_copy(
        src_ref=src, dst_ref=dst, send_sem=send, recv_sem=recv, device_id=device, device_id_type=MESH
    )


def planes_kernel(
    val_ref, con_ref, wz_ref, ty_ref, mask_ref, out_ref, val, con, msg, wz, even, odd, first_even, first_odd, scr, con_sem, own_sem, wz_sem, vs, vr, ms, mr, local_sem
):
    g, gat = place_in_groups()
    s, sat = place_in_slabs()
    own = pltpu.make_async_copy(val_ref.at[0], val.at[0], own_sem)
    own.start()
    weights = pltpu.make_async_copy(wz_ref, wz, wz_sem)
    weights.start()

    def band(i):
        k = lax.rem(i + 16, 16) // 2
        step = lax.rem(k + 1, 4)
        step = step + lax.rem(s, 2) * (4 - 2 * step)
        return sat(lax.rem(step, 4), lax.rem(i + 17, 2), 1 - k // 4)

    def con_copy(c):
        return pltpu.make_async_copy(con_ref.at[c], con.at[c], con_sem.at[c])

    def start_con(i, _):
        con_copy(band(i)).start()
        return 0

    lax.fori_loop(0, NSLAB, start_con, 0)
    partner, ahead, behind = gat(0, 1), gat(1, 0), gat(-1, 0)
    enter([partner, ahead, behind], [lax.rem(s + i, NSLAB) for i in range(1, NSLAB)])
    own.wait()

    def hop(k, slot, to, landing):
        return [
            remote(
                val.at[slot, pl.ds(half * HX, HX)],
                val.at[landing, pl.ds(half * HX, HX)],
                vs.at[k, half],
                vr.at[landing, half],
                {"grp": to},
            )
            for half in range(2)
        ]

    to_partner, to_ahead, to_behind = hop(0, 0, partner, 1), hop(1, 0, ahead, 2), hop(2, 0, behind, 3)
    p_ahead, p_behind = hop(3, 1, ahead, 4), hop(4, 1, behind, 5)
    l_ahead, r_behind = hop(5, 2, ahead, 6), hop(6, 5, behind, 7)
    for half in range(2):
        to_ahead[half].start()
        to_behind[half].start()
        to_partner[half].start()
    weights.wait()

    def message(vg, half, c):
        return remote(
            msg.at[vg, half, c], out_ref.at[vg, half, s], ms.at[vg, half, c], mr.at[vg, half, s], {"slab": c}
        )

    def arrival(vg, half, src):
        return remote(
            msg.at[vg, half, src],
            out_ref.at[vg, half, src],
            ms.at[vg, half, src],
            mr.at[vg, half, src],
            {"slab": src},
        )

    def kept(vg, half):
        return pltpu.make_async_copy(msg.at[vg, half, s], out_ref.at[vg, half, s], local_sem.at[vg, half])

    def density(vg, half, c, buf, x):
        for y0 in range(0, NF, 32):
            rows = pl.ds(y0, 32)
            put = pl.ds(x * NF + y0, 32)
            cr = con[c, half * HX + x, rows, 0:NF]
            ci = con[c, half * HX + x, rows, NF : 2 * NF]
            for vl in range(4):
                pr = val[vg * 4 + vl, half * HX + x, rows, 0:NF]
                pi = val[vg * 4 + vl, half * HX + x, rows, NF : 2 * NF]
                buf[put, vl * 256 : vl * 256 + NF] = pr * cr + pi * ci
                buf[put, vl * 256 + NF : vl * 256 + 256] = pr * ci - pi * cr

    def along_z(part, buf, first):
        rows = pl.ds(part * HX * NF // 2, HX * NF // 2)
        first[rows, :] = jnp.dot(buf[rows, :], wz[...], preferred_element_type=F32).astype(BF)

    def along_y(x, first):
        o = jnp.dot(ty_ref[...], first[x * NF : x * NF + NF, :], preferred_element_type=F32)
        keep = mask_ref[...] > 0.5
        for reim in range(2):
            if reim == 0:
                full = o[0:32, 0:128] + o[32:64, 128:256]
            else:
                full = o[0:32, 128:256] - o[32:64, 0:128]
            merged = jnp.where(keep, full[16:24], pltpu.roll(full[24:32], 64, 1))
            base = (reim * HX + x) * NR
            scr[base : base + 16, :] = full[0:16]
            scr[base + 16 : base + 24, :] = merged

    def pack(vg, half, c):
        for r in range(0, NR, 2):
            both = jnp.concatenate(
                [scr[pl.ds(r, 2 * HX, stride=NR), :], scr[pl.ds(r + 1, 2 * HX, stride=NR), :]], 0
            )
            msg[vg, half, c, r // 2] = both.astype(BF)

    def one_band(vg, half, before, after, buf, other, first, last):
        along_z(0, buf, first)
        density(vg, half, after, other, 0)
        density(vg, half, after, other, 1)
        along_y(0, last)
        along_y(1, last)
        along_z(1, buf, first)
        density(vg, half, after, other, 2)
        density(vg, half, after, other, 3)
        along_y(2, last)
        along_y(3, last)
        pack(vg, half, before)

    for phase in range(4):
        vg, half = phase // 2, phase % 2
        if phase == 0:
            for copies in (to_partner, to_ahead, to_behind):
                copies[0].wait_recv()
            p_behind[0].start()
            p_ahead[0].start()
            l_ahead[0].start()
        if phase == 1:
            for copies in (to_partner, to_ahead, to_behind):
                copies[1].wait_recv()
            p_ahead[1].start()
            p_behind[0].wait_recv()
            r_behind[0].start()
            p_behind[1].start()
            l_ahead[1].start()
        if phase >= 2:
            for copies in (p_ahead, l_ahead, r_behind):
                copies[half].wait_recv()
        start = band(0)
        if phase == 0:
            con_copy(start).wait()
        for x in range(HX):
            density(vg, half, start, even, x)

        def two_bands(j, _):
            before, c0, c1, c2 = band(2 * j - 1), band(2 * j), band(2 * j + 1), band(2 * j + 2)
            if phase == 0:
                con_copy(c1).wait()

                @pl.when(j < NSLAB // 2 - 1)
                def _():
                    con_copy(c2).wait()

            if phase == 2:

                @pl.when(j == 2)
                def _():
                    p_behind[1].wait_recv()
                    r_behind[1].start()

            one_band(vg, half, before, c1, even, odd, first_even, first_odd)

            @pl.when(j > 0)
            def _():
                message(vg, half, before).start()

            one_band(vg, half, c0, c2, odd, even, first_odd, first_even)
            message(vg, half, c0).start()
            return 0

        lax.fori_loop(0, NSLAB // 2, two_bands, 0)
        for x in range(HX):
            along_y(x, first_odd)
        pack(vg, half, s)
        kept(vg, half).start()

    def finish(i, _):
        other = lax.rem(s + i + 1, NSLAB)
        for vg in range(2):
            for half in range(2):
                arrival(vg, half, other).wait_recv()
                message(vg, half, other).wait_send()
        return 0

    lax.fori_loop(0, NSLAB - 1, finish, 0)
    for vg in range(2):
        for half in range(2):
            kept(vg, half).wait()
    for copies in (to_partner, to_ahead, to_behind, p_ahead, p_behind, l_ahead, r_behind):
        for half in range(2):
            copies[half].wait_send()


def planes_call(valence, conduction):
    anywhere = pl.BlockSpec(memory_space=pl.ANY)
    vmem = pl.BlockSpec(memory_space=pltpu.VMEM)
    return pl.pallas_call(
        planes_kernel,
        name="planes",
        out_shape=jax.ShapeDtypeStruct((2, 2, NSLAB, NR // 2, 16, 128), BF),
        in_specs=[anywhere, anywhere, anywhere, vmem, vmem],
        out_specs=vmem,
        scratch_shapes=[
            pltpu.VMEM((8, NX, NF, 2 * NF), BF),
            pltpu.VMEM((NSLAB, NX, NF, 2 * NF), BF),
            pltpu.VMEM((2, 2, NSLAB, NR // 2, 16, 128), BF),
            pltpu.VMEM((8 * NF, 2 * NF), BF),
            pltpu.VMEM((HX * NF, 8 * NF), BF),
            pltpu.VMEM((HX * NF, 8 * NF), BF),
            pltpu.VMEM((HX * NF, 2 * NF), BF),
            pltpu.VMEM((HX * NF, 2 * NF), BF),
            pltpu.VMEM((2 * HX * NR, 128), F32),
            pltpu.SemaphoreType.DMA((NSLAB,)),
            pltpu.SemaphoreType.DMA,
            pltpu.SemaphoreType.DMA,
            pltpu.SemaphoreType.DMA((7, 2)),
            pltpu.SemaphoreType.DMA((8, 2)),
            pltpu.SemaphoreType.DMA((2, 2, NSLAB)),
            pltpu.SemaphoreType.DMA((2, 2, NSLAB)),
            pltpu.SemaphoreType.DMA((2, 2)),
        ],
        compiler_params=pltpu.CompilerParams(
            collective_id=0, has_side_effects=True, vmem_limit_bytes=56 * 1024 * 1024
        ),
    )(
        valence,
        conduction,
        jnp.asarray(depth_weights()),
        jnp.asarray(height_weights()),
        jnp.asarray(wide_mask()),
    )


def panels_kernel(
    idx_ref, ve_ref, ce_ref, oc_ref, in_ref, tab_ref, order_ref, acc_ref, left_ref, right_ref,
    rp_ref, cab_ref, xb, wide, box, blk, rows, cols, landed, cp,
    rsa, rra, csa, cra, rs, rr, cs, cr, sib_s, sib_r, lsem,
):
    g, gat = place_in_groups()
    s, sat = place_in_slabs()
    gx, gz = g // 2, lax.rem(g, 2)
    sz, yc, sc = s // 8, lax.rem(s, 8), lax.rem(s, 2)
    scaling = 0.5 / float(NF) ** 1.5

    barrier = pltpu.get_barrier_semaphore()
    for i in range(2 * NSLAB):
        if i:
            to = {"grp": gat(0, i // NSLAB), "slab": lax.rem(s + i, NSLAB)}
            pl.semaphore_signal(barrier, inc=1, device_id=to, device_id_type=MESH)
    for i in range(4, 16):
        to = {"grp": gat(i // 4, i // 2 % 2), "slab": sat(0, i % 2, 0)}
        pl.semaphore_signal(barrier, inc=1, device_id=to, device_id_type=MESH)

    def four_rows(j, _):
        for k in range(2):
            p = j * 2 + k
            a = [in_ref[vg, :, :, pl.ds(p, 1)].reshape(4 * NF, 128) for vg in range(2)]
            both = jnp.dot(tab_ref[...], jnp.concatenate(a, 1), preferred_element_type=F32)
            for r in range(2):
                o = both[r * 128 : r * 128 + 128]
                o = ((o[0:64] + o[64:128]) * scaling).astype(BF)
                put = pl.ds(pl.multiple_of((p * 2 + r) * KB, KB), KB)
                xb[put, 0:256] = o[0:32]
                xb[put, 256:512] = o[32:64]
        return 0

    lax.fori_loop(0, NR // 4, four_rows, 0)
    wide[...] = jnp.dot(xb[...], order_ref[...], preferred_element_type=F32)

    def spread(j, _):
        base = pl.multiple_of(j * 96, 32)
        for kz in range(KB):
            part = wide[pl.ds(base, 96), (kz // 8) * 128 : (kz // 8 + 1) * 128]
            if kz % 8:
                part = pltpu.roll(part, 128 - 16 * (kz % 8), 1)
            box[pl.ds(pl.multiple_of(kz * NBOX + base, 8), 96), :] = part
        return 0

    lax.fori_loop(0, NBOX // 96, spread, 0)
    blk[1496:1536, :] = jnp.zeros((40, 128), F32)
    for chunk in range(6):
        cab_ref[chunk * 256 + 128 : chunk * 256 + 192, :] = jnp.zeros((64, 2 * CP), BF)
    slot = lax.rem(lax.broadcasted_iota(jnp.int32, (16, CP), 0), 8)
    charge, gap = jnp.zeros((16, CP), F32), jnp.ones((16, CP), F32)
    for place, spot in enumerate([(0, 0), (0, 1), (-1, 0), (1, 0), (-1, 1), (1, 1), (2, 0), (2, 1)]):
        v = gat(*spot)
        charge = jnp.where(slot == place, oc_ref[v].astype(F32), charge)
        gap = jnp.where(slot == place, ve_ref[v] - ce_ref[s], gap)
    factor = (charge / (gap * math.sqrt(NV * NC)))[:, 0:1]
    pl.semaphore_wait(barrier, 43)

    lane = lax.broadcasted_iota(jnp.int32, (16, 128), 1)
    row = lax.broadcasted_iota(jnp.int32, (16, 128), 0)
    unit = jnp.where(lane == row, 1.0, 0.0).astype(BF)
    contract = (((1,), (1,)), ((), ()))

    def row_copy(b, z):
        to = {"grp": b, "slab": z * 8 + yc}
        dx = lax.rem(gx - b // 2 + 4, 4)
        return remote(rows.at[b], landed.at[dx, gz, sz], rsa.at[b, z], rra.at[dx, gz, sz], to)

    def row_in(b, z):
        to = {"grp": b, "slab": z * 8 + yc}
        dx, bz = lax.rem(b // 2 - gx + 4, 4), lax.rem(b, 2)
        return remote(rows.at[b], landed.at[dx, bz, z], rsa.at[b, z], rra.at[dx, bz, z], to)

    def row_keep():
        return pltpu.make_async_copy(rows.at[g], landed.at[0, gz, sz], lsem.at[0])

    def col_copy(t, z):
        to = {"grp": gx * 2 + z, "slab": t}
        return remote(cols.at[t], cp.at[gx, gz, s], csa.at[t, z], cra.at[gz, s], to)

    def col_in(t, z):
        to = {"grp": gx * 2 + z, "slab": t}
        return remote(cols.at[t], cp.at[gx, z, t], csa.at[t, z], cra.at[z, t], to)

    def col_keep():
        return pltpu.make_async_copy(cols.at[s], cp.at[gx, gz, s], lsem.at[1])

    def one_block(i, _):
        b = lax.rem(g + yc // 2 + sz * 4 + i, NGRP)

        def pick(j, _):
            base = j * 60
            for k in range(60):
                blk[pl.ds(base + k, 1), :] = box[pl.ds(idx_ref[b * RB + base + k], 1), :]
            return 0

        lax.fori_loop(0, RB // 60, pick, 0)
        o = lax.dot_general(unit, blk[0:RP, :].astype(BF), contract, preferred_element_type=F32)
        rows[b] = (o * factor).astype(BF)
        for half in range(2):
            part = blk[half * CB : half * CB + CP, :].astype(BF)
            cols[2 * b + half] = lax.dot_general(unit, part, contract, preferred_element_type=F32).astype(BF)
        for z in range(2):
            mine = jnp.logical_and(b == g, z == sz)

            @pl.when(mine)
            def _():
                row_keep().start()

            @pl.when(jnp.logical_not(mine))
            def _():
                row_copy(b, z).start()

            for half in range(2):
                own = jnp.logical_and(2 * b + half == s, z == gz)

                @pl.when(own)
                def _():
                    col_keep().start()

                @pl.when(jnp.logical_not(own))
                def _():
                    col_copy(2 * b + half, z).start()

        return 0

    lax.fori_loop(0, NGRP, one_block, 0)

    def over_rows(act):
        def step(i, _):
            b, z = i // 2, lax.rem(i, 2)

            @pl.when(jnp.logical_not(jnp.logical_and(b == g, z == sz)))
            def _():
                act(b, z)

            return 0

        lax.fori_loop(0, 2 * NGRP, step, 0)

    def over_cols(act):
        def step(i, _):
            t, z = i // 2, lax.rem(i, 2)

            @pl.when(jnp.logical_not(jnp.logical_and(t == s, z == gz)))
            def _():
                act(t, z)

            return 0

        lax.fori_loop(0, 2 * NSLAB, step, 0)

    def row_part(dy, dc, half):
        return rp_ref.at[PLACE[dy], lax.rem(sc + dc, 2), pl.ds(half * 768, 768)]

    def row_hop(k, dy, half, to, land):
        there = dy - to if dy - to > -2 else 2
        return remote(
            row_part(dy, 0, half), row_part(there, 0, half), rs.at[k], rr.at[land], {"slab": sat(to, 0, 0)}
        )

    def row_wait(land, dy, half):
        part = row_part(dy, 0, half)
        remote(part, part, rs.at[0], rr.at[land], {"slab": sat(1, 0, 0)}).wait_recv()

    def side(k, dy, half, dc=0):
        part = row_part(dy, dc, half)
        return remote(part, part, sib_s.at[k], sib_r.at[k], {"slab": sat(0, 0, 1)})

    def col_part(dx, half):
        return cp.at[gat(dx, 0) // 2, half]

    def col_hop(k, dx, half, to, land):
        part = col_part(dx, half)
        return remote(part, part, cs.at[k], cr.at[land], {"grp": gat(to, 0)})

    def col_wait(land, dx, half):
        part = col_part(dx, half)
        remote(part, part, cs.at[0], cr.at[land], {"grp": gat(1, 0)}).wait_recv()

    hops = [(0, 0, 1, 0), (0, 1, -1, 3), (0, 1, 1, 1), (0, 0, -1, 2), (-1, 0, 1, 4), (1, 1, -1, 5)]
    arrivals = [(0, -1, 0), (3, 1, 1), (1, -1, 1), (2, 1, 0), (4, 2, 0), (5, 2, 1)]
    own_and_near = [(0, 0), (0, 1)] + [(dy, half) for _, dy, half in arrivals]
    row_hops = [row_hop(k, *hop) for k, hop in enumerate(hops)]
    col_hops = [col_hop(k, *hop) for k, hop in enumerate(hops)]
    sides = [side(0, 0, 0), side(1, 0, 1)] + [side(2 + k, dy, half) for k, (_, dy, half) in enumerate(arrivals)]

    def arrange(dx, half):
        x = gat(dx, 0) // 2
        for dy in (0, -1, 1, 2):
            for dc in range(2):
                chunk = PLACE[dy] * 2 + dc
                for z in range(2):
                    t = z * 8 + lax.rem(yc // 2 + dy + 4, 4) * 2 + dc
                    part = cp[x, half, pl.ds(t, 1)].reshape(16, CP)
                    value = part.astype(F32)
                    turned = jnp.concatenate([-value[8:16], value[0:8]], 0).astype(BF)
                    put = (dx % 4) * 64 + half * 32 + z * 16
                    if dy == 2:
                        to, put = right_ref, dc * 256 + put
                    elif dx == 2:
                        to, put = right_ref, 512 + chunk * 64 + half * 32 + z * 16
                    else:
                        to, put = cab_ref, chunk * 256 + put
                    to[put : put + 16, 0:CP] = part
                    to[put : put + 16, CP : 2 * CP] = turned

    row_keep().wait()
    over_rows(lambda b, z: row_in(b, z).wait_recv())
    for j in range(RP // 128):
        part = landed[:, :, :, :, j * 128 : (j + 1) * 128].reshape(256, 128).astype(F32)
        rp_ref[0, sc, j * 128 : (j + 1) * 128, :] = part.T.astype(BF)
        if j == 5:
            row_hops[0].start()
            sides[0].start()
    row_hops[1].start()
    row_hops[2].start()
    row_hops[3].start()
    sides[1].start()
    col_keep().wait()
    over_cols(lambda t, z: col_in(t, z).wait_recv())
    for k in range(4):
        col_hops[k].start()
    arrange(0, 0)
    arrange(0, 1)
    for k, (land, d, half) in enumerate(arrivals):
        row_wait(land, d, half)
        if k < 2:
            row_hops[4 + k].start()
        sides[2 + k].start()
        col_wait(land, d, half)
        if k < 2:
            col_hops[4 + k].start()
        arrange(d, half)
        if k == 3:
            for n in range(6):
                side(n, *own_and_near[n], 1).wait_recv()

            def near(m, _):
                put = pl.ds(pl.multiple_of(m * 256, 256), 256)
                parts = [rp_ref[p, c, put, :] for p in range(3) for c in range(2)]
                acc_ref[put, :] = jnp.dot(jnp.concatenate(parts, 1), cab_ref[...], preferred_element_type=F32)
                for pair in range(3):
                    both = [parts[2 * pair][:, 128:192], parts[2 * pair + 1][:, 128:192]]
                    left_ref[put, 512 + pair * 128 : 640 + pair * 128] = jnp.concatenate(both, 1)
                return 0

            lax.fori_loop(0, RP // 256, near, 0)
    for n in range(6, 8):
        side(n, *own_and_near[n], 1).wait_recv()
    for c in range(2):
        left_ref[:, c * 256 : c * 256 + 256] = rp_ref[3, c]
    over_rows(lambda b, z: row_copy(b, z).wait_send())
    over_cols(lambda t, z: col_copy(t, z).wait_send())
    for copy in row_hops + col_hops + sides:
        copy.wait_send()


PLACE = {0: 0, -1: 1, 1: 2, 2: 3}


def panels_call(index, planes, valence_energy, conduction_energy, occupation):
    smem = pl.BlockSpec(memory_space=pltpu.SMEM)
    vmem = pl.BlockSpec(memory_space=pltpu.VMEM)
    dma = pltpu.SemaphoreType.DMA
    return pl.pallas_call(
        panels_kernel,
        name="panels",
        out_shape=(
            jax.ShapeDtypeStruct((RP, 2 * CP), F32),
            jax.ShapeDtypeStruct((RP, 896), BF),
            jax.ShapeDtypeStruct((896, 2 * CP), BF),
        ),
        in_specs=[smem, smem, smem, smem, vmem, vmem, vmem],
        out_specs=(vmem, vmem, vmem),
        scratch_shapes=[
            pltpu.VMEM((4, 2, RP, 256), BF),
            pltpu.VMEM((1536, 2 * CP), BF),
            pltpu.VMEM((NBOX, 512), BF),
            pltpu.VMEM((NBOX, 512), F32),
            pltpu.VMEM((KB * NBOX, 128), F32),
            pltpu.VMEM((RP, 128), F32),
            pltpu.VMEM((NGRP, 16, RP), BF),
            pltpu.VMEM((NSLAB, 16, CP), BF),
            pltpu.VMEM((4, 2, 2, 16, RP), BF),
            pltpu.VMEM((4, 2, NSLAB, 16, CP), BF),
            dma((NGRP, 2)),
            dma((4, 2, 2)),
            dma((NSLAB, 2)),
            dma((2, NSLAB)),
            dma((6,)),
            dma((6,)),
            dma((6,)),
            dma((6,)),
            dma((8,)),
            dma((8,)),
            dma((2,)),
        ],
        compiler_params=pltpu.CompilerParams(
            collective_id=1, has_side_effects=True, vmem_limit_bytes=34 * 1024 * 1024
        ),
    )(
        index,
        valence_energy,
        conduction_energy,
        occupation,
        planes,
        jnp.asarray(box_weights()),
        jnp.asarray(lane_order()),
    )


def tile_kernel(acc_ref, left_ref, right_ref, out_ref):
    rows = pl.ds(pl.multiple_of(pl.program_id(0) * 256, 256), 256)
    o = jnp.dot(left_ref[rows, :], right_ref[...], preferred_element_type=F32) + acc_ref[rows, :]
    out_ref[:, 0, :] = o[:, 0:CB]
    out_ref[:, 1, :] = o[:, CP : CP + CB]


def tile_call(near, left, right):
    rows = 256
    tiles = pl.pallas_call(
        tile_kernel,
        name="tile",
        grid=(RP // rows,),
        out_shape=jax.ShapeDtypeStruct((RB, 2, CB), F32),
        in_specs=[
            pl.BlockSpec((RP, 2 * CP), lambda i: (0, 0)),
            pl.BlockSpec((RP, 896), lambda i: (0, 0)),
            pl.BlockSpec((896, 2 * CP), lambda i: (0, 0)),
        ],
        out_specs=pl.BlockSpec((rows, 2, CB), lambda i: (i, 0, 0)),
        compiler_params=pltpu.CompilerParams(vmem_limit_bytes=32 * 1024 * 1024),
    )(near, left, right)
    return jnp.transpose(tiles, (1, 0, 2))


def table_look_up(index, table):
    found = jnp.zeros_like(index)
    for place, value in enumerate(table):
        found = jnp.where(index == place, int(value), found)
    return found


def on_device(
    valence_waves, conduction_waves, valence_energy, conduction_energy, occupation, gvec_ids
):
    row, shifted = row_tables()
    along_x = gvec_ids // (KB * KB)
    along_y = gvec_ids // KB % KB
    along_z = gvec_ids % KB
    place = table_look_up(along_y, row * KB + shifted * 1024 * KB)
    index = (along_z ^ (place // (1024 * KB))) * NBOX + place % (1024 * KB) + along_x

    planes = planes_call(valence_waves, conduction_waves)
    near, left, right = panels_call(index, planes, valence_energy, conduction_energy, occupation)
    return tile_call(near, left, right)


def solution(mesh):
    in_specs = (P("grp", "slab", None, None), P("grp", "slab", None, None), P(), P("grp"), P(), P())
    out_specs = P(None, "grp", "slab")
    return jax.shard_map(
        on_device, mesh=mesh, in_specs=in_specs, out_specs=out_specs, check_vma=False
    )
```

```python
import functools
import math

import jax
import jax.numpy as jnp
import ml_dtypes
import numpy as np
from jax import lax
from jax.experimental import pallas as pl
from jax.experimental.pallas import tpu as pltpu
from jax.sharding import PartitionSpec as P

NV = 8
NC = 128
NF = 128
KB = 32
NG = 12000
NGRP = 8
NSLAB = 16
NX = NF // NSLAB
HX = NX // 2
NR = 24
RB = NG // NGRP
CB = NG // NSLAB
RP = 1536
CP = 768
NBOX = NR * KB
MESH = pl.DeviceIdType.MESH
BF = jnp.bfloat16
F32 = jnp.float32

WIDE = [9, -9, 11, -11, 5, -5]
NARROW = [13, -13, 12, -12, 14, -14]
SINGLE = [0, 1, -1, 2, -2, 3, -3, 4, -4, 6, -6, 7, -7, 8, -8, 10, -10]
ROW_FREQ = SINGLE[:16] + [SINGLE[16]] + WIDE + [15] + [15] + NARROW + [15]


def freq(j):
    return j - KB if j >= KB // 2 else j


def row_tables():
    row = np.zeros(KB, np.int32)
    shifted = np.zeros(KB, np.int32)
    for place, f in enumerate(ROW_FREQ[:NR]):
        if f != 15:
            row[f % KB] = place
    for place, f in enumerate(NARROW):
        row[f % KB] = 17 + place
        shifted[f % KB] = KB // 2
    return row, shifted


def phases(positions, freqs):
    angle = np.mod(np.outer(positions, freqs), NF).astype(np.float32) * np.float32(2.0 * math.pi / NF)
    return np.cos(angle).astype(np.float32), np.sin(angle).astype(np.float32)


def depth_weights():
    cos, sin = phases(np.arange(NF), [freq(j) for j in range(KB)])
    w = np.zeros((4, 2, NF, 2, KB, 4), np.float32)
    for vl in range(4):
        w[vl, 0, :, 0, :, vl] = cos
        w[vl, 1, :, 0, :, vl] = sin
        w[vl, 0, :, 1, :, vl] = -sin
        w[vl, 1, :, 1, :, vl] = cos
    return w.reshape(8 * NF, 8 * KB).astype(ml_dtypes.bfloat16)


def height_weights():
    cos, sin = phases(np.arange(NF), ROW_FREQ)
    return np.concatenate([cos.T, sin.T], 0).astype(ml_dtypes.bfloat16)


def wide_mask():
    mask = np.ones((8, KB, 4), np.float32)
    for place, f in enumerate(WIDE):
        half = math.isqrt(196 - f * f)
        for j in range(KB):
            if abs(freq(j)) > half:
                mask[1 + place, j] = 0.0
    return mask.reshape(8, 4 * KB)


def box_weights():
    cos, sin = phases(np.arange(NF), [freq(j) for j in range(KB)])
    cos = cos.T.reshape(KB, NSLAB, 2, HX).transpose(0, 2, 1, 3)
    sin = sin.T.reshape(KB, NSLAB, 2, HX).transpose(0, 2, 1, 3)
    t = np.zeros((2, KB, 2, NSLAB, 2, HX), np.float32)
    t[0, :, :, :, 0] = cos
    t[0, :, :, :, 1] = sin
    t[1, :, :, :, 0] = -sin
    t[1, :, :, :, 1] = cos
    high = t.astype(ml_dtypes.bfloat16)
    low = (t - high.astype(np.float32)).astype(ml_dtypes.bfloat16)
    pair = np.zeros((2, 2, 2, KB, 2, NSLAB, 2, 2, HX), ml_dtypes.bfloat16)
    for r in range(2):
        pair[r, 0, :, :, :, :, r] = high
        pair[r, 1, :, :, :, :, r] = low
    return pair.reshape(8 * KB, 4 * NF)


def lane_order():
    m = np.zeros((2, 2, KB, 4, KB, 2, 2, 4), np.float32)
    for reim in range(2):
        for vg in range(2):
            for kz in range(KB):
                for vl in range(4):
                    m[reim, vg, kz, vl, kz, reim, vg, vl] = 1.0
    return m.reshape(512, 512).astype(ml_dtypes.bfloat16)


def place_in_groups():
    g = lax.axis_index("grp")
    gx, gz = g // 2, lax.rem(g, 2)

    def at(dx, dz):
        return lax.rem(gx + dx + 4, 4) * 2 + (lax.rem(gz + dz, 2))

    return g, at


def place_in_slabs():
    s = lax.axis_index("slab")
    sz, sy, sc = s // 8, lax.rem(s // 2, 4), lax.rem(s, 2)

    def at(dy, dz, dc):
        return lax.rem(sz + dz, 2) * 8 + lax.rem(sy + dy + 4, 4) * 2 + lax.rem(sc + dc, 2)

    return s, at


def enter(groups, slabs):
    barrier = pltpu.get_barrier_semaphore()
    for one in groups:
        pl.semaphore_signal(barrier, inc=1, device_id={"grp": one}, device_id_type=MESH)
    for one in slabs:
        pl.semaphore_signal(barrier, inc=1, device_id={"slab": one}, device_id_type=MESH)
    pl.semaphore_wait(barrier, len(groups) + len(slabs))


def remote(src, dst, send, recv, device):
    return pltpu.make_async_remote_copy(
        src_ref=src, dst_ref=dst, send_sem=send, recv_sem=recv, device_id=device, device_id_type=MESH
    )


def planes_kernel(
    val_ref, con_ref, wz_ref, ty_ref, mask_ref, out_ref, val, con, msg, wz, even, odd, first_even, first_odd, scr, con_sem, own_sem, wz_sem, vs, vr, ms, mr, local_sem
):
    g, gat = place_in_groups()
    s, sat = place_in_slabs()
    own = pltpu.make_async_copy(val_ref.at[0], val.at[0], own_sem)
    own.start()
    weights = pltpu.make_async_copy(wz_ref, wz, wz_sem)
    weights.start()

    def band(i):
        k = lax.rem(i + 16, 16) // 2
        step = lax.rem(k + 1, 4)
        step = step + lax.rem(s, 2) * (4 - 2 * step)
        return sat(lax.rem(step, 4), lax.rem(i + 17, 2), 1 - k // 4)

    def con_copy(c):
        return pltpu.make_async_copy(con_ref.at[c], con.at[c], con_sem.at[c])

    def start_con(i, _):
        con_copy(band(i)).start()
        return 0

    lax.fori_loop(0, NSLAB, start_con, 0)
    partner, ahead, behind = gat(0, 1), gat(1, 0), gat(-1, 0)
    enter([partner, ahead, behind], [lax.rem(s + i, NSLAB) for i in range(1, NSLAB)])
    own.wait()

    def hop(k, slot, to, landing):
        return [
            remote(
                val.at[slot, pl.ds(half * HX, HX)],
                val.at[landing, pl.ds(half * HX, HX)],
                vs.at[k, half],
                vr.at[landing, half],
                {"grp": to},
            )
            for half in range(2)
        ]

    to_partner, to_ahead, to_behind = hop(0, 0, partner, 1), hop(1, 0, ahead, 2), hop(2, 0, behind, 3)
    p_ahead, p_behind = hop(3, 1, ahead, 4), hop(4, 1, behind, 5)
    l_ahead, r_behind = hop(5, 2, ahead, 6), hop(6, 5, behind, 7)
    for half in range(2):
        to_ahead[half].start()
        to_behind[half].start()
        to_partner[half].start()
    weights.wait()

    def message(vg, half, c):
        return remote(
            msg.at[vg, half, c], out_ref.at[vg, half, s], ms.at[vg, half, c], mr.at[vg, half, s], {"slab": c}
        )

    def arrival(vg, half, src):
        return remote(
            msg.at[vg, half, src],
            out_ref.at[vg, half, src],
            ms.at[vg, half, src],
            mr.at[vg, half, src],
            {"slab": src},
        )

    def kept(vg, half):
        return pltpu.make_async_copy(msg.at[vg, half, s], out_ref.at[vg, half, s], local_sem.at[vg, half])

    def density(vg, half, c, buf, x):
        for y0 in range(0, NF, 32):
            rows = pl.ds(y0, 32)
            put = pl.ds(x * NF + y0, 32)
            cr = con[c, half * HX + x, rows, 0:NF]
            ci = con[c, half * HX + x, rows, NF : 2 * NF]
            for vl in range(4):
                pr = val[vg * 4 + vl, half * HX + x, rows, 0:NF]
                pi = val[vg * 4 + vl, half * HX + x, rows, NF : 2 * NF]
                buf[put, vl * 256 : vl * 256 + NF] = pr * cr + pi * ci
                buf[put, vl * 256 + NF : vl * 256 + 256] = pr * ci - pi * cr

    def along_z(part, buf, first):
        rows = pl.ds(part * HX * NF // 2, HX * NF // 2)
        first[rows, :] = jnp.dot(buf[rows, :], wz[...], preferred_element_type=F32).astype(BF)

    def along_y(x, first):
        o = jnp.dot(ty_ref[...], first[x * NF : x * NF + NF, :], preferred_element_type=F32)
        keep = mask_ref[...] > 0.5
        for reim in range(2):
            if reim == 0:
                full = o[0:32, 0:128] + o[32:64, 128:256]
            else:
                full = o[0:32, 128:256] - o[32:64, 0:128]
            merged = jnp.where(keep, full[16:24], pltpu.roll(full[24:32], 64, 1))
            base = (reim * HX + x) * NR
            scr[base : base + 16, :] = full[0:16]
            scr[base + 16 : base + 24, :] = merged

    def pack(vg, half, c):
        for r in range(0, NR, 2):
            both = jnp.concatenate(
                [scr[pl.ds(r, 2 * HX, stride=NR), :], scr[pl.ds(r + 1, 2 * HX, stride=NR), :]], 0
            )
            msg[vg, half, c, r // 2] = both.astype(BF)

    def one_band(vg, half, before, after, buf, other, first, last):
        along_z(0, buf, first)
        density(vg, half, after, other, 0)
        density(vg, half, after, other, 1)
        along_y(0, last)
        along_y(1, last)
        along_z(1, buf, first)
        density(vg, half, after, other, 2)
        density(vg, half, after, other, 3)
        along_y(2, last)
        along_y(3, last)
        pack(vg, half, before)

    for phase in range(4):
        vg, half = phase // 2, phase % 2
        if phase == 0:
            for copies in (to_partner, to_ahead, to_behind):
                copies[0].wait_recv()
            p_behind[0].start()
            p_ahead[0].start()
            l_ahead[0].start()
        if phase == 1:
            for copies in (to_partner, to_ahead, to_behind):
                copies[1].wait_recv()
            p_ahead[1].start()
            p_behind[0].wait_recv()
            r_behind[0].start()
            p_behind[1].start()
            l_ahead[1].start()
        if phase >= 2:
            for copies in (p_ahead, l_ahead, r_behind):
                copies[half].wait_recv()
        start = band(0)
        if phase == 0:
            con_copy(start).wait()
        for x in range(HX):
            density(vg, half, start, even, x)

        def two_bands(j, _):
            before, c0, c1, c2 = band(2 * j - 1), band(2 * j), band(2 * j + 1), band(2 * j + 2)
            if phase == 0:
                con_copy(c1).wait()

                @pl.when(j < NSLAB // 2 - 1)
                def _():
                    con_copy(c2).wait()

            if phase == 2:

                @pl.when(j == 2)
                def _():
                    p_behind[1].wait_recv()
                    r_behind[1].start()

            one_band(vg, half, before, c1, even, odd, first_even, first_odd)

            @pl.when(j > 0)
            def _():
                message(vg, half, before).start()

            one_band(vg, half, c0, c2, odd, even, first_odd, first_even)
            message(vg, half, c0).start()
            return 0

        lax.fori_loop(0, NSLAB // 2, two_bands, 0)
        for x in range(HX):
            along_y(x, first_odd)
        pack(vg, half, s)
        kept(vg, half).start()

    def finish(i, _):
        other = lax.rem(s + i + 1, NSLAB)
        for vg in range(2):
            for half in range(2):
                arrival(vg, half, other).wait_recv()
                message(vg, half, other).wait_send()
        return 0

    lax.fori_loop(0, NSLAB - 1, finish, 0)
    for vg in range(2):
        for half in range(2):
            kept(vg, half).wait()
    for copies in (to_partner, to_ahead, to_behind, p_ahead, p_behind, l_ahead, r_behind):
        for half in range(2):
            copies[half].wait_send()


def planes_call(valence, conduction):
    anywhere = pl.BlockSpec(memory_space=pl.ANY)
    vmem = pl.BlockSpec(memory_space=pltpu.VMEM)
    return pl.pallas_call(
        planes_kernel,
        name="planes",
        out_shape=jax.ShapeDtypeStruct((2, 2, NSLAB, NR // 2, 16, 128), BF),
        in_specs=[anywhere, anywhere, anywhere, vmem, vmem],
        out_specs=vmem,
        scratch_shapes=[
            pltpu.VMEM((8, NX, NF, 2 * NF), BF),
            pltpu.VMEM((NSLAB, NX, NF, 2 * NF), BF),
            pltpu.VMEM((2, 2, NSLAB, NR // 2, 16, 128), BF),
            pltpu.VMEM((8 * NF, 2 * NF), BF),
            pltpu.VMEM((HX * NF, 8 * NF), BF),
            pltpu.VMEM((HX * NF, 8 * NF), BF),
            pltpu.VMEM((HX * NF, 2 * NF), BF),
            pltpu.VMEM((HX * NF, 2 * NF), BF),
            pltpu.VMEM((2 * HX * NR, 128), F32),
            pltpu.SemaphoreType.DMA((NSLAB,)),
            pltpu.SemaphoreType.DMA,
            pltpu.SemaphoreType.DMA,
            pltpu.SemaphoreType.DMA((7, 2)),
            pltpu.SemaphoreType.DMA((8, 2)),
            pltpu.SemaphoreType.DMA((2, 2, NSLAB)),
            pltpu.SemaphoreType.DMA((2, 2, NSLAB)),
            pltpu.SemaphoreType.DMA((2, 2)),
        ],
        compiler_params=pltpu.CompilerParams(
            collective_id=0, has_side_effects=True, vmem_limit_bytes=56 * 1024 * 1024
        ),
    )(
        valence,
        conduction,
        jnp.asarray(depth_weights()),
        jnp.asarray(height_weights()),
        jnp.asarray(wide_mask()),
    )


def panels_kernel(
    idx_ref, ve_ref, ce_ref, oc_ref, in_ref, tab_ref, order_ref, acc_ref, left_ref, right_ref,
    rp_ref, cab_ref, xb, wide, box, blk, rows, cols, landed, cp,
    rsa, rra, csa, cra, rs, rr, cs, cr, sib_s, sib_r, lsem,
):
    g, gat = place_in_groups()
    s, sat = place_in_slabs()
    gx, gz = g // 2, lax.rem(g, 2)
    sz, yc, sc = s // 8, lax.rem(s, 8), lax.rem(s, 2)
    scaling = 0.5 / float(NF) ** 1.5

    barrier = pltpu.get_barrier_semaphore()
    for i in range(2 * NSLAB):
        if i:
            to = {"grp": gat(0, i // NSLAB), "slab": lax.rem(s + i, NSLAB)}
            pl.semaphore_signal(barrier, inc=1, device_id=to, device_id_type=MESH)
    for i in range(4, 16):
        to = {"grp": gat(i // 4, i // 2 % 2), "slab": sat(0, i % 2, 0)}
        pl.semaphore_signal(barrier, inc=1, device_id=to, device_id_type=MESH)

    def four_rows(j, _):
        for k in range(2):
            p = j * 2 + k
            a = [in_ref[vg, :, :, pl.ds(p, 1)].reshape(4 * NF, 128) for vg in range(2)]
            both = jnp.dot(tab_ref[...], jnp.concatenate(a, 1), preferred_element_type=F32)
            for r in range(2):
                o = both[r * 128 : r * 128 + 128]
                o = ((o[0:64] + o[64:128]) * scaling).astype(BF)
                put = pl.ds(pl.multiple_of((p * 2 + r) * KB, KB), KB)
                xb[put, 0:256] = o[0:32]
                xb[put, 256:512] = o[32:64]
        return 0

    lax.fori_loop(0, NR // 4, four_rows, 0)
    wide[...] = jnp.dot(xb[...], order_ref[...], preferred_element_type=F32)

    def spread(j, _):
        base = pl.multiple_of(j * 96, 32)
        for kz in range(KB):
            part = wide[pl.ds(base, 96), (kz // 8) * 128 : (kz // 8 + 1) * 128]
            if kz % 8:
                part = pltpu.roll(part, 128 - 16 * (kz % 8), 1)
            box[pl.ds(pl.multiple_of(kz * NBOX + base, 8), 96), :] = part
        return 0

    lax.fori_loop(0, NBOX // 96, spread, 0)
    blk[CP : CP + 32, :] = jnp.zeros((32, 128), F32)
    for chunk in range(6):
        cab_ref[chunk * 256 + 128 : chunk * 256 + 192, :] = jnp.zeros((64, 2 * CP), BF)
    slot = lax.rem(lax.broadcasted_iota(jnp.int32, (16, CP), 0), 8)
    charge, gap = jnp.zeros((16, CP), F32), jnp.ones((16, CP), F32)
    for place, spot in enumerate([(0, 0), (0, 1), (-1, 0), (1, 0), (-1, 1), (1, 1), (2, 0), (2, 1)]):
        v = gat(*spot)
        charge = jnp.where(slot == place, oc_ref[v].astype(F32), charge)
        gap = jnp.where(slot == place, ve_ref[v] - ce_ref[s], gap)
    factor = (charge / (gap * math.sqrt(NV * NC)))[:, 0:1]
    pl.semaphore_wait(barrier, 43)

    lane = lax.broadcasted_iota(jnp.int32, (16, 128), 1)
    row = lax.broadcasted_iota(jnp.int32, (16, 128), 0)
    unit = jnp.where(lane == row, 1.0, 0.0).astype(BF)
    contract = (((1,), (1,)), ((), ()))

    def row_copy(h, b, z):
        to = {"grp": b, "slab": z * 8 + yc}
        dx = lax.rem(gx - b // 2 + 4, 4)
        return remote(rows.at[h, b], landed.at[h, dx, gz, sz], rsa.at[h, b, z], rra.at[h, dx, gz, sz], to)

    def row_in(h, b, z):
        to = {"grp": b, "slab": z * 8 + yc}
        dx, bz = lax.rem(b // 2 - gx + 4, 4), lax.rem(b, 2)
        return remote(rows.at[h, b], landed.at[h, dx, bz, z], rsa.at[h, b, z], rra.at[h, dx, bz, z], to)

    def row_keep(h):
        return pltpu.make_async_copy(rows.at[h, g], landed.at[h, 0, gz, sz], lsem.at[h])

    def col_copy(t, z):
        to = {"grp": gx * 2 + z, "slab": t}
        return remote(cols.at[t], cp.at[gx, gz, s], csa.at[t, z], cra.at[gz, s], to)

    def col_in(t, z):
        to = {"grp": gx * 2 + z, "slab": t}
        return remote(cols.at[t], cp.at[gx, z, t], csa.at[t, z], cra.at[z, t], to)

    def col_keep():
        return pltpu.make_async_copy(cols.at[s], cp.at[gx, gz, s], lsem.at[2])

    def one_block(h, i):
        b = lax.rem(g + yc // 2 + sz * 4 + i, NGRP)
        count, many = (CP, 64) if h == 0 else (CB, 50)
        origin = b * RB + h * CB

        def pick(j, _):
            base = j * many
            for k in range(many):
                blk[pl.ds(base + k, 1), :] = box[pl.ds(idx_ref[origin + base + k], 1), :]
            return 0

        lax.fori_loop(0, count // many, pick, 0)
        skip = h * (CP - CB)
        o = lax.dot_general(unit, blk[skip : skip + CP, :].astype(BF), contract, preferred_element_type=F32)
        rows[h, b] = (o * factor).astype(BF)
        o = lax.dot_general(unit, blk[0:CP, :].astype(BF), contract, preferred_element_type=F32)
        cols[2 * b + h] = o.astype(BF)
        for z in range(2):
            mine = jnp.logical_and(b == g, z == sz)

            @pl.when(mine)
            def _():
                row_keep(h).start()

            @pl.when(jnp.logical_not(mine))
            def _():
                row_copy(h, b, z).start()

            own = jnp.logical_and(2 * b + h == s, z == gz)

            @pl.when(own)
            def _():
                col_keep().start()

            @pl.when(jnp.logical_not(own))
            def _():
                col_copy(2 * b + h, z).start()

    for h in range(2):

        def block_step(i, _):
            one_block(h, i)
            return 0

        lax.fori_loop(0, NGRP, block_step, 0)

    def over_rows(act):
        def step(i, _):
            b, z = i // 2, lax.rem(i, 2)

            @pl.when(jnp.logical_not(jnp.logical_and(b == g, z == sz)))
            def _():
                act(b, z)

            return 0

        lax.fori_loop(0, 2 * NGRP, step, 0)

    def over_cols(act):
        def step(i, _):
            t, z = i // 2, lax.rem(i, 2)

            @pl.when(jnp.logical_not(jnp.logical_and(t == s, z == gz)))
            def _():
                act(t, z)

            return 0

        lax.fori_loop(0, 2 * NSLAB, step, 0)

    def row_part(dy, dc, half):
        return rp_ref.at[PLACE[dy], lax.rem(sc + dc, 2), pl.ds(half * 768, 768)]

    def row_hop(k, dy, half, to, land):
        there = dy - to if dy - to > -2 else 2
        return remote(
            row_part(dy, 0, half), row_part(there, 0, half), rs.at[k], rr.at[land], {"slab": sat(to, 0, 0)}
        )

    def row_wait(land, dy, half):
        part = row_part(dy, 0, half)
        remote(part, part, rs.at[0], rr.at[land], {"slab": sat(1, 0, 0)}).wait_recv()

    def side(k, dy, half, dc=0):
        part = row_part(dy, dc, half)
        return remote(part, part, sib_s.at[k], sib_r.at[k], {"slab": sat(0, 0, 1)})

    def col_part(dx, half):
        return cp.at[gat(dx, 0) // 2, half]

    def col_hop(k, dx, half, to, land):
        part = col_part(dx, half)
        return remote(part, part, cs.at[k], cr.at[land], {"grp": gat(to, 0)})

    def col_wait(land, dx, half):
        part = col_part(dx, half)
        remote(part, part, cs.at[0], cr.at[land], {"grp": gat(1, 0)}).wait_recv()

    hops = [(0, 0, 1, 0), (0, 1, -1, 3), (0, 1, 1, 1), (0, 0, -1, 2), (-1, 0, 1, 4), (1, 1, -1, 5)]
    arrivals = [(0, -1, 0), (2, 1, 0), (3, 1, 1), (1, -1, 1), (4, 2, 0), (5, 2, 1)]
    own_and_near = [(0, 0), (0, 1)] + [(dy, half) for _, dy, half in arrivals]
    row_hops = [row_hop(k, *hop) for k, hop in enumerate(hops)]
    col_hops = [col_hop(k, *hop) for k, hop in enumerate(hops)]
    sides = [side(0, 0, 0), side(1, 0, 1)] + [side(2 + k, dy, half) for k, (_, dy, half) in enumerate(arrivals)]

    def arrange(dx, half):
        x = gat(dx, 0) // 2
        for dy in (0, -1, 1, 2):
            for dc in range(2):
                chunk = PLACE[dy] * 2 + dc
                for z in range(2):
                    t = z * 8 + lax.rem(yc // 2 + dy + 4, 4) * 2 + dc
                    part = cp[x, half, pl.ds(t, 1)].reshape(16, CP)
                    value = part.astype(F32)
                    turned = jnp.concatenate([-value[8:16], value[0:8]], 0).astype(BF)
                    put = (dx % 4) * 64 + half * 32 + z * 16
                    if dy == 2:
                        to, put = right_ref, dc * 256 + put
                    elif dx == 2:
                        to, put = right_ref, 512 + chunk * 64 + half * 32 + z * 16
                    else:
                        to, put = cab_ref, chunk * 256 + put
                    to[put : put + 16, 0:CP] = part
                    to[put : put + 16, CP : 2 * CP] = turned

    def own_columns():
        col_keep().wait()
        over_cols(lambda t, z: col_in(t, z).wait_recv())
        for k in (0, 3, 1, 2):
            col_hops[k].start()

    for h in range(2):
        row_keep(h).wait()
        over_rows(lambda b, z: row_in(h, b, z).wait_recv())
        for j in range(CP // 128):
            part = landed[h, :, :, :, :, j * 128 : (j + 1) * 128].reshape(256, 128).astype(F32)
            rp_ref[0, sc, h * CP + j * 128 : h * CP + (j + 1) * 128, :] = part.T.astype(BF)
        for k in ((0, 3), (1, 2))[h]:
            row_hops[k].start()
        sides[h].start()

        @pl.when(sc == h)
        def _():
            own_columns()

    arrange(0, 0)
    arrange(0, 1)
    for k, (land, d, half) in enumerate(arrivals):
        row_wait(land, d, half)
        if k in (0, 2):
            row_hops[4 + k // 2].start()
        sides[2 + k].start()
        col_wait(land, d, half)
        if k in (0, 2):
            col_hops[4 + k // 2].start()
        arrange(d, half)
        if k == 3:
            for n in range(6):
                side(n, *own_and_near[n], 1).wait_recv()

            def near(m, _):
                put = pl.ds(pl.multiple_of(m * 256, 256), 256)
                parts = [rp_ref[p, c, put, :] for p in range(3) for c in range(2)]
                acc_ref[put, :] = jnp.dot(jnp.concatenate(parts, 1), cab_ref[...], preferred_element_type=F32)
                for pair in range(3):
                    both = [parts[2 * pair][:, 128:192], parts[2 * pair + 1][:, 128:192]]
                    left_ref[put, 512 + pair * 128 : 640 + pair * 128] = jnp.concatenate(both, 1)
                return 0

            lax.fori_loop(0, RP // 256, near, 0)
    for n in range(6, 8):
        side(n, *own_and_near[n], 1).wait_recv()
    for c in range(2):
        left_ref[:, c * 256 : c * 256 + 256] = rp_ref[3, c]
    for h in range(2):
        over_rows(lambda b, z: row_copy(h, b, z).wait_send())
    over_cols(lambda t, z: col_copy(t, z).wait_send())
    for copy in row_hops + col_hops + sides:
        copy.wait_send()


PLACE = {0: 0, -1: 1, 1: 2, 2: 3}


def panels_call(index, planes, valence_energy, conduction_energy, occupation):
    smem = pl.BlockSpec(memory_space=pltpu.SMEM)
    vmem = pl.BlockSpec(memory_space=pltpu.VMEM)
    dma = pltpu.SemaphoreType.DMA
    return pl.pallas_call(
        panels_kernel,
        name="panels",
        out_shape=(
            jax.ShapeDtypeStruct((RP, 2 * CP), F32),
            jax.ShapeDtypeStruct((RP, 896), BF),
            jax.ShapeDtypeStruct((896, 2 * CP), BF),
        ),
        in_specs=[smem, smem, smem, smem, vmem, vmem, vmem],
        out_specs=(vmem, vmem, vmem),
        scratch_shapes=[
            pltpu.VMEM((4, 2, RP, 256), BF),
            pltpu.VMEM((1536, 2 * CP), BF),
            pltpu.VMEM((NBOX, 512), BF),
            pltpu.VMEM((NBOX, 512), F32),
            pltpu.VMEM((KB * NBOX, 128), F32),
            pltpu.VMEM((CP + 32, 128), F32),
            pltpu.VMEM((2, NGRP, 16, CP), BF),
            pltpu.VMEM((NSLAB, 16, CP), BF),
            pltpu.VMEM((2, 4, 2, 2, 16, CP), BF),
            pltpu.VMEM((4, 2, NSLAB, 16, CP), BF),
            dma((2, NGRP, 2)),
            dma((2, 4, 2, 2)),
            dma((NSLAB, 2)),
            dma((2, NSLAB)),
            dma((6,)),
            dma((6,)),
            dma((6,)),
            dma((6,)),
            dma((8,)),
            dma((8,)),
            dma((3,)),
        ],
        compiler_params=pltpu.CompilerParams(
            collective_id=1, has_side_effects=True, vmem_limit_bytes=34 * 1024 * 1024
        ),
    )(
        index,
        valence_energy,
        conduction_energy,
        occupation,
        planes,
        jnp.asarray(box_weights()),
        jnp.asarray(lane_order()),
    )


def tile_kernel(acc_ref, left_ref, right_ref, out_ref):
    rows = pl.ds(pl.multiple_of(pl.program_id(0) * 256, 256), 256)
    o = jnp.dot(left_ref[rows, :], right_ref[...], preferred_element_type=F32) + acc_ref[rows, :]
    out_ref[:, 0, :] = o[:, 0:CB]
    out_ref[:, 1, :] = o[:, CP : CP + CB]


def tile_call(near, left, right):
    rows = 256
    tiles = pl.pallas_call(
        tile_kernel,
        name="tile",
        grid=(RP // rows,),
        out_shape=jax.ShapeDtypeStruct((RB, 2, CB), F32),
        in_specs=[
            pl.BlockSpec((RP, 2 * CP), lambda i: (0, 0)),
            pl.BlockSpec((RP, 896), lambda i: (0, 0)),
            pl.BlockSpec((896, 2 * CP), lambda i: (0, 0)),
        ],
        out_specs=pl.BlockSpec((rows, 2, CB), lambda i: (i, 0, 0)),
        compiler_params=pltpu.CompilerParams(vmem_limit_bytes=32 * 1024 * 1024),
    )(near, left, right)
    return jnp.transpose(tiles, (1, 0, 2))


def table_look_up(index, table):
    found = jnp.zeros_like(index)
    for place, value in enumerate(table):
        found = jnp.where(index == place, int(value), found)
    return found


def on_device(
    valence_waves, conduction_waves, valence_energy, conduction_energy, occupation, gvec_ids
):
    row, shifted = row_tables()
    along_x = gvec_ids // (KB * KB)
    along_y = gvec_ids // KB % KB
    along_z = gvec_ids % KB
    place = table_look_up(along_y, row * KB + shifted * 1024 * KB)
    index = (along_z ^ (place // (1024 * KB))) * NBOX + place % (1024 * KB) + along_x

    planes = planes_call(valence_waves, conduction_waves)
    near, left, right = panels_call(index, planes, valence_energy, conduction_energy, occupation)
    return tile_call(near, left, right)


def solution(mesh):
    in_specs = (P("grp", "slab", None, None), P("grp", "slab", None, None), P(), P("grp"), P(), P())
    out_specs = P(None, "grp", "slab")
    return jax.shard_map(
        on_device, mesh=mesh, in_specs=in_specs, out_specs=out_specs, check_vma=False
    )
```

```python
import functools
import math

import jax
import jax.numpy as jnp
import ml_dtypes
import numpy as np
from jax import lax
from jax.experimental import pallas as pl
from jax.experimental.pallas import tpu as pltpu
from jax.sharding import PartitionSpec as P

NV = 8
NC = 128
NF = 128
KB = 32
NG = 12000
NGRP = 8
NSLAB = 16
NX = NF // NSLAB
HX = NX // 2
NR = 24
RB = NG // NGRP
CB = NG // NSLAB
RP = 1536
CP = 768
NBOX = NR * KB
MESH = pl.DeviceIdType.MESH
BF = jnp.bfloat16
F32 = jnp.float32

WIDE = [9, -9, 11, -11, 5, -5]
NARROW = [13, -13, 12, -12, 14, -14]
SINGLE = [0, 1, -1, 2, -2, 3, -3, 4, -4, 6, -6, 7, -7, 8, -8, 10, -10]
ROW_FREQ = SINGLE[:16] + [SINGLE[16]] + WIDE + [15] + [15] + NARROW + [15]


def freq(j):
    return j - KB if j >= KB // 2 else j


def row_tables():
    row = np.zeros(KB, np.int32)
    shifted = np.zeros(KB, np.int32)
    for place, f in enumerate(ROW_FREQ[:NR]):
        if f != 15:
            row[f % KB] = place
    for place, f in enumerate(NARROW):
        row[f % KB] = 17 + place
        shifted[f % KB] = KB // 2
    return row, shifted


def phases(positions, freqs):
    angle = np.mod(np.outer(positions, freqs), NF).astype(np.float32) * np.float32(2.0 * math.pi / NF)
    return np.cos(angle).astype(np.float32), np.sin(angle).astype(np.float32)


def depth_weights():
    cos, sin = phases(np.arange(NF), [freq(j) for j in range(KB)])
    w = np.zeros((4, 2, NF, 2, KB, 4), np.float32)
    for vl in range(4):
        w[vl, 0, :, 0, :, vl] = cos
        w[vl, 1, :, 0, :, vl] = sin
        w[vl, 0, :, 1, :, vl] = -sin
        w[vl, 1, :, 1, :, vl] = cos
    return w.reshape(8 * NF, 8 * KB).astype(ml_dtypes.bfloat16)


def height_weights():
    cos, sin = phases(np.arange(NF), ROW_FREQ)
    return np.concatenate([cos.T, sin.T], 0).astype(ml_dtypes.bfloat16)


def wide_mask():
    mask = np.ones((8, KB, 4), np.float32)
    for place, f in enumerate(WIDE):
        half = math.isqrt(196 - f * f)
        for j in range(KB):
            if abs(freq(j)) > half:
                mask[1 + place, j] = 0.0
    return mask.reshape(8, 4 * KB)


def box_weights():
    cos, sin = phases(np.arange(NF), [freq(j) for j in range(KB)])
    cos = cos.T.reshape(KB, NSLAB, 2, HX).transpose(0, 2, 1, 3)
    sin = sin.T.reshape(KB, NSLAB, 2, HX).transpose(0, 2, 1, 3)
    t = np.zeros((2, KB, 2, NSLAB, 2, HX), np.float32)
    t[0, :, :, :, 0] = cos
    t[0, :, :, :, 1] = sin
    t[1, :, :, :, 0] = -sin
    t[1, :, :, :, 1] = cos
    high = t.astype(ml_dtypes.bfloat16)
    low = (t - high.astype(np.float32)).astype(ml_dtypes.bfloat16)
    pair = np.zeros((2, 2, 2, KB, 2, NSLAB, 2, 2, HX), ml_dtypes.bfloat16)
    for r in range(2):
        pair[r, 0, :, :, :, :, r] = high
        pair[r, 1, :, :, :, :, r] = low
    return pair.reshape(8 * KB, 4 * NF)


def lane_order():
    m = np.zeros((2, 2, KB, 4, KB, 2, 2, 4), np.float32)
    for reim in range(2):
        for vg in range(2):
            for kz in range(KB):
                for vl in range(4):
                    m[reim, vg, kz, vl, kz, reim, vg, vl] = 1.0
    return m.reshape(512, 512).astype(ml_dtypes.bfloat16)


def place_in_groups():
    g = lax.axis_index("grp")
    gx, gz = g // 2, lax.rem(g, 2)

    def at(dx, dz):
        return lax.rem(gx + dx + 4, 4) * 2 + (lax.rem(gz + dz, 2))

    return g, at


def place_in_slabs():
    s = lax.axis_index("slab")
    sz, sy, sc = s // 8, lax.rem(s // 2, 4), lax.rem(s, 2)

    def at(dy, dz, dc):
        return lax.rem(sz + dz, 2) * 8 + lax.rem(sy + dy + 4, 4) * 2 + lax.rem(sc + dc, 2)

    return s, at


def enter(groups, slabs):
    barrier = pltpu.get_barrier_semaphore()
    for one in groups:
        pl.semaphore_signal(barrier, inc=1, device_id={"grp": one}, device_id_type=MESH)
    for one in slabs:
        pl.semaphore_signal(barrier, inc=1, device_id={"slab": one}, device_id_type=MESH)
    pl.semaphore_wait(barrier, len(groups) + len(slabs))


def remote(src, dst, send, recv, device):
    return pltpu.make_async_remote_copy(
        src_ref=src, dst_ref=dst, send_sem=send, recv_sem=recv, device_id=device, device_id_type=MESH
    )


def planes_kernel(
    val_ref, con_ref, wz_ref, ty_ref, mask_ref, out_ref, val, con, msg, wz, even, odd, first_even, first_odd, scr, con_sem, own_sem, wz_sem, vs, vr, ms, mr, local_sem
):
    g, gat = place_in_groups()
    s, sat = place_in_slabs()
    own = pltpu.make_async_copy(val_ref.at[0], val.at[0], own_sem)
    own.start()
    weights = pltpu.make_async_copy(wz_ref, wz, wz_sem)
    weights.start()

    def band(i):
        k = lax.rem(i + 16, 16) // 2
        step = lax.rem(k + 1, 4)
        step = step + lax.rem(s, 2) * (4 - 2 * step)
        return sat(lax.rem(step, 4), lax.rem(i + 17, 2), 1 - k // 4)

    def con_copy(c):
        return pltpu.make_async_copy(con_ref.at[c], con.at[c], con_sem.at[c])

    def start_con(i, _):
        con_copy(band(i)).start()
        return 0

    lax.fori_loop(0, NSLAB, start_con, 0)
    partner, ahead, behind = gat(0, 1), gat(1, 0), gat(-1, 0)
    enter([partner, ahead, behind], [lax.rem(s + i, NSLAB) for i in range(1, NSLAB)])
    own.wait()

    def hop(k, slot, to, landing):
        return [
            remote(
                val.at[slot, pl.ds(half * HX, HX)],
                val.at[landing, pl.ds(half * HX, HX)],
                vs.at[k, half],
                vr.at[landing, half],
                {"grp": to},
            )
            for half in range(2)
        ]

    to_partner, to_ahead, to_behind = hop(0, 0, partner, 1), hop(1, 0, ahead, 2), hop(2, 0, behind, 3)
    p_ahead, p_behind = hop(3, 1, ahead, 4), hop(4, 1, behind, 5)
    l_ahead, r_behind = hop(5, 2, ahead, 6), hop(6, 5, behind, 7)
    for half in range(2):
        to_ahead[half].start()
        to_behind[half].start()
        to_partner[half].start()
    weights.wait()

    def message(vg, half, c):
        return remote(
            msg.at[vg, half, c], out_ref.at[vg, half, s], ms.at[vg, half, c], mr.at[vg, half, s], {"slab": c}
        )

    def arrival(vg, half, src):
        return remote(
            msg.at[vg, half, src],
            out_ref.at[vg, half, src],
            ms.at[vg, half, src],
            mr.at[vg, half, src],
            {"slab": src},
        )

    def kept(vg, half):
        return pltpu.make_async_copy(msg.at[vg, half, s], out_ref.at[vg, half, s], local_sem.at[vg, half])

    def density(vg, half, c, buf, x):
        for y0 in range(0, NF, 32):
            rows = pl.ds(y0, 32)
            put = pl.ds(x * NF + y0, 32)
            cr = con[c, half * HX + x, rows, 0:NF]
            ci = con[c, half * HX + x, rows, NF : 2 * NF]
            for vl in range(4):
                pr = val[vg * 4 + vl, half * HX + x, rows, 0:NF]
                pi = val[vg * 4 + vl, half * HX + x, rows, NF : 2 * NF]
                buf[put, vl * 256 : vl * 256 + NF] = pr * cr + pi * ci
                buf[put, vl * 256 + NF : vl * 256 + 256] = pr * ci - pi * cr

    def along_z(part, buf, first):
        rows = pl.ds(part * HX * NF // 2, HX * NF // 2)
        first[rows, :] = jnp.dot(buf[rows, :], wz[...], preferred_element_type=F32).astype(BF)

    def along_y(x, first):
        o = jnp.dot(ty_ref[...], first[x * NF : x * NF + NF, :], preferred_element_type=F32)
        keep = mask_ref[...] > 0.5
        for reim in range(2):
            if reim == 0:
                full = o[0:32, 0:128] + o[32:64, 128:256]
            else:
                full = o[0:32, 128:256] - o[32:64, 0:128]
            merged = jnp.where(keep, full[16:24], pltpu.roll(full[24:32], 64, 1))
            base = (reim * HX + x) * NR
            scr[base : base + 16, :] = full[0:16]
            scr[base + 16 : base + 24, :] = merged

    def pack(vg, half, c):
        for r in range(0, NR, 2):
            both = jnp.concatenate(
                [scr[pl.ds(r, 2 * HX, stride=NR), :], scr[pl.ds(r + 1, 2 * HX, stride=NR), :]], 0
            )
            msg[vg, half, c, r // 2] = both.astype(BF)

    def one_band(vg, half, before, after, buf, other, first, last):
        along_z(0, buf, first)
        density(vg, half, after, other, 0)
        density(vg, half, after, other, 1)
        along_y(0, last)
        along_y(1, last)
        along_z(1, buf, first)
        density(vg, half, after, other, 2)
        density(vg, half, after, other, 3)
        along_y(2, last)
        along_y(3, last)
        pack(vg, half, before)

    for phase in range(4):
        vg, half = phase // 2, phase % 2
        if phase == 0:
            for copies in (to_partner, to_ahead, to_behind):
                copies[0].wait_recv()
            p_behind[0].start()
            p_ahead[0].start()
            l_ahead[0].start()
        if phase == 1:
            for copies in (to_partner, to_ahead, to_behind):
                copies[1].wait_recv()
            p_ahead[1].start()
            p_behind[0].wait_recv()
            r_behind[0].start()
            p_behind[1].start()
            l_ahead[1].start()
        if phase >= 2:
            for copies in (p_ahead, l_ahead, r_behind):
                copies[half].wait_recv()
        start = band(0)
        if phase == 0:
            con_copy(start).wait()
        for x in range(HX):
            density(vg, half, start, even, x)

        def two_bands(j, _):
            before, c0, c1, c2 = band(2 * j - 1), band(2 * j), band(2 * j + 1), band(2 * j + 2)
            if phase == 0:
                con_copy(c1).wait()

                @pl.when(j < NSLAB // 2 - 1)
                def _():
                    con_copy(c2).wait()

            if phase == 2:

                @pl.when(j == 2)
                def _():
                    p_behind[1].wait_recv()
                    r_behind[1].start()

            one_band(vg, half, before, c1, even, odd, first_even, first_odd)

            @pl.when(j > 0)
            def _():
                message(vg, half, before).start()

            one_band(vg, half, c0, c2, odd, even, first_odd, first_even)
            message(vg, half, c0).start()
            return 0

        lax.fori_loop(0, NSLAB // 2, two_bands, 0)
        for x in range(HX):
            along_y(x, first_odd)
        pack(vg, half, s)
        kept(vg, half).start()

    def finish(i, _):
        other = lax.rem(s + i + 1, NSLAB)
        for vg in range(2):
            for half in range(2):
                arrival(vg, half, other).wait_recv()
                message(vg, half, other).wait_send()
        return 0

    lax.fori_loop(0, NSLAB - 1, finish, 0)
    for vg in range(2):
        for half in range(2):
            kept(vg, half).wait()
    for copies in (to_partner, to_ahead, to_behind, p_ahead, p_behind, l_ahead, r_behind):
        for half in range(2):
            copies[half].wait_send()


def planes_call(valence, conduction):
    anywhere = pl.BlockSpec(memory_space=pl.ANY)
    vmem = pl.BlockSpec(memory_space=pltpu.VMEM)
    return pl.pallas_call(
        planes_kernel,
        name="planes",
        out_shape=jax.ShapeDtypeStruct((2, 2, NSLAB, NR // 2, 16, 128), BF),
        in_specs=[anywhere, anywhere, anywhere, vmem, vmem],
        out_specs=vmem,
        scratch_shapes=[
            pltpu.VMEM((8, NX, NF, 2 * NF), BF),
            pltpu.VMEM((NSLAB, NX, NF, 2 * NF), BF),
            pltpu.VMEM((2, 2, NSLAB, NR // 2, 16, 128), BF),
            pltpu.VMEM((8 * NF, 2 * NF), BF),
            pltpu.VMEM((HX * NF, 8 * NF), BF),
            pltpu.VMEM((HX * NF, 8 * NF), BF),
            pltpu.VMEM((HX * NF, 2 * NF), BF),
            pltpu.VMEM((HX * NF, 2 * NF), BF),
            pltpu.VMEM((2 * HX * NR, 128), F32),
            pltpu.SemaphoreType.DMA((NSLAB,)),
            pltpu.SemaphoreType.DMA,
            pltpu.SemaphoreType.DMA,
            pltpu.SemaphoreType.DMA((7, 2)),
            pltpu.SemaphoreType.DMA((8, 2)),
            pltpu.SemaphoreType.DMA((2, 2, NSLAB)),
            pltpu.SemaphoreType.DMA((2, 2, NSLAB)),
            pltpu.SemaphoreType.DMA((2, 2)),
        ],
        compiler_params=pltpu.CompilerParams(
            collective_id=0, has_side_effects=True, vmem_limit_bytes=56 * 1024 * 1024
        ),
    )(
        valence,
        conduction,
        jnp.asarray(depth_weights()),
        jnp.asarray(height_weights()),
        jnp.asarray(wide_mask()),
    )


def panels_kernel(
    idx_ref, ve_ref, ce_ref, oc_ref, in_ref, tab_ref, order_ref, acc_ref, left_ref, right_ref,
    rp_ref, cab_ref, xb, wide, box, blk, rows, cols, landed, cp,
    rsa, rra, csa, cra, rs, rr, cs, cr, sib_s, sib_r, lsem,
):
    g, gat = place_in_groups()
    s, sat = place_in_slabs()
    gx, gz = g // 2, lax.rem(g, 2)
    sz, yc, sc = s // 8, lax.rem(s, 8), lax.rem(s, 2)
    scaling = 0.5 / float(NF) ** 1.5

    barrier = pltpu.get_barrier_semaphore()
    for i in range(2 * NSLAB):
        if i:
            to = {"grp": gat(0, i // NSLAB), "slab": lax.rem(s + i, NSLAB)}
            pl.semaphore_signal(barrier, inc=1, device_id=to, device_id_type=MESH)
    for i in range(4, 16):
        to = {"grp": gat(i // 4, i // 2 % 2), "slab": sat(0, i % 2, 0)}
        pl.semaphore_signal(barrier, inc=1, device_id=to, device_id_type=MESH)

    def four_rows(j, _):
        for k in range(2):
            p = j * 2 + k
            a = [in_ref[vg, :, :, pl.ds(p, 1)].reshape(4 * NF, 128) for vg in range(2)]
            both = jnp.dot(tab_ref[...], jnp.concatenate(a, 1), preferred_element_type=F32)
            for r in range(2):
                o = both[r * 128 : r * 128 + 128]
                o = ((o[0:64] + o[64:128]) * scaling).astype(BF)
                put = pl.ds(pl.multiple_of((p * 2 + r) * KB, KB), KB)
                xb[put, 0:256] = o[0:32]
                xb[put, 256:512] = o[32:64]
        return 0

    lax.fori_loop(0, NR // 4, four_rows, 0)
    wide[...] = jnp.dot(xb[...], order_ref[...], preferred_element_type=F32)

    def spread(j, _):
        base = pl.multiple_of(j * 96, 32)
        for kz in range(KB):
            part = wide[pl.ds(base, 96), (kz // 8) * 128 : (kz // 8 + 1) * 128]
            if kz % 8:
                part = pltpu.roll(part, 128 - 16 * (kz % 8), 1)
            box[pl.ds(pl.multiple_of(kz * NBOX + base, 8), 96), :] = part
        return 0

    lax.fori_loop(0, NBOX // 96, spread, 0)
    blk[CP : CP + 32, :] = jnp.zeros((32, 128), F32)
    for chunk in range(6):
        cab_ref[chunk * 256 + 128 : chunk * 256 + 192, :] = jnp.zeros((64, 2 * CP), BF)
    slot = lax.rem(lax.broadcasted_iota(jnp.int32, (16, CP), 0), 8)
    charge, gap = jnp.zeros((16, CP), F32), jnp.ones((16, CP), F32)
    for place, spot in enumerate([(0, 0), (0, 1), (-1, 0), (1, 0), (-1, 1), (1, 1), (2, 0), (2, 1)]):
        v = gat(*spot)
        charge = jnp.where(slot == place, oc_ref[v].astype(F32), charge)
        gap = jnp.where(slot == place, ve_ref[v] - ce_ref[s], gap)
    factor = (charge / (gap * math.sqrt(NV * NC)))[:, 0:1]
    pl.semaphore_wait(barrier, 43)

    lane = lax.broadcasted_iota(jnp.int32, (16, 128), 1)
    row = lax.broadcasted_iota(jnp.int32, (16, 128), 0)
    unit = jnp.where(lane == row, 1.0, 0.0).astype(BF)
    contract = (((1,), (1,)), ((), ()))

    def row_copy(h, b, z):
        to = {"grp": b, "slab": z * 8 + yc}
        dx = lax.rem(gx - b // 2 + 4, 4)
        return remote(rows.at[h, b], landed.at[h, dx, gz, sz], rsa.at[h, b, z], rra.at[h, dx, gz, sz], to)

    def row_in(h, b, z):
        to = {"grp": b, "slab": z * 8 + yc}
        dx, bz = lax.rem(b // 2 - gx + 4, 4), lax.rem(b, 2)
        return remote(rows.at[h, b], landed.at[h, dx, bz, z], rsa.at[h, b, z], rra.at[h, dx, bz, z], to)

    def row_keep(h):
        return pltpu.make_async_copy(rows.at[h, g], landed.at[h, 0, gz, sz], lsem.at[h])

    def col_copy(t, z):
        to = {"grp": gx * 2 + z, "slab": t}
        return remote(cols.at[t], cp.at[gx, gz, s], csa.at[t, z], cra.at[gz, s], to)

    def col_in(t, z):
        to = {"grp": gx * 2 + z, "slab": t}
        return remote(cols.at[t], cp.at[gx, z, t], csa.at[t, z], cra.at[z, t], to)

    def col_keep():
        return pltpu.make_async_copy(cols.at[s], cp.at[gx, gz, s], lsem.at[2])

    def one_block(h, i):
        b = lax.rem(g + yc // 2 + sz * 4 + i, NGRP)
        count, many = (CP, 64) if h == 0 else (CB, 50)
        origin = b * RB + h * CB

        def pick(j, _):
            base = j * many
            for k in range(many):
                blk[pl.ds(base + k, 1), :] = box[pl.ds(idx_ref[origin + base + k], 1), :]
            return 0

        lax.fori_loop(0, count // many, pick, 0)
        skip = h * (CP - CB)
        o = lax.dot_general(unit, blk[skip : skip + CP, :].astype(BF), contract, preferred_element_type=F32)
        rows[h, b] = (o * factor).astype(BF)
        o = lax.dot_general(unit, blk[0:CP, :].astype(BF), contract, preferred_element_type=F32)
        cols[2 * b + h] = o.astype(BF)
        for z in range(2):
            mine = jnp.logical_and(b == g, z == sz)

            @pl.when(mine)
            def _():
                row_keep(h).start()

            @pl.when(jnp.logical_not(mine))
            def _():
                row_copy(h, b, z).start()

            own = jnp.logical_and(2 * b + h == s, z == gz)

            @pl.when(own)
            def _():
                col_keep().start()

            @pl.when(jnp.logical_not(own))
            def _():
                col_copy(2 * b + h, z).start()

    for h in range(2):

        def block_step(i, _):
            one_block(h, i)
            return 0

        lax.fori_loop(0, NGRP, block_step, 0)

    def over_rows(act):
        def step(i, _):
            b, z = i // 2, lax.rem(i, 2)

            @pl.when(jnp.logical_not(jnp.logical_and(b == g, z == sz)))
            def _():
                act(b, z)

            return 0

        lax.fori_loop(0, 2 * NGRP, step, 0)

    def over_cols(act):
        def step(i, _):
            t, z = i // 2, lax.rem(i, 2)

            @pl.when(jnp.logical_not(jnp.logical_and(t == s, z == gz)))
            def _():
                act(t, z)

            return 0

        lax.fori_loop(0, 2 * NSLAB, step, 0)

    def row_part(dy, dc, half):
        return rp_ref.at[PLACE[dy], lax.rem(sc + dc, 2), pl.ds(half * 768, 768)]

    def row_hop(k, dy, half, to, land):
        there = dy - to if dy - to > -2 else 2
        return remote(
            row_part(dy, 0, half), row_part(there, 0, half), rs.at[k], rr.at[land], {"slab": sat(to, 0, 0)}
        )

    def row_wait(land, dy, half):
        part = row_part(dy, 0, half)
        remote(part, part, rs.at[0], rr.at[land], {"slab": sat(1, 0, 0)}).wait_recv()

    def side(k, dy, half, dc=0):
        part = row_part(dy, dc, half)
        return remote(part, part, sib_s.at[k], sib_r.at[k], {"slab": sat(0, 0, 1)})

    def col_part(dx, half):
        return cp.at[gat(dx, 0) // 2, half]

    def col_hop(k, dx, half, to, land):
        part = col_part(dx, half)
        return remote(part, part, cs.at[k], cr.at[land], {"grp": gat(to, 0)})

    def col_wait(land, dx, half):
        part = col_part(dx, half)
        remote(part, part, cs.at[0], cr.at[land], {"grp": gat(1, 0)}).wait_recv()

    hops = [(0, 0, 1, 0), (0, 1, -1, 3), (0, 1, 1, 1), (0, 0, -1, 2), (-1, 0, 1, 4), (1, 1, -1, 5)]
    arrivals = [(0, -1, 0), (2, 1, 0), (3, 1, 1), (1, -1, 1), (4, 2, 0), (5, 2, 1)]
    own_and_near = [(0, 0), (0, 1)] + [(dy, half) for _, dy, half in arrivals]
    row_hops = [row_hop(k, *hop) for k, hop in enumerate(hops)]
    col_hops = [col_hop(k, *hop) for k, hop in enumerate(hops)]
    sides = [side(0, 0, 0), side(1, 0, 1)] + [side(2 + k, dy, half) for k, (_, dy, half) in enumerate(arrivals)]

    def arrange(dx, half):
        x = gat(dx, 0) // 2
        for dy in (0, -1, 1, 2):
            for dc in range(2):
                chunk = PLACE[dy] * 2 + dc
                for z in range(2):
                    t = z * 8 + lax.rem(yc // 2 + dy + 4, 4) * 2 + dc
                    part = cp[x, half, pl.ds(t, 1)].reshape(16, CP)
                    value = part.astype(F32)
                    turned = jnp.concatenate([-value[8:16], value[0:8]], 0).astype(BF)
                    put = (dx % 4) * 64 + half * 32 + z * 16
                    if dy == 2:
                        to, put = right_ref, dc * 256 + put
                    elif dx == 2:
                        to, put = right_ref, 512 + chunk * 64 + half * 32 + z * 16
                    else:
                        to, put = cab_ref, chunk * 256 + put
                    to[put : put + 16, 0:CP] = part
                    to[put : put + 16, CP : 2 * CP] = turned

    def own_columns():
        col_keep().wait()
        over_cols(lambda t, z: col_in(t, z).wait_recv())
        for k in (0, 3, 1, 2):
            col_hops[k].start()

    for h in range(2):
        row_keep(h).wait()
        over_rows(lambda b, z: row_in(h, b, z).wait_recv())
        for j in range(CP // 128):
            part = landed[h, :, :, :, :, j * 128 : (j + 1) * 128].reshape(256, 128).astype(F32)
            rp_ref[0, sc, h * CP + j * 128 : h * CP + (j + 1) * 128, :] = part.T.astype(BF)
        for k in ((0, 3), (1, 2))[h]:
            row_hops[k].start()
        sides[h].start()

        @pl.when(sc == h)
        def _():
            own_columns()

    arrange(0, 0)
    arrange(0, 1)
    def take(k):
        land, d, half = arrivals[k]
        row_wait(land, d, half)
        if k in (0, 2):
            row_hops[4 + k // 2].start()
        sides[2 + k].start()
        col_wait(land, d, half)
        if k in (0, 2):
            col_hops[4 + k // 2].start()
        arrange(d, half)

    for k in (0, 1, 2, 3, 5):
        take(k)
        if k == 3:
            for n in range(6):
                side(n, *own_and_near[n], 1).wait_recv()

            def near(m, _):
                put = pl.ds(pl.multiple_of(m * 256, 256), 256)
                parts = [rp_ref[p, c, put, :] for p in range(3) for c in range(2)]
                acc_ref[put, :] = jnp.dot(jnp.concatenate(parts, 1), cab_ref[...], preferred_element_type=F32)
                for pair in range(3):
                    both = [parts[2 * pair][:, 128:192], parts[2 * pair + 1][:, 128:192]]
                    left_ref[put, 512 + pair * 128 : 640 + pair * 128] = jnp.concatenate(both, 1)
                return 0

            lax.fori_loop(0, RP // 512, near, 0)
            take(4)
            lax.fori_loop(RP // 512, RP // 256, near, 0)
    for n in range(6, 8):
        side(n, *own_and_near[n], 1).wait_recv()
    for c in range(2):
        left_ref[:, c * 256 : c * 256 + 256] = rp_ref[3, c]
    for h in range(2):
        over_rows(lambda b, z: row_copy(h, b, z).wait_send())
    over_cols(lambda t, z: col_copy(t, z).wait_send())
    for copy in row_hops + col_hops + sides:
        copy.wait_send()


PLACE = {0: 0, -1: 1, 1: 2, 2: 3}


def panels_call(index, planes, valence_energy, conduction_energy, occupation):
    smem = pl.BlockSpec(memory_space=pltpu.SMEM)
    vmem = pl.BlockSpec(memory_space=pltpu.VMEM)
    dma = pltpu.SemaphoreType.DMA
    return pl.pallas_call(
        panels_kernel,
        name="panels",
        out_shape=(
            jax.ShapeDtypeStruct((RP, 2 * CP), F32),
            jax.ShapeDtypeStruct((RP, 896), BF),
            jax.ShapeDtypeStruct((896, 2 * CP), BF),
        ),
        in_specs=[smem, smem, smem, smem, vmem, vmem, vmem],
        out_specs=(vmem, vmem, vmem),
        scratch_shapes=[
            pltpu.VMEM((4, 2, RP, 256), BF),
            pltpu.VMEM((1536, 2 * CP), BF),
            pltpu.VMEM((NBOX, 512), BF),
            pltpu.VMEM((NBOX, 512), F32),
            pltpu.VMEM((KB * NBOX, 128), F32),
            pltpu.VMEM((CP + 32, 128), F32),
            pltpu.VMEM((2, NGRP, 16, CP), BF),
            pltpu.VMEM((NSLAB, 16, CP), BF),
            pltpu.VMEM((2, 4, 2, 2, 16, CP), BF),
            pltpu.VMEM((4, 2, NSLAB, 16, CP), BF),
            dma((2, NGRP, 2)),
            dma((2, 4, 2, 2)),
            dma((NSLAB, 2)),
            dma((2, NSLAB)),
            dma((6,)),
            dma((6,)),
            dma((6,)),
            dma((6,)),
            dma((8,)),
            dma((8,)),
            dma((3,)),
        ],
        compiler_params=pltpu.CompilerParams(
            collective_id=1, has_side_effects=True, vmem_limit_bytes=34 * 1024 * 1024
        ),
    )(
        index,
        valence_energy,
        conduction_energy,
        occupation,
        planes,
        jnp.asarray(box_weights()),
        jnp.asarray(lane_order()),
    )


def tile_kernel(acc_ref, left_ref, right_ref, out_ref):
    rows = pl.ds(pl.multiple_of(pl.program_id(0) * 256, 256), 256)
    o = jnp.dot(left_ref[rows, :], right_ref[...], preferred_element_type=F32) + acc_ref[rows, :]
    out_ref[:, 0, :] = o[:, 0:CB]
    out_ref[:, 1, :] = o[:, CP : CP + CB]


def tile_call(near, left, right):
    rows = 256
    tiles = pl.pallas_call(
        tile_kernel,
        name="tile",
        grid=(RP // rows,),
        out_shape=jax.ShapeDtypeStruct((RB, 2, CB), F32),
        in_specs=[
            pl.BlockSpec((RP, 2 * CP), lambda i: (0, 0)),
            pl.BlockSpec((RP, 896), lambda i: (0, 0)),
            pl.BlockSpec((896, 2 * CP), lambda i: (0, 0)),
        ],
        out_specs=pl.BlockSpec((rows, 2, CB), lambda i: (i, 0, 0)),
        compiler_params=pltpu.CompilerParams(vmem_limit_bytes=32 * 1024 * 1024),
    )(near, left, right)
    return jnp.transpose(tiles, (1, 0, 2))


def table_look_up(index, table):
    found = jnp.zeros_like(index)
    for place, value in enumerate(table):
        found = jnp.where(index == place, int(value), found)
    return found


def on_device(
    valence_waves, conduction_waves, valence_energy, conduction_energy, occupation, gvec_ids
):
    row, shifted = row_tables()
    along_x = gvec_ids // (KB * KB)
    along_y = gvec_ids // KB % KB
    along_z = gvec_ids % KB
    place = table_look_up(along_y, row * KB + shifted * 1024 * KB)
    index = (along_z ^ (place // (1024 * KB))) * NBOX + place % (1024 * KB) + along_x

    planes = planes_call(valence_waves, conduction_waves)
    near, left, right = panels_call(index, planes, valence_energy, conduction_energy, occupation)
    return tile_call(near, left, right)


def solution(mesh):
    in_specs = (P("grp", "slab", None, None), P("grp", "slab", None, None), P(), P("grp"), P(), P())
    out_specs = P(None, "grp", "slab")
    return jax.shard_map(
        on_device, mesh=mesh, in_specs=in_specs, out_specs=out_specs, check_vma=False
    )
```

```python
import functools
import math

import jax
import jax.numpy as jnp
import ml_dtypes
import numpy as np
from jax import lax
from jax.experimental import pallas as pl
from jax.experimental.pallas import tpu as pltpu
from jax.sharding import PartitionSpec as P

NV = 8
NC = 128
NF = 128
KB = 32
NG = 12000
NGRP = 8
NSLAB = 16
NX = NF // NSLAB
HX = NX // 2
NR = 24
RB = NG // NGRP
CB = NG // NSLAB
RP = 1536
CP = 768
NBOX = NR * KB
MESH = pl.DeviceIdType.MESH
BF = jnp.bfloat16
F32 = jnp.float32

WIDE = [9, -9, 11, -11, 5, -5]
NARROW = [13, -13, 12, -12, 14, -14]
SINGLE = [0, 1, -1, 2, -2, 3, -3, 4, -4, 6, -6, 7, -7, 8, -8, 10, -10]
ROW_FREQ = SINGLE[:16] + [SINGLE[16]] + WIDE + [15] + [15] + NARROW + [15]


def freq(j):
    return j - KB if j >= KB // 2 else j


def row_tables():
    row = np.zeros(KB, np.int32)
    shifted = np.zeros(KB, np.int32)
    for place, f in enumerate(ROW_FREQ[:NR]):
        if f != 15:
            row[f % KB] = place
    for place, f in enumerate(NARROW):
        row[f % KB] = 17 + place
        shifted[f % KB] = KB // 2
    return row, shifted


def phases(positions, freqs):
    angle = np.mod(np.outer(positions, freqs), NF).astype(np.float32) * np.float32(2.0 * math.pi / NF)
    return np.cos(angle).astype(np.float32), np.sin(angle).astype(np.float32)


def depth_weights():
    cos, sin = phases(np.arange(NF), [freq(j) for j in range(KB)])
    w = np.zeros((4, 2, NF, 2, KB, 4), np.float32)
    for vl in range(4):
        w[vl, 0, :, 0, :, vl] = cos
        w[vl, 1, :, 0, :, vl] = sin
        w[vl, 0, :, 1, :, vl] = -sin
        w[vl, 1, :, 1, :, vl] = cos
    return w.reshape(8 * NF, 8 * KB).astype(ml_dtypes.bfloat16)


def height_weights():
    cos, sin = phases(np.arange(NF), ROW_FREQ)
    return np.concatenate([cos.T, sin.T], 0).astype(ml_dtypes.bfloat16)


def wide_mask():
    mask = np.ones((8, KB, 4), np.float32)
    for place, f in enumerate(WIDE):
        half = math.isqrt(196 - f * f)
        for j in range(KB):
            if abs(freq(j)) > half:
                mask[1 + place, j] = 0.0
    return mask.reshape(8, 4 * KB)


def box_weights():
    cos, sin = phases(np.arange(NF), [freq(j) for j in range(KB)])
    cos = cos.T.reshape(KB, NSLAB, 2, HX).transpose(0, 2, 1, 3)
    sin = sin.T.reshape(KB, NSLAB, 2, HX).transpose(0, 2, 1, 3)
    t = np.zeros((2, KB, 2, NSLAB, 2, HX), np.float32)
    t[0, :, :, :, 0] = cos
    t[0, :, :, :, 1] = sin
    t[1, :, :, :, 0] = -sin
    t[1, :, :, :, 1] = cos
    high = t.astype(ml_dtypes.bfloat16)
    low = (t - high.astype(np.float32)).astype(ml_dtypes.bfloat16)
    pair = np.zeros((2, 2, 2, KB, 2, NSLAB, 2, 2, HX), ml_dtypes.bfloat16)
    for r in range(2):
        pair[r, 0, :, :, :, :, r] = high
        pair[r, 1, :, :, :, :, r] = low
    return pair.reshape(8 * KB, 4 * NF)


def lane_order():
    m = np.zeros((2, 2, KB, 4, KB, 2, 2, 4), np.float32)
    for reim in range(2):
        for vg in range(2):
            for kz in range(KB):
                for vl in range(4):
                    m[reim, vg, kz, vl, kz, reim, vg, vl] = 1.0
    return m.reshape(512, 512).astype(ml_dtypes.bfloat16)


def place_in_groups():
    g = lax.axis_index("grp")
    gx, gz = g // 2, lax.rem(g, 2)

    def at(dx, dz):
        return lax.rem(gx + dx + 4, 4) * 2 + (lax.rem(gz + dz, 2))

    return g, at


def place_in_slabs():
    s = lax.axis_index("slab")
    sz, sy, sc = s // 8, lax.rem(s // 2, 4), lax.rem(s, 2)

    def at(dy, dz, dc):
        return lax.rem(sz + dz, 2) * 8 + lax.rem(sy + dy + 4, 4) * 2 + lax.rem(sc + dc, 2)

    return s, at


def enter(groups, slabs):
    barrier = pltpu.get_barrier_semaphore()
    for one in groups:
        pl.semaphore_signal(barrier, inc=1, device_id={"grp": one}, device_id_type=MESH)
    for one in slabs:
        pl.semaphore_signal(barrier, inc=1, device_id={"slab": one}, device_id_type=MESH)
    pl.semaphore_wait(barrier, len(groups) + len(slabs))


def remote(src, dst, send, recv, device):
    return pltpu.make_async_remote_copy(
        src_ref=src, dst_ref=dst, send_sem=send, recv_sem=recv, device_id=device, device_id_type=MESH
    )


def planes_kernel(
    val_ref, con_ref, wz_ref, ty_ref, mask_ref, tab_ref, xb_ref, out_ref, part, val, con, msg, wz, even, odd, first_even, first_odd, scr, con_sem, own_sem, wz_sem, vs, vr, ms, mr, local_sem
):
    g, gat = place_in_groups()
    s, sat = place_in_slabs()
    own = pltpu.make_async_copy(val_ref.at[0], val.at[0], own_sem)
    own.start()
    weights = pltpu.make_async_copy(wz_ref, wz, wz_sem)
    weights.start()

    def band(i):
        k = lax.rem(i + 16, 16) // 2
        step = lax.rem(k + 1, 4)
        step = step + lax.rem(s, 2) * (4 - 2 * step)
        return sat(lax.rem(step, 4), lax.rem(i + 17, 2), 1 - k // 4)

    def con_copy(c):
        return pltpu.make_async_copy(con_ref.at[c], con.at[c], con_sem.at[c])

    def start_con(i, _):
        con_copy(band(i)).start()
        return 0

    lax.fori_loop(0, NSLAB, start_con, 0)
    partner, ahead, behind = gat(0, 1), gat(1, 0), gat(-1, 0)
    enter([partner, ahead, behind], [lax.rem(s + i, NSLAB) for i in range(1, NSLAB)])
    own.wait()

    def hop(k, slot, to, landing):
        return [
            remote(
                val.at[slot, pl.ds(half * HX, HX)],
                val.at[landing, pl.ds(half * HX, HX)],
                vs.at[k, half],
                vr.at[landing, half],
                {"grp": to},
            )
            for half in range(2)
        ]

    to_partner, to_ahead, to_behind = hop(0, 0, partner, 1), hop(1, 0, ahead, 2), hop(2, 0, behind, 3)
    p_ahead, p_behind = hop(3, 1, ahead, 4), hop(4, 1, behind, 5)
    l_ahead, r_behind = hop(5, 2, ahead, 6), hop(6, 5, behind, 7)
    for half in range(2):
        to_ahead[half].start()
        to_behind[half].start()
        to_partner[half].start()
    weights.wait()

    def message(vg, half, c):
        return remote(
            msg.at[vg, half, c], out_ref.at[vg, half, s], ms.at[vg, half, c], mr.at[vg, half, s], {"slab": c}
        )

    def arrival(vg, half, src):
        return remote(
            msg.at[vg, half, src],
            out_ref.at[vg, half, src],
            ms.at[vg, half, src],
            mr.at[vg, half, src],
            {"slab": src},
        )

    def kept(vg, half):
        return pltpu.make_async_copy(msg.at[vg, half, s], out_ref.at[vg, half, s], local_sem.at[vg, half])

    def density(vg, half, c, buf, x):
        for y0 in range(0, NF, 32):
            rows = pl.ds(y0, 32)
            put = pl.ds(x * NF + y0, 32)
            cr = con[c, half * HX + x, rows, 0:NF]
            ci = con[c, half * HX + x, rows, NF : 2 * NF]
            for vl in range(4):
                pr = val[vg * 4 + vl, half * HX + x, rows, 0:NF]
                pi = val[vg * 4 + vl, half * HX + x, rows, NF : 2 * NF]
                buf[put, vl * 256 : vl * 256 + NF] = pr * cr + pi * ci
                buf[put, vl * 256 + NF : vl * 256 + 256] = pr * ci - pi * cr

    def along_z(part, buf, first):
        rows = pl.ds(part * HX * NF // 2, HX * NF // 2)
        first[rows, :] = jnp.dot(buf[rows, :], wz[...], preferred_element_type=F32).astype(BF)

    def along_y(x, first):
        o = jnp.dot(ty_ref[...], first[x * NF : x * NF + NF, :], preferred_element_type=F32)
        keep = mask_ref[...] > 0.5
        for reim in range(2):
            if reim == 0:
                full = o[0:32, 0:128] + o[32:64, 128:256]
            else:
                full = o[0:32, 128:256] - o[32:64, 0:128]
            merged = jnp.where(keep, full[16:24], pltpu.roll(full[24:32], 64, 1))
            base = (reim * HX + x) * NR
            scr[base : base + 16, :] = full[0:16]
            scr[base + 16 : base + 24, :] = merged

    def pack(vg, half, c):
        for r in range(0, NR, 2):
            both = jnp.concatenate(
                [scr[pl.ds(r, 2 * HX, stride=NR), :], scr[pl.ds(r + 1, 2 * HX, stride=NR), :]], 0
            )
            msg[vg, half, c, r // 2] = both.astype(BF)

    def one_band(vg, half, before, after, buf, other, first, last):
        along_z(0, buf, first)
        density(vg, half, after, other, 0)
        density(vg, half, after, other, 1)
        along_y(0, last)
        along_y(1, last)
        along_z(1, buf, first)
        density(vg, half, after, other, 2)
        density(vg, half, after, other, 3)
        along_y(2, last)
        along_y(3, last)
        pack(vg, half, before)

    for phase in range(4):
        vg, half = phase // 2, phase % 2
        if phase == 0:
            for copies in (to_partner, to_ahead, to_behind):
                copies[0].wait_recv()
            p_behind[0].start()
            p_ahead[0].start()
            l_ahead[0].start()
        if phase == 1:
            for copies in (to_partner, to_ahead, to_behind):
                copies[1].wait_recv()
            p_ahead[1].start()
            p_behind[0].wait_recv()
            r_behind[0].start()
            p_behind[1].start()
            l_ahead[1].start()
        if phase >= 2:
            for copies in (p_ahead, l_ahead, r_behind):
                copies[half].wait_recv()
        start = band(0)
        if phase == 0:
            con_copy(start).wait()
        for x in range(HX):
            density(vg, half, start, even, x)

        def two_bands(j, _):
            before, c0, c1, c2 = band(2 * j - 1), band(2 * j), band(2 * j + 1), band(2 * j + 2)
            if phase == 0:
                con_copy(c1).wait()

                @pl.when(j < NSLAB // 2 - 1)
                def _():
                    con_copy(c2).wait()

            if phase == 2:

                @pl.when(j == 2)
                def _():
                    p_behind[1].wait_recv()
                    r_behind[1].start()

            one_band(vg, half, before, c1, even, odd, first_even, first_odd)

            @pl.when(j > 0)
            def _():
                message(vg, half, before).start()

            one_band(vg, half, c0, c2, odd, even, first_odd, first_even)
            message(vg, half, c0).start()
            return 0

        lax.fori_loop(0, NSLAB // 2, two_bands, 0)
        for x in range(HX):
            along_y(x, first_odd)
        pack(vg, half, s)
        kept(vg, half).start()

    scaling = 0.5 / float(NF) ** 1.5
    for vg in range(2):
        for half in range(2):

            def finish(i, _):
                arrival(vg, half, lax.rem(s + i + 1, NSLAB)).wait_recv()
                return 0

            lax.fori_loop(0, NSLAB - 1, finish, 0)
            kept(vg, half).wait()
            for p in range(NR // 2):
                held = out_ref[vg, half, :, p].reshape(2 * NF, 128)
                both = jnp.dot(tab_ref[:, half * 256 : half * 256 + 256], held, preferred_element_type=F32)
                for r in range(2):
                    o = both[r * 128 : r * 128 + 64] + both[r * 128 + 64 : r * 128 + 128]
                    if half == 0:
                        part[2 * p + r] = o
                    else:
                        o = ((o + part[2 * p + r]) * scaling).astype(BF)
                        put = (2 * p + r) * KB
                        xb_ref[put : put + KB, vg * 128 : vg * 128 + 128] = o[0:32]
                        xb_ref[put : put + KB, 256 + vg * 128 : 384 + vg * 128] = o[32:64]

    def sent(i, _):
        for vg in range(2):
            for half in range(2):
                message(vg, half, lax.rem(s + i + 1, NSLAB)).wait_send()
        return 0

    lax.fori_loop(0, NSLAB - 1, sent, 0)
    for copies in (to_partner, to_ahead, to_behind, p_ahead, p_behind, l_ahead, r_behind):
        for half in range(2):
            copies[half].wait_send()


def planes_call(valence, conduction):
    anywhere = pl.BlockSpec(memory_space=pl.ANY)
    vmem = pl.BlockSpec(memory_space=pltpu.VMEM)
    return pl.pallas_call(
        planes_kernel,
        name="planes",
        out_shape=jax.ShapeDtypeStruct((NBOX, 512), BF),
        in_specs=[anywhere, anywhere, anywhere, vmem, vmem, vmem],
        out_specs=vmem,
        scratch_shapes=[
            pltpu.VMEM((2, 2, NSLAB, NR // 2, 16, 128), BF),
            pltpu.VMEM((NR, 2 * KB, 128), F32),
            pltpu.VMEM((8, NX, NF, 2 * NF), BF),
            pltpu.VMEM((NSLAB, NX, NF, 2 * NF), BF),
            pltpu.VMEM((2, 2, NSLAB, NR // 2, 16, 128), BF),
            pltpu.VMEM((8 * NF, 2 * NF), BF),
            pltpu.VMEM((HX * NF, 8 * NF), BF),
            pltpu.VMEM((HX * NF, 8 * NF), BF),
            pltpu.VMEM((HX * NF, 2 * NF), BF),
            pltpu.VMEM((HX * NF, 2 * NF), BF),
            pltpu.VMEM((2 * HX * NR, 128), F32),
            pltpu.SemaphoreType.DMA((NSLAB,)),
            pltpu.SemaphoreType.DMA,
            pltpu.SemaphoreType.DMA,
            pltpu.SemaphoreType.DMA((7, 2)),
            pltpu.SemaphoreType.DMA((8, 2)),
            pltpu.SemaphoreType.DMA((2, 2, NSLAB)),
            pltpu.SemaphoreType.DMA((2, 2, NSLAB)),
            pltpu.SemaphoreType.DMA((2, 2)),
        ],
        compiler_params=pltpu.CompilerParams(
            collective_id=0, has_side_effects=True, vmem_limit_bytes=56 * 1024 * 1024
        ),
    )(
        valence,
        conduction,
        jnp.asarray(depth_weights()),
        jnp.asarray(height_weights()),
        jnp.asarray(wide_mask()),
        jnp.asarray(box_weights()),
    )


def panels_kernel(
    idx_ref, ve_ref, ce_ref, oc_ref, xb_ref, order_ref, acc_ref, left_ref, right_ref,
    rp_ref, cab_ref, wide, box, blk, rows, cols, landed, cp,
    rsa, rra, csa, cra, rs, rr, cs, cr, sib_s, sib_r, lsem,
):
    g, gat = place_in_groups()
    s, sat = place_in_slabs()
    gx, gz = g // 2, lax.rem(g, 2)
    sz, yc, sc = s // 8, lax.rem(s, 8), lax.rem(s, 2)

    barrier = pltpu.get_barrier_semaphore()
    for i in range(2 * NSLAB):
        if i:
            to = {"grp": gat(0, i // NSLAB), "slab": lax.rem(s + i, NSLAB)}
            pl.semaphore_signal(barrier, inc=1, device_id=to, device_id_type=MESH)
    for i in range(4, 16):
        to = {"grp": gat(i // 4, i // 2 % 2), "slab": sat(0, i % 2, 0)}
        pl.semaphore_signal(barrier, inc=1, device_id=to, device_id_type=MESH)

    wide[...] = jnp.dot(xb_ref[...], order_ref[...], preferred_element_type=F32)

    def spread(j, _):
        base = pl.multiple_of(j * 96, 32)
        for kz in range(KB):
            part = wide[pl.ds(base, 96), (kz // 8) * 128 : (kz // 8 + 1) * 128]
            if kz % 8:
                part = pltpu.roll(part, 128 - 16 * (kz % 8), 1)
            box[pl.ds(pl.multiple_of(kz * NBOX + base, 8), 96), :] = part
        return 0

    lax.fori_loop(0, NBOX // 96, spread, 0)
    blk[CP : CP + 32, :] = jnp.zeros((32, 128), F32)
    for chunk in range(6):
        cab_ref[chunk * 256 + 128 : chunk * 256 + 192, :] = jnp.zeros((64, 2 * CP), BF)
    slot = lax.rem(lax.broadcasted_iota(jnp.int32, (16, CP), 0), 8)
    charge, gap = jnp.zeros((16, CP), F32), jnp.ones((16, CP), F32)
    for place, spot in enumerate([(0, 0), (0, 1), (-1, 0), (1, 0), (-1, 1), (1, 1), (2, 0), (2, 1)]):
        v = gat(*spot)
        charge = jnp.where(slot == place, oc_ref[v].astype(F32), charge)
        gap = jnp.where(slot == place, ve_ref[v] - ce_ref[s], gap)
    factor = (charge / (gap * math.sqrt(NV * NC)))[:, 0:1]
    pl.semaphore_wait(barrier, 43)

    lane = lax.broadcasted_iota(jnp.int32, (16, 128), 1)
    row = lax.broadcasted_iota(jnp.int32, (16, 128), 0)
    unit = jnp.where(lane == row, 1.0, 0.0).astype(BF)
    contract = (((1,), (1,)), ((), ()))

    def row_copy(h, b, z):
        to = {"grp": b, "slab": z * 8 + yc}
        dx = lax.rem(gx - b // 2 + 4, 4)
        return remote(rows.at[h, b], landed.at[h, dx, gz, sz], rsa.at[h, b, z], rra.at[h, dx, gz, sz], to)

    def row_in(h, b, z):
        to = {"grp": b, "slab": z * 8 + yc}
        dx, bz = lax.rem(b // 2 - gx + 4, 4), lax.rem(b, 2)
        return remote(rows.at[h, b], landed.at[h, dx, bz, z], rsa.at[h, b, z], rra.at[h, dx, bz, z], to)

    def row_keep(h):
        return pltpu.make_async_copy(rows.at[h, g], landed.at[h, 0, gz, sz], lsem.at[h])

    def col_copy(t, z):
        to = {"grp": gx * 2 + z, "slab": t}
        return remote(cols.at[t], cp.at[gx, gz, s], csa.at[t, z], cra.at[gz, s], to)

    def col_in(t, z):
        to = {"grp": gx * 2 + z, "slab": t}
        return remote(cols.at[t], cp.at[gx, z, t], csa.at[t, z], cra.at[z, t], to)

    def col_keep():
        return pltpu.make_async_copy(cols.at[s], cp.at[gx, gz, s], lsem.at[2])

    def one_block(h, i):
        b = lax.rem(g + yc // 2 + sz * 4 + i, NGRP)
        count, many = (CP, 64) if h == 0 else (CB, 50)
        origin = b * RB + h * CB

        def pick(j, _):
            base = j * many
            for k in range(many):
                blk[pl.ds(base + k, 1), :] = box[pl.ds(idx_ref[origin + base + k], 1), :]
            return 0

        lax.fori_loop(0, count // many, pick, 0)
        skip = h * (CP - CB)
        o = lax.dot_general(unit, blk[skip : skip + CP, :].astype(BF), contract, preferred_element_type=F32)
        rows[h, b] = (o * factor).astype(BF)
        o = lax.dot_general(unit, blk[0:CP, :].astype(BF), contract, preferred_element_type=F32)
        cols[2 * b + h] = o.astype(BF)
        for z in range(2):
            mine = jnp.logical_and(b == g, z == sz)

            @pl.when(mine)
            def _():
                row_keep(h).start()

            @pl.when(jnp.logical_not(mine))
            def _():
                row_copy(h, b, z).start()

            own = jnp.logical_and(2 * b + h == s, z == gz)

            @pl.when(own)
            def _():
                col_keep().start()

            @pl.when(jnp.logical_not(own))
            def _():
                col_copy(2 * b + h, z).start()

    for h in range(2):

        def block_step(i, _):
            one_block(h, i)
            return 0

        lax.fori_loop(0, NGRP, block_step, 0)

    def over_rows(act):
        def step(i, _):
            b, z = i // 2, lax.rem(i, 2)

            @pl.when(jnp.logical_not(jnp.logical_and(b == g, z == sz)))
            def _():
                act(b, z)

            return 0

        lax.fori_loop(0, 2 * NGRP, step, 0)

    def over_cols(act):
        def step(i, _):
            t, z = i // 2, lax.rem(i, 2)

            @pl.when(jnp.logical_not(jnp.logical_and(t == s, z == gz)))
            def _():
                act(t, z)

            return 0

        lax.fori_loop(0, 2 * NSLAB, step, 0)

    def row_part(dy, dc, half):
        return rp_ref.at[PLACE[dy], lax.rem(sc + dc, 2), pl.ds(half * 768, 768)]

    def row_hop(k, dy, half, to, land):
        there = dy - to if dy - to > -2 else 2
        return remote(
            row_part(dy, 0, half), row_part(there, 0, half), rs.at[k], rr.at[land], {"slab": sat(to, 0, 0)}
        )

    def row_wait(land, dy, half):
        part = row_part(dy, 0, half)
        remote(part, part, rs.at[0], rr.at[land], {"slab": sat(1, 0, 0)}).wait_recv()

    def side(k, dy, half, dc=0):
        part = row_part(dy, dc, half)
        return remote(part, part, sib_s.at[k], sib_r.at[k], {"slab": sat(0, 0, 1)})

    def col_part(dx, half):
        return cp.at[gat(dx, 0) // 2, half]

    def col_hop(k, dx, half, to, land):
        part = col_part(dx, half)
        return remote(part, part, cs.at[k], cr.at[land], {"grp": gat(to, 0)})

    def col_wait(land, dx, half):
        part = col_part(dx, half)
        remote(part, part, cs.at[0], cr.at[land], {"grp": gat(1, 0)}).wait_recv()

    hops = [(0, 0, 1, 0), (0, 1, -1, 3), (0, 1, 1, 1), (0, 0, -1, 2), (-1, 0, 1, 4), (1, 1, -1, 5)]
    arrivals = [(0, -1, 0), (2, 1, 0), (3, 1, 1), (1, -1, 1), (4, 2, 0), (5, 2, 1)]
    own_and_near = [(0, 0), (0, 1)] + [(dy, half) for _, dy, half in arrivals]
    row_hops = [row_hop(k, *hop) for k, hop in enumerate(hops)]
    col_hops = [col_hop(k, *hop) for k, hop in enumerate(hops)]
    sides = [side(0, 0, 0), side(1, 0, 1)] + [side(2 + k, dy, half) for k, (_, dy, half) in enumerate(arrivals)]

    def arrange(dx, half):
        x = gat(dx, 0) // 2
        for dy in (0, -1, 1, 2):
            for dc in range(2):
                chunk = PLACE[dy] * 2 + dc
                for z in range(2):
                    t = z * 8 + lax.rem(yc // 2 + dy + 4, 4) * 2 + dc
                    part = cp[x, half, pl.ds(t, 1)].reshape(16, CP)
                    value = part.astype(F32)
                    turned = jnp.concatenate([-value[8:16], value[0:8]], 0).astype(BF)
                    put = (dx % 4) * 64 + half * 32 + z * 16
                    if dy == 2:
                        to, put = right_ref, dc * 256 + put
                    elif dx == 2:
                        to, put = right_ref, 512 + chunk * 64 + half * 32 + z * 16
                    else:
                        to, put = cab_ref, chunk * 256 + put
                    to[put : put + 16, 0:CP] = part
                    to[put : put + 16, CP : 2 * CP] = turned

    def own_columns():
        col_keep().wait()
        over_cols(lambda t, z: col_in(t, z).wait_recv())
        for k in (0, 3, 1, 2):
            col_hops[k].start()

    for h in range(2):
        row_keep(h).wait()
        over_rows(lambda b, z: row_in(h, b, z).wait_recv())
        for j in range(CP // 128):
            part = landed[h, :, :, :, :, j * 128 : (j + 1) * 128].reshape(256, 128).astype(F32)
            rp_ref[0, sc, h * CP + j * 128 : h * CP + (j + 1) * 128, :] = part.T.astype(BF)
        for k in ((0, 3), (1, 2))[h]:
            row_hops[k].start()
        sides[h].start()

        @pl.when(sc == h)
        def _():
            own_columns()

    arrange(0, 0)
    arrange(0, 1)
    for k, (land, d, half) in enumerate(arrivals):
        row_wait(land, d, half)
        if k in (0, 2):
            row_hops[4 + k // 2].start()
        sides[2 + k].start()
        col_wait(land, d, half)
        if k in (0, 2):
            col_hops[4 + k // 2].start()
        arrange(d, half)
        if k == 3:
            for n in range(6):
                side(n, *own_and_near[n], 1).wait_recv()

            def near(m, _):
                put = pl.ds(pl.multiple_of(m * 256, 256), 256)
                parts = [rp_ref[p, c, put, :] for p in range(3) for c in range(2)]
                acc_ref[put, :] = jnp.dot(jnp.concatenate(parts, 1), cab_ref[...], preferred_element_type=F32)
                for pair in range(3):
                    both = [parts[2 * pair][:, 128:192], parts[2 * pair + 1][:, 128:192]]
                    left_ref[put, 512 + pair * 128 : 640 + pair * 128] = jnp.concatenate(both, 1)
                return 0

            lax.fori_loop(0, RP // 256, near, 0)
    for n in range(6, 8):
        side(n, *own_and_near[n], 1).wait_recv()
    for c in range(2):
        left_ref[:, c * 256 : c * 256 + 256] = rp_ref[3, c]
    for h in range(2):
        over_rows(lambda b, z: row_copy(h, b, z).wait_send())
    over_cols(lambda t, z: col_copy(t, z).wait_send())
    for copy in row_hops + col_hops + sides:
        copy.wait_send()


PLACE = {0: 0, -1: 1, 1: 2, 2: 3}


def panels_call(index, planes, valence_energy, conduction_energy, occupation):
    smem = pl.BlockSpec(memory_space=pltpu.SMEM)
    vmem = pl.BlockSpec(memory_space=pltpu.VMEM)
    dma = pltpu.SemaphoreType.DMA
    return pl.pallas_call(
        panels_kernel,
        name="panels",
        out_shape=(
            jax.ShapeDtypeStruct((RP, 2 * CP), F32),
            jax.ShapeDtypeStruct((RP, 896), BF),
            jax.ShapeDtypeStruct((896, 2 * CP), BF),
        ),
        in_specs=[smem, smem, smem, smem, vmem, vmem],
        out_specs=(vmem, vmem, vmem),
        scratch_shapes=[
            pltpu.VMEM((4, 2, RP, 256), BF),
            pltpu.VMEM((1536, 2 * CP), BF),
            pltpu.VMEM((NBOX, 512), F32),
            pltpu.VMEM((KB * NBOX, 128), F32),
            pltpu.VMEM((CP + 32, 128), F32),
            pltpu.VMEM((2, NGRP, 16, CP), BF),
            pltpu.VMEM((NSLAB, 16, CP), BF),
            pltpu.VMEM((2, 4, 2, 2, 16, CP), BF),
            pltpu.VMEM((4, 2, NSLAB, 16, CP), BF),
            dma((2, NGRP, 2)),
            dma((2, 4, 2, 2)),
            dma((NSLAB, 2)),
            dma((2, NSLAB)),
            dma((6,)),
            dma((6,)),
            dma((6,)),
            dma((6,)),
            dma((8,)),
            dma((8,)),
            dma((3,)),
        ],
        compiler_params=pltpu.CompilerParams(
            collective_id=1, has_side_effects=True, vmem_limit_bytes=34 * 1024 * 1024
        ),
    )(
        index,
        valence_energy,
        conduction_energy,
        occupation,
        planes,
        jnp.asarray(lane_order()),
    )


def tile_kernel(acc_ref, left_ref, right_ref, out_ref):
    rows = pl.ds(pl.multiple_of(pl.program_id(0) * 256, 256), 256)
    o = jnp.dot(left_ref[rows, :], right_ref[...], preferred_element_type=F32) + acc_ref[rows, :]
    out_ref[:, 0, :] = o[:, 0:CB]
    out_ref[:, 1, :] = o[:, CP : CP + CB]


def tile_call(near, left, right):
    rows = 256
    tiles = pl.pallas_call(
        tile_kernel,
        name="tile",
        grid=(RP // rows,),
        out_shape=jax.ShapeDtypeStruct((RB, 2, CB), F32),
        in_specs=[
            pl.BlockSpec((RP, 2 * CP), lambda i: (0, 0)),
            pl.BlockSpec((RP, 896), lambda i: (0, 0)),
            pl.BlockSpec((896, 2 * CP), lambda i: (0, 0)),
        ],
        out_specs=pl.BlockSpec((rows, 2, CB), lambda i: (i, 0, 0)),
        compiler_params=pltpu.CompilerParams(vmem_limit_bytes=32 * 1024 * 1024),
    )(near, left, right)
    return jnp.transpose(tiles, (1, 0, 2))


def table_look_up(index, table):
    found = jnp.zeros_like(index)
    for place, value in enumerate(table):
        found = jnp.where(index == place, int(value), found)
    return found


def on_device(
    valence_waves, conduction_waves, valence_energy, conduction_energy, occupation, gvec_ids
):
    row, shifted = row_tables()
    along_x = gvec_ids // (KB * KB)
    along_y = gvec_ids // KB % KB
    along_z = gvec_ids % KB
    place = table_look_up(along_y, row * KB + shifted * 1024 * KB)
    index = (along_z ^ (place // (1024 * KB))) * NBOX + place % (1024 * KB) + along_x

    planes = planes_call(valence_waves, conduction_waves)
    near, left, right = panels_call(index, planes, valence_energy, conduction_energy, occupation)
    return tile_call(near, left, right)


def solution(mesh):
    in_specs = (P("grp", "slab", None, None), P("grp", "slab", None, None), P(), P("grp"), P(), P())
    out_specs = P(None, "grp", "slab")
    return jax.shard_map(
        on_device, mesh=mesh, in_specs=in_specs, out_specs=out_specs, check_vma=False
    )
```
